256 devices in a mesh: dp: 16 (over x_lo, z), tensor: 16 (over y, x_hi, core).
Axes of the slice: x: 4 (x_hi: 2, x_lo: 2; x = x_hi * 2 + x_lo), y: 4, z: 8, core: 2. Of those that a mesh axis runs over, the one named last changes fastest.
Arguments:
- attention: bfloat16 [4096, 8192], P('dp', 'tensor'), may hold values from -6 to 6
- output_weight_frozen: bfloat16 [8192, 16384], P('dp', 'tensor'), may hold values from -0.0625 to 0.0625
- residual: bfloat16 [4096, 16384], P('dp', 'tensor'), may hold values from -40 to 40
- cotangent: bfloat16 [4, 4096, 16384], P(None, 'dp', 'tensor'), may hold values from -1 to 1
- output_norm_scale: float32 [16384], P('tensor'), may hold values from 0.5 to 1.5
- adapter_down_weights: bfloat16 [4, 64, 8192], replicated, may hold values from -0.0625 to 0.0625
- adapter_up_weights: bfloat16 [4, 64, 16384], P(None, None, 'tensor'), may hold values from -0.625 to 0.625
- objective: int32 [4], replicated, may hold values from 0 to 3
Outputs:
- fisher_a: float32 [4, 64, 8192], P(None, 'dp', 'tensor')
- fisher_b: float32 [4, 64, 16384], P(None, 'dp', 'tensor')
The draws below stay inside these ranges and needn't reach their ends.
All inputs are finite; a program needn't handle non-finite values.
Results may differ from the reference program's by a relative error of at most 0.0015.
Values may be sent and summed in bfloat16 or wider, within the bound.
A program may use at most 128 MiB of HBM per device.

```python
import jax
import jax.numpy as jnp
from jax import lax

MODEL_WIDTH = 16384
ADAPTER_RANK = 64
ADAPTER_COUNT = 4
PASSES = 4
LEN = 256
ATTN_FEATURES = 8192
EXAMPLES = 16
TOKENS = 4096


def draw_residual(key, part):
    key = jax.random.fold_in(key, 7)
    key_norm, key_block, key_column, key_row = jax.random.split(key, 4)
    position = jnp.arange(MODEL_WIDTH, dtype=jnp.float32) / MODEL_WIDTH
    block_index = jnp.arange(MODEL_WIDTH, dtype=jnp.int32) * 64 // MODEL_WIDTH
    block_scale = jnp.exp(jax.random.uniform(key_block, (64,), jnp.float32, -0.69, 0.69))[block_index]
    column_scale = jnp.exp(jax.random.uniform(key_column, (MODEL_WIDTH,), jnp.float32, -0.35, 0.35))
    values = jax.random.normal(key_norm, (TOKENS, MODEL_WIDTH), jnp.float32)
    ramp = 3.0 ** position
    row_scale = jnp.exp(jax.random.uniform(key_row, (TOKENS, 1), jnp.float32, -0.92, 1.38))
    values = values * row_scale * (ramp * block_scale * column_scale)[None, :]
    return jnp.clip(values, -40.0, 40.0).astype(jnp.bfloat16)


def plant(drawn, rng, smallest, largest):
    longest = drawn.shape.index(max(drawn.shape))
    spots = []
    for shift in (0, 1):
        where = [jax.random.randint(jax.random.fold_in(rng, axis), (), 0, length) for axis, length in enumerate(drawn.shape)]
        where[longest] = (where[longest] + shift) % drawn.shape[longest]
        spots.append(tuple(where))
    return drawn.at[spots[0]].set(smallest).at[spots[1]].set(largest)


def shard_levels(stream_key, dims, pieces, low, high):
    def one(axis_at, blocks):
        heights = jax.random.uniform(jax.random.fold_in(jax.random.fold_in(stream_key, 6), axis_at), (blocks,), jnp.float32, low / len(pieces), high / len(pieces))
        return jnp.repeat(jnp.exp(heights), dims[axis_at] // blocks).reshape((-1,) + (1,) * (len(dims) - axis_at - 1))

    gain = one(*pieces[0])
    for cut in pieces[1:]:
        gain = gain * one(*cut)
    return gain


def scatter_about(rng, dims, scale, bound, pieces=(), kind=jnp.bfloat16):
    factor_of = shard_levels(rng, dims, pieces, -0.22, 0.18) if pieces else 1.0
    values = jax.random.normal(rng, dims, jnp.float32) * scale * factor_of
    return jnp.minimum(jnp.maximum(values, -bound), bound).astype(kind)


def setup_inputs(seed: int = 0) -> dict:
    arg_keys = jax.random.split(jax.random.key(seed), 9)
    return {
        "attention": scatter_about(arg_keys[0], (TOKENS, ATTN_FEATURES), 1.0, 6.0, ((0, 16), (1, 16))),
        "output_weight_frozen": scatter_about(arg_keys[1], (ATTN_FEATURES, MODEL_WIDTH), ATTN_FEATURES ** -0.5, 0.0625, ((0, 16), (1, 16))),
        "residual": draw_residual(jax.random.fold_in(arg_keys[8], 71), 0),
        "cotangent": scatter_about(arg_keys[3], (PASSES, TOKENS, MODEL_WIDTH), (LEN ** -0.5), 1.0, ((1, 16), (2, 16))),
        "output_norm_scale": jnp.clip(1.0 + 0.1 * jax.random.normal(arg_keys[4], (MODEL_WIDTH,), jnp.float32), 0.5, 1.5),
        "adapter_down_weights": scatter_about(arg_keys[5], (ADAPTER_COUNT, ADAPTER_RANK, ATTN_FEATURES), ATTN_FEATURES ** -0.5, 0.0625),
        "adapter_up_weights": scatter_about(arg_keys[6], (ADAPTER_COUNT, ADAPTER_RANK, MODEL_WIDTH), 0.04, 0.625, ((2, 16),)),
        "objective": plant(jax.random.randint(arg_keys[7], (PASSES,), 0, ADAPTER_COUNT), jax.random.fold_in(arg_keys[7], 1), 0, ADAPTER_COUNT - 1).astype(jnp.int32),
    }


epsilon = 1e-05

def reference(attention, output_weight_frozen, residual, cotangent, output_norm_scale, adapter_down_weights, adapter_up_weights, objective):
    base = jnp.dot(attention, output_weight_frozen, preferred_element_type=jnp.float32)
    partial_sum = residual.astype(jnp.float32) + base
    fisher_a = jnp.zeros((ADAPTER_COUNT, ADAPTER_RANK, ATTN_FEATURES), jnp.float32)
    fisher_b = jnp.zeros((ADAPTER_COUNT, ADAPTER_RANK, MODEL_WIDTH), jnp.float32)
    attn_blocks = attention.astype(jnp.float32).reshape(EXAMPLES, LEN, ATTN_FEATURES)
    for step in range(PASSES):
        picked_adapter = objective[step]
        down_projection = lax.dynamic_index_in_dim(adapter_down_weights, picked_adapter, 0, keepdims=False)
        up_projection = lax.dynamic_index_in_dim(adapter_up_weights, picked_adapter, 0, keepdims=False)
        lowered = jnp.dot(attention, down_projection.T, preferred_element_type=jnp.float32).astype(jnp.bfloat16)
        hidden_sum = partial_sum + jnp.dot(lowered, up_projection, preferred_element_type=jnp.float32)
        weighted = cotangent[step].astype(jnp.float32) * output_norm_scale
        squares = lax.optimization_barrier(jnp.sum(hidden_sum * hidden_sum, axis=-1, keepdims=True))
        inner = lax.optimization_barrier(jnp.sum(weighted * hidden_sum, axis=-1, keepdims=True))
        scale_inv = lax.rsqrt(squares / MODEL_WIDTH + epsilon)
        grad_out = (scale_inv * weighted - hidden_sum * inner * scale_inv ** 3 / MODEL_WIDTH).astype(jnp.bfloat16)
        grad_low = jnp.dot(grad_out, up_projection.T, preferred_element_type=jnp.float32).astype(jnp.bfloat16)
        per_b = jnp.einsum('etr,etd->erd', lowered.astype(jnp.float32).reshape(EXAMPLES, LEN, ADAPTER_RANK), grad_out.astype(jnp.float32).reshape(EXAMPLES, LEN, MODEL_WIDTH))
        per_a = jnp.einsum('etr,eth->erh', grad_low.astype(jnp.float32).reshape(EXAMPLES, LEN, ADAPTER_RANK), attn_blocks)
        adapter_picker = (jnp.arange(ADAPTER_COUNT, dtype=jnp.int32) == picked_adapter).astype(jnp.float32)
        fisher_a = fisher_a + adapter_picker[:, None, None] * (lax.optimization_barrier(jnp.sum(per_a * per_a, axis=0)) / EXAMPLES)[None]
        fisher_b = fisher_b + adapter_picker[:, None, None] * (lax.optimization_barrier(jnp.sum(per_b * per_b, axis=0)) / EXAMPLES)[None]
    return (fisher_a, fisher_b)
```

```python
import jax
import jax.numpy as jnp
from jax import lax
from jax.experimental import pallas as pl
from jax.experimental.pallas import tpu as pltpu
from jax.sharding import PartitionSpec as P

MODEL_WIDTH = 16384
ADAPTER_RANK = 64
ADAPTER_COUNT = 4
PASSES = 4
LEN = 256
EXAMPLES = 16
GROUP = 16
MESH = pl.DeviceIdType.MESH

epsilon = 1e-05


def to_tensor(step):
    return (lax.axis_index("dp"), lax.rem(lax.axis_index("tensor") + step, GROUP))


def to_dp(step):
    return (lax.rem(lax.axis_index("dp") + step, GROUP), lax.axis_index("tensor"))


def each_other(action):
    def one(step, carry):
        action(step)
        return carry

    lax.fori_loop(1, GROUP, one, 0)


def spread_rows(step):
    per = ADAPTER_RANK // GROUP
    row = lax.broadcasted_iota(jnp.int32, (PASSES * ADAPTER_RANK, ADAPTER_RANK), 0)
    col = lax.broadcasted_iota(jnp.int32, (PASSES * ADAPTER_RANK, ADAPTER_RANK), 1)
    goal = (col // per) * (PASSES * per) + step * per + col % per
    return jnp.where(row == goal, 1.0, 0.0).astype(jnp.bfloat16)


def tail_kernel(
    objective,
    partial,
    low,
    cotangent,
    scale,
    up,
    attention,
    out_a,
    out_b,
    hidden,
    grads,
    low_wide,
    up_wide,
    stat_slots,
    low_terms,
    low_slots,
    grad_low,
    square_b,
    slots_b,
    square_a,
    slots_a,
    stat_send,
    stat_recv,
    term_send,
    term_recv,
    full_send,
    full_recv,
    b_send,
    b_recv,
    a_send,
    a_recv,
):
    me_d = lax.axis_index("dp")
    me_t = lax.axis_index("tensor")
    barrier = pltpu.get_barrier_semaphore()

    def greet(step):
        pl.semaphore_signal(barrier, inc=1, device_id=to_tensor(step), device_id_type=MESH)
        pl.semaphore_signal(barrier, inc=1, device_id=to_dp(step), device_id_type=MESH)

    each_other(greet)

    lane = lax.broadcasted_iota(jnp.int32, (LEN, 128), 1)
    stats = jnp.zeros((LEN, 128), jnp.float32)
    for step in range(PASSES):
        picked = objective[step]
        spread = spread_rows(step)
        low_wide[step] = lax.dot_general(
            low[picked], spread, (((1,), (1,)), ((), ())), preferred_element_type=jnp.float32
        ).astype(jnp.bfloat16)
        up_wide[step] = jnp.dot(
            spread, up[picked], preferred_element_type=jnp.float32
        ).astype(jnp.bfloat16)
        value = partial[...] + jnp.dot(
            low_wide[step], up_wide[step], preferred_element_type=jnp.float32
        )
        hidden[step] = value
        weighted = cotangent[step].astype(jnp.float32) * scale[...]
        squares = jnp.sum(value * value, axis=1, keepdims=True)
        inner = jnp.sum(weighted * value, axis=1, keepdims=True)
        stats = jnp.where(lane == 2 * step, squares, stats)
        stats = jnp.where(lane == 2 * step + 1, inner, stats)
    stat_slots[0] = stats.T[: 2 * PASSES]

    pl.semaphore_wait(barrier, 2 * (GROUP - 1))

    def stat_copy(step):
        return pltpu.make_async_remote_copy(
            src_ref=stat_slots.at[0],
            dst_ref=stat_slots.at[step],
            send_sem=stat_send.at[step],
            recv_sem=stat_recv.at[step],
            device_id=to_tensor(step),
            device_id_type=MESH,
        )

    each_other(lambda step: stat_copy(step).start())
    each_other(lambda step: stat_copy(step).wait())
    totals = jnp.sum(stat_slots[...], axis=0)
    kinds = lax.broadcasted_iota(jnp.int32, totals.shape, 0)
    inner_first = jnp.concatenate([totals[1:], totals[:1]], axis=0)
    scale_inv = lax.rsqrt(totals / MODEL_WIDTH + epsilon)
    weight_hidden = inner_first * scale_inv**3 / MODEL_WIDTH
    keep = jnp.concatenate(
        [scale_inv, weight_hidden, jnp.zeros((128 - 4 * PASSES, LEN), jnp.float32)], axis=0
    )
    keep = jnp.where(
        lax.broadcasted_iota(jnp.int32, keep.shape, 0) % 2 == 0, keep, 0.0
    )
    columns = keep.T

    terms = None
    for step in range(PASSES):
        weighted = cotangent[step].astype(jnp.float32) * scale[...]
        per_token = columns[:, 2 * step : 2 * step + 1]
        back = columns[:, 2 * PASSES + 2 * step : 2 * PASSES + 2 * step + 1]
        grads[step] = (per_token * weighted - hidden[step] * back).astype(jnp.bfloat16)
        term = lax.dot_general(
            grads[step], up_wide[step], (((1,), (1,)), ((), ())), preferred_element_type=jnp.float32
        )
        terms = term if terms is None else terms + term
    low_terms[...] = terms.reshape(low_terms.shape)

    def term_copy(step):
        return pltpu.make_async_remote_copy(
            src_ref=low_terms.at[lax.rem(me_t + step, GROUP)],
            dst_ref=low_slots.at[step],
            send_sem=term_send.at[step],
            recv_sem=term_recv.at[step],
            device_id=to_tensor(step),
            device_id_type=MESH,
        )

    each_other(lambda step: term_copy(step).start())

    per_b = None
    for step in range(PASSES):
        term = lax.dot_general(
            low_wide[step], grads[step], (((0,), (0,)), ((), ())), preferred_element_type=jnp.float32
        )
        per_b = term if per_b is None else per_b + term
    square_b[...] = (per_b * per_b).astype(jnp.bfloat16).reshape(square_b.shape)

    def b_copy(step):
        return pltpu.make_async_remote_copy(
            src_ref=square_b.at[lax.rem(me_d + step, GROUP)],
            dst_ref=slots_b.at[step],
            send_sem=b_send.at[step],
            recv_sem=b_recv.at[step],
            device_id=to_dp(step),
            device_id_type=MESH,
        )

    each_other(lambda step: b_copy(step).start())

    each_other(lambda step: term_copy(step).wait())
    low_slots[0] = low_terms[me_t]
    rows = LEN // GROUP
    mine = pl.ds(pl.multiple_of(me_t * rows, rows), rows)
    grad_low[mine, :] = jnp.sum(low_slots[...], axis=0).astype(jnp.bfloat16)

    def full_copy(step, owner):
        place = pl.ds(pl.multiple_of(owner * rows, rows), rows)
        return pltpu.make_async_remote_copy(
            src_ref=grad_low.at[place, :],
            dst_ref=grad_low.at[place, :],
            send_sem=full_send.at[step],
            recv_sem=full_recv.at[step],
            device_id=to_tensor(step),
            device_id_type=MESH,
        )

    each_other(lambda step: full_copy(step, me_t).start())
    each_other(lambda step: full_copy(step, me_t).wait_send())
    each_other(
        lambda step: full_copy(step, lax.rem(me_t + GROUP - step, GROUP)).wait_recv()
    )
    per_a = lax.dot_general(
        grad_low[...], attention[...], (((0,), (0,)), ((), ())), preferred_element_type=jnp.float32
    )
    square_a[...] = (per_a * per_a).astype(jnp.bfloat16).reshape(square_a.shape)

    def a_copy(step):
        return pltpu.make_async_remote_copy(
            src_ref=square_a.at[lax.rem(me_d + step, GROUP)],
            dst_ref=slots_a.at[step],
            send_sem=a_send.at[step],
            recv_sem=a_recv.at[step],
            device_id=to_dp(step),
            device_id_type=MESH,
        )

    each_other(lambda step: a_copy(step).start())

    per = ADAPTER_RANK // GROUP

    def finish(copy, squares, slots, out):
        each_other(lambda step: copy(step).wait())
        slots[0] = squares[me_d]
        total = jnp.sum(slots[...].astype(jnp.float32), axis=0)
        for adapter in range(ADAPTER_COUNT):
            chosen = None
            for step in range(PASSES):
                share = jnp.where(objective[step] == adapter, 1.0 / EXAMPLES, 0.0)
                piece = share * total[step * per : (step + 1) * per]
                chosen = piece if chosen is None else chosen + piece
            out[adapter] = chosen

    finish(b_copy, square_b, slots_b, out_b)
    finish(a_copy, square_a, slots_a, out_a)


def tail(objective, partial, low, cotangent, scale, up, attention):
    columns = partial.shape[1]
    features = attention.shape[1]
    per = ADAPTER_RANK // GROUP
    wide = PASSES * ADAPTER_RANK
    rows = LEN // GROUP
    bf16, f32 = jnp.bfloat16, jnp.float32
    vmem = pl.BlockSpec(memory_space=pltpu.VMEM)
    return pl.pallas_call(
        tail_kernel,
        name="tail",
        out_shape=(
            jax.ShapeDtypeStruct((ADAPTER_COUNT, per, features), f32),
            jax.ShapeDtypeStruct((ADAPTER_COUNT, per, columns), f32),
        ),
        in_specs=[pl.BlockSpec(memory_space=pltpu.SMEM)] + [vmem] * 6,
        out_specs=(vmem, vmem),
        scratch_shapes=[
            pltpu.VMEM((PASSES, LEN, columns), f32),
            pltpu.VMEM((PASSES, LEN, columns), bf16),
            pltpu.VMEM((PASSES, LEN, wide), bf16),
            pltpu.VMEM((PASSES, wide, columns), bf16),
            pltpu.VMEM((GROUP, 2 * PASSES, LEN), f32),
            pltpu.VMEM((GROUP, rows, wide), f32),
            pltpu.VMEM((GROUP, rows, wide), f32),
            pltpu.VMEM((LEN, wide), bf16),
            pltpu.VMEM((GROUP, wide // GROUP, columns), bf16),
            pltpu.VMEM((GROUP, wide // GROUP, columns), bf16),
            pltpu.VMEM((GROUP, wide // GROUP, features), bf16),
            pltpu.VMEM((GROUP, wide // GROUP, features), bf16),
        ]
        + [pltpu.SemaphoreType.DMA((GROUP,))] * 10,
        compiler_params=pltpu.CompilerParams(
            collective_id=0, has_side_effects=True, vmem_limit_bytes=56 * 2**20
        ),
    )(objective, partial, low, cotangent, scale, up, attention)


def body(
    attention,
    output_weight_frozen,
    residual,
    cotangent,
    output_norm_scale,
    adapter_down_weights,
    adapter_up_weights,
    objective,
):
    gathered = lax.all_gather(attention, "tensor", axis=1, tiled=True)
    low = jnp.einsum(
        "th,krh->ktr", gathered, adapter_down_weights, preferred_element_type=jnp.float32
    ).astype(jnp.bfloat16)
    base = jnp.dot(
        gathered,
        lax.all_gather(output_weight_frozen, "dp", axis=0, tiled=True),
        preferred_element_type=jnp.float32,
    )
    partial = residual.astype(jnp.float32) + base
    return tail(
        objective, partial, low, cotangent, output_norm_scale[None], adapter_up_weights, attention
    )


def solution(mesh):
    placed = (
        P("dp", "tensor"),
        P("dp", "tensor"),
        P("dp", "tensor"),
        P(None, "dp", "tensor"),
        P("tensor"),
        P(),
        P(None, None, "tensor"),
        P(),
    )
    return jax.shard_map(
        body,
        mesh=mesh,
        in_specs=placed,
        out_specs=(P(None, "dp", "tensor"), P(None, "dp", "tensor")),
        check_vma=False,
    )
```

```python
import jax
import jax.numpy as jnp
from jax import lax
from jax.experimental import pallas as pl
from jax.experimental.pallas import tpu as pltpu
from jax.sharding import PartitionSpec as P

MODEL_WIDTH = 16384
ADAPTER_RANK = 64
ADAPTER_COUNT = 4
PASSES = 4
LEN = 256
EXAMPLES = 16
GROUP = 16
MESH = pl.DeviceIdType.MESH

epsilon = 1e-05


def to_tensor(step):
    return (lax.axis_index("dp"), lax.rem(lax.axis_index("tensor") + step, GROUP))


def to_dp(step):
    return (lax.rem(lax.axis_index("dp") + step, GROUP), lax.axis_index("tensor"))


def each_other(action):
    def one(step, carry):
        action(step)
        return carry

    lax.fori_loop(1, GROUP, one, 0)


RING = 8
NEAR = (4, 3, -3, 2, -2, 1, -1, 0)
CHUNK = 256
PIECE = 32


def spread(picked, step):
    per = ADAPTER_RANK // GROUP
    size = (ADAPTER_COUNT * ADAPTER_RANK, PASSES * ADAPTER_RANK)
    row = lax.broadcasted_iota(jnp.int32, size, 0)
    col = lax.broadcasted_iota(jnp.int32, size, 1)
    goal = picked * ADAPTER_RANK + col // (PASSES * per) * per + col % per
    chosen = (row == goal) & (col // per % PASSES == step)
    return jnp.where(chosen, 1.0, 0.0).astype(jnp.bfloat16)


def remote(src, dst, send, recv, device):
    return pltpu.make_async_remote_copy(
        src_ref=src,
        dst_ref=dst,
        send_sem=send,
        recv_sem=recv,
        device_id=device,
        device_id_type=MESH,
    )


def whole_kernel(
    objective,
    scale,
    attention,
    weight_hbm,
    residual_hbm,
    cotangent_hbm,
    down_hbm,
    up_hbm,
    out_a,
    out_b,
    tokens,
    weight,
    residual,
    cotangent,
    down,
    up,
    ring_out,
    ring_in,
    hidden,
    sums,
    grads,
    low_terms,
    low_slots,
    low_all,
    low_wide,
    up_wide,
    stat_slots,
    back_terms,
    back_slots,
    back_all,
    square_b,
    slots_b,
    square_a,
    slots_a,
    local,
    first_send,
    first_recv,
    weight_send,
    weight_recv,
    y_send,
    y_recv,
    f_send,
    f_recv,
    core_send,
    core_recv,
    ring_send,
    ring_recv,
    low_sems,
    back_sems,
    stat_send,
    stat_recv,
    b_send,
    b_recv,
    a_send,
    a_recv,
):
    me_d = lax.axis_index("dp")
    me_t = lax.axis_index("tensor")
    half = me_d // RING
    me_z = lax.rem(me_d, RING)
    side = me_t // RING
    goal_z = lax.rem(me_t, RING)
    me_y = me_t // 4
    core = lax.rem(me_t, 2)
    has_own = goal_z == me_z
    rows = LEN // GROUP
    wide = PASSES * ADAPTER_RANK
    columns = weight.shape[2]
    chunks = columns // CHUNK
    features = attention.shape[1]

    barrier = pltpu.get_barrier_semaphore()

    def greet(step):
        pl.semaphore_signal(barrier, inc=1, device_id=to_tensor(step), device_id_type=MESH)
        pl.semaphore_signal(barrier, inc=1, device_id=to_dp(step), device_id_type=MESH)

    each_other(greet)

    def greet_sender(number, carry):
        z = number // 2
        t = lax.rem(number, 2) * RING + me_z

        @pl.when((z != me_z) | (t != me_t))
        def _():
            pl.semaphore_signal(
                barrier, inc=1, device_id=(half * RING + z, t), device_id_type=MESH
            )

        return carry

    lax.fori_loop(0, 2 * RING, greet_sender, 0)

    def load(number):
        place = pl.ds(pl.multiple_of(me_t * features, features), features)
        pairs = (
            (down_hbm.at[:, :, place], down),
            (weight_hbm, weight.at[half]),
            (up_hbm, up),
            (residual_hbm, residual),
            (cotangent_hbm, cotangent),
        )
        return pltpu.make_async_copy(*pairs[number], local.at[number])

    for number in range(5):
        load(number).start()

    load(0).wait()
    low_terms[...] = lax.dot_general(
        attention[...],
        down[...].reshape(ADAPTER_COUNT * ADAPTER_RANK, features),
        (((1,), (1,)), ((), ())),
        preferred_element_type=jnp.float32,
    ).reshape(low_terms.shape)

    pl.semaphore_wait(barrier, 2 * (GROUP - 1) + 2 * RING - jnp.where(has_own, 1, 0))

    def piece(t):
        number = t // 4 * 2 + lax.rem(t, 2)
        return pl.ds(pl.multiple_of(number * PIECE, PIECE), PIECE)

    def first_copy(step):
        t = lax.rem(me_t + step, GROUP)
        return remote(
            attention.at[piece(t), :],
            tokens.at[me_z, side, piece(t), :],
            first_send.at[step],
            first_recv.at[me_z * 2 + side],
            (half * RING + goal_z, t),
        )

    each_other(lambda step: first_copy(step).start())

    @pl.when(has_own)
    def _():
        tokens[me_z, side, piece(me_t), :] = attention[piece(me_t), :]

    @pl.when(jnp.logical_not(has_own))
    def _():
        first_copy(0).start()

    def weight_copy(chunk, slot):
        place = pl.ds(chunk * CHUNK, CHUNK)
        return remote(
            weight_hbm.at[:, place],
            weight.at[slot, :, place],
            weight_send.at[chunk],
            weight_recv.at[chunk],
            (lax.rem(me_d + RING, GROUP), me_t),
        )

    for chunk in range(chunks):
        weight_copy(chunk, half).start()

    def add_rows(terms, slots, total, sems):
        def term_copy(step):
            return remote(
                terms.at[lax.rem(me_t + step, GROUP)],
                slots.at[step],
                sems.at[0, step],
                sems.at[1, step],
                to_tensor(step),
            )

        def full_copy(step, owner):
            place = pl.ds(pl.multiple_of(owner * rows, rows), rows)
            return remote(
                total.at[place, :],
                total.at[place, :],
                sems.at[2, step],
                sems.at[3, step],
                to_tensor(step),
            )

        def begin():
            each_other(lambda step: term_copy(step).start())

        def middle():
            each_other(lambda step: term_copy(step).wait())
            slots[0] = terms[me_t]
            mine = pl.ds(pl.multiple_of(me_t * rows, rows), rows)
            total[mine, :] = jnp.sum(slots[...], axis=0).astype(jnp.bfloat16)
            each_other(lambda step: full_copy(step, me_t).start())

        def end():
            each_other(lambda step: full_copy(step, me_t).wait_send())
            each_other(
                lambda step: full_copy(step, lax.rem(me_t + GROUP - step, GROUP)).wait_recv()
            )

        return begin, middle, end

    low_begin, low_middle, low_end = add_rows(low_terms, low_slots, low_all, low_sems)
    back_begin, back_middle, back_end = add_rows(back_terms, back_slots, back_all, back_sems)
    low_begin()

    def at_y(shift):
        return lax.rem(me_t + (shift % 4) * 4, GROUP)

    other = me_t + 1 - 2 * core

    def z_of(number):
        return lax.rem(me_z + NEAR[number] + RING, RING)

    def y_copy(number, way, owner):
        part = tokens.at[z_of(number), :, piece(owner), :]
        return remote(
            part, part, y_send.at[number, way], y_recv.at[number, way], (me_d, at_y((1, -1)[way]))
        )

    def f_copy(number, way, owner):
        part = tokens.at[z_of(number), way, piece(owner), :]
        return remote(
            part, part, f_send.at[number, way], f_recv.at[number, way], (me_d, at_y((1, -1)[way]))
        )

    def core_copy(number, shift, owner):
        part = tokens.at[z_of(number), :, piece(owner), :]
        return remote(
            part, part, core_send.at[number, shift], core_recv.at[number, shift], (me_d, other)
        )

    def spread_own(number):
        z = z_of(number)
        for h in range(2):
            wait = remote(
                attention.at[piece(me_t), :],
                tokens.at[z, h, piece(me_t), :],
                first_send.at[0],
                first_recv.at[z * 2 + h],
                (me_d, other),
            ).wait_recv
            if NEAR[number] == 0:
                pl.when(jnp.logical_not(has_own & (side == h)))(wait)
            else:
                wait()
        y_copy(number, 0, me_t).start()
        y_copy(number, 1, me_t).start()
        core_copy(number, 0, me_t).start()

    def spread_next(number):
        y_copy(number, 0, at_y(-1)).wait_recv()
        f_copy(number, 0, at_y(-1)).start()
        core_copy(number, 3, at_y(-1)).start()
        y_copy(number, 1, at_y(1)).wait_recv()
        f_copy(number, 1, at_y(1)).start()
        core_copy(number, 1, at_y(1)).start()

    def spread_last(number):
        f_copy(number, 0, at_y(2)).wait_recv()
        f_copy(number, 1, at_y(2)).wait_recv()
        core_copy(number, 2, at_y(2)).start()

    def arrived(number):
        for shift in range(4):
            owner = lax.rem(other + shift * 4, GROUP)
            core_copy(number, shift, owner).wait_recv()

    def product(number, cols):
        z = z_of(number)
        total = jnp.dot(tokens[z, 0], weight[0, :, cols], preferred_element_type=jnp.float32)
        return total + jnp.dot(
            tokens[z, 1], weight[1, :, cols], preferred_element_type=jnp.float32
        )

    def ring_copy(way, far, chunk, slot):
        if far == 4:
            place = pl.ds(way * (LEN // 2), LEN // 2)
        else:
            place = pl.ds(0, LEN)
        z = lax.rem(me_z + (1, RING - 1)[way], RING)
        return remote(
            ring_out.at[way, far - 1, chunk, place, :],
            ring_in.at[way, far - 1, chunk, place, :],
            ring_send.at[way, far - 1, chunk],
            ring_recv.at[way, far - 1, chunk],
            (half * RING + z, me_t),
        )

    def cols_of(chunk):
        return pl.ds(pl.multiple_of(chunk * CHUNK, CHUNK), CHUNK)

    def send_products(far, begin):
        def one(chunk, carry):
            cols = cols_of(chunk)
            if far == 4:
                value = product(0, cols).astype(jnp.bfloat16)
                for way in range(2):
                    mine = slice(way * (LEN // 2), (way + 1) * (LEN // 2))
                    ring_out[way, 3, chunk, mine, :] = value[mine]
                    ring_copy(way, 4, chunk, 0).start()
                return carry
            for way in range(2):
                number = NEAR.index((far, -far)[way])
                value = product(number, cols)
                ring_copy(way, far + 1, chunk, 0).wait_recv()
                if far == 3:
                    mine = slice(way * (LEN // 2), (way + 1) * (LEN // 2))
                    rest = slice((1 - way) * (LEN // 2), (2 - way) * (LEN // 2))
                    ring_out[way, 2, chunk, mine, :] = (
                        value[mine] + ring_in[way, 3, chunk, mine, :].astype(jnp.float32)
                    ).astype(jnp.bfloat16)
                    ring_out[way, 2, chunk, rest, :] = value[rest].astype(jnp.bfloat16)
                else:
                    ring_out[way, far - 1, chunk] = (
                        value + ring_in[way, far, chunk].astype(jnp.float32)
                    ).astype(jnp.bfloat16)
                ring_copy(way, far, chunk, 0).start()
            return carry

        lax.fori_loop(begin, begin + chunks // 2, one, 0)

    def own_products(begin):
        def one(chunk, carry):
            cols = cols_of(chunk)
            value = product(NEAR.index(0), cols)
            for way in range(2):
                ring_copy(way, 1, chunk, 0).wait_recv()
                value = value + ring_in[way, 0, chunk].astype(jnp.float32)
            value = value + residual[:, cols].astype(jnp.float32)
            for step in range(PASSES):
                here = value + jnp.dot(
                    low_wide[step], up_wide[step, :, cols], preferred_element_type=jnp.float32
                )
                hidden[step, :, cols] = here
                weighted = cotangent[step, :, cols].astype(jnp.float32) * scale[:, cols]
                squares = here * here
                inner = weighted * here
                sums[2 * step] += squares[:, :128] + squares[:, 128:]
                sums[2 * step + 1] += inner[:, :128] + inner[:, 128:]
            return carry

        lax.fori_loop(begin, begin + chunks // 2, one, 0)

    spread_own(0)
    spread_own(1)
    spread_own(2)
    spread_next(0)
    spread_own(3)
    spread_next(1)
    spread_last(0)
    spread_own(4)
    spread_next(2)
    spread_last(1)
    load(1).wait()
    for chunk in range(chunks // 2):
        weight_copy(chunk, 1 - half).wait_recv()
    arrived(0)
    send_products(4, 0)
    spread_own(5)
    spread_next(3)
    spread_last(2)
    arrived(1)
    arrived(2)
    send_products(3, 0)
    spread_own(6)
    spread_next(4)
    spread_last(3)
    spread_own(7)
    spread_next(5)
    spread_last(4)
    arrived(3)
    arrived(4)
    send_products(2, 0)
    spread_next(6)
    spread_last(5)
    spread_next(7)
    spread_last(6)
    arrived(5)
    arrived(6)
    send_products(1, 0)
    spread_last(7)
    arrived(7)
    for chunk in range(chunks // 2, chunks):
        weight_copy(chunk, 1 - half).wait_recv()
    send_products(4, chunks // 2)
    low_middle()
    send_products(3, chunks // 2)
    low_end()
    for number in range(2, 5):
        load(number).wait()
    up_rows = up[...].reshape(ADAPTER_COUNT * ADAPTER_RANK, columns)
    for step in range(PASSES):
        choice = spread(objective[step], step)
        low_wide[step] = jnp.dot(
            low_all[...], choice, preferred_element_type=jnp.float32
        ).astype(jnp.bfloat16)
        up_wide[step] = lax.dot_general(
            choice, up_rows, (((0,), (0,)), ((), ())), preferred_element_type=jnp.float32
        ).astype(jnp.bfloat16)
    sums[...] = jnp.zeros(sums.shape, jnp.float32)
    send_products(2, chunks // 2)
    own_products(0)
    send_products(1, chunks // 2)
    own_products(chunks // 2)

    lane = lax.broadcasted_iota(jnp.int32, (LEN, 128), 1)
    stats = jnp.zeros((LEN, 128), jnp.float32)
    for kind in range(2 * PASSES):
        stats = jnp.where(lane == kind, jnp.sum(sums[kind], axis=1, keepdims=True), stats)
    stat_slots[0] = stats.T[: 2 * PASSES]

    def stat_copy(step):
        return remote(
            stat_slots.at[0],
            stat_slots.at[step],
            stat_send.at[step],
            stat_recv.at[step],
            to_tensor(step),
        )

    each_other(lambda step: stat_copy(step).start())
    each_other(lambda step: stat_copy(step).wait())
    totals = jnp.sum(stat_slots[...], axis=0)
    inner_first = jnp.concatenate([totals[1:], totals[:1]], axis=0)
    scale_inv = lax.rsqrt(totals / MODEL_WIDTH + epsilon)
    weight_hidden = inner_first * scale_inv**3 / MODEL_WIDTH
    keep = jnp.concatenate(
        [scale_inv, weight_hidden, jnp.zeros((128 - 4 * PASSES, LEN), jnp.float32)], axis=0
    )
    keep = jnp.where(lax.broadcasted_iota(jnp.int32, keep.shape, 0) % 2 == 0, keep, 0.0)
    by_token = keep.T

    terms = None
    for step in range(PASSES):
        weighted = cotangent[step].astype(jnp.float32) * scale[...]
        per_token = by_token[:, 2 * step : 2 * step + 1]
        back = by_token[:, 2 * PASSES + 2 * step : 2 * PASSES + 2 * step + 1]
        grads[step] = (per_token * weighted - hidden[step] * back).astype(jnp.bfloat16)
        term = lax.dot_general(
            grads[step], up_wide[step], (((1,), (1,)), ((), ())), preferred_element_type=jnp.float32
        )
        terms = term if terms is None else terms + term
    back_terms[...] = terms.reshape(back_terms.shape)
    back_begin()

    per_b = None
    for step in range(PASSES):
        term = lax.dot_general(
            low_wide[step], grads[step], (((0,), (0,)), ((), ())), preferred_element_type=jnp.float32
        )
        per_b = term if per_b is None else per_b + term
    square_b[...] = (per_b * per_b).astype(jnp.bfloat16).reshape(square_b.shape)

    def owner_copy(step, squares, slots, send, recv):
        return remote(
            squares.at[lax.rem(me_d + step, GROUP)],
            slots.at[step],
            send.at[step],
            recv.at[step],
            to_dp(step),
        )

    each_other(lambda step: owner_copy(step, square_b, slots_b, b_send, b_recv).start())

    back_middle()
    back_end()
    per_a = lax.dot_general(
        back_all[...], attention[...], (((0,), (0,)), ((), ())), preferred_element_type=jnp.float32
    )
    square_a[...] = (per_a * per_a).astype(jnp.bfloat16).reshape(square_a.shape)
    each_other(lambda step: owner_copy(step, square_a, slots_a, a_send, a_recv).start())

    per = ADAPTER_RANK // GROUP

    def finish(squares, slots, send, recv, out):
        each_other(lambda step: owner_copy(step, squares, slots, send, recv).wait())
        slots[0] = squares[me_d]
        total = jnp.sum(slots[...].astype(jnp.float32), axis=0)
        for adapter in range(ADAPTER_COUNT):
            chosen = None
            for step in range(PASSES):
                share = jnp.where(objective[step] == adapter, 1.0 / EXAMPLES, 0.0)
                part = share * total[step * per : (step + 1) * per]
                chosen = part if chosen is None else chosen + part
            out[adapter] = chosen

    finish(square_b, slots_b, b_send, b_recv, out_b)

    each_other(lambda step: first_copy(step).wait_send())
    pl.when(jnp.logical_not(has_own))(lambda: first_copy(0).wait_send())
    for chunk in range(chunks):
        weight_copy(chunk, half).wait_send()
    for number in range(RING):
        for way in range(2):
            y_copy(number, way, me_t).wait_send()
            f_copy(number, way, me_t).wait_send()
        for shift in range(4):
            core_copy(number, shift, me_t).wait_send()

    def ring_done(chunk, carry):
        for way in range(2):
            for far in range(1, 5):
                ring_copy(way, far, chunk, 0).wait_send()
        return carry

    lax.fori_loop(0, chunks, ring_done, 0)
    finish(square_a, slots_a, a_send, a_recv, out_a)


def body(
    attention,
    output_weight_frozen,
    residual,
    cotangent,
    output_norm_scale,
    adapter_down_weights,
    adapter_up_weights,
    objective,
):
    features = attention.shape[1]
    depth, columns = output_weight_frozen.shape
    chunks = columns // CHUNK
    per = ADAPTER_RANK // GROUP
    wide = PASSES * ADAPTER_RANK
    rows = LEN // GROUP
    bf16, f32 = jnp.bfloat16, jnp.float32
    vmem = pl.BlockSpec(memory_space=pltpu.VMEM)
    hbm = pl.BlockSpec(memory_space=pl.ANY)
    sem = pltpu.SemaphoreType.DMA
    return pl.pallas_call(
        whole_kernel,
        name="fisher",
        out_shape=(
            jax.ShapeDtypeStruct((ADAPTER_COUNT, per, features), f32),
            jax.ShapeDtypeStruct((ADAPTER_COUNT, per, columns), f32),
        ),
        in_specs=[pl.BlockSpec(memory_space=pltpu.SMEM), vmem, vmem] + [hbm] * 5,
        out_specs=(vmem, vmem),
        scratch_shapes=[
            pltpu.VMEM((RING, 2, LEN, features), bf16),
            pltpu.VMEM((2, depth, columns), bf16),
            pltpu.VMEM((LEN, columns), bf16),
            pltpu.VMEM((PASSES, LEN, columns), bf16),
            pltpu.VMEM((ADAPTER_COUNT, ADAPTER_RANK, features), bf16),
            pltpu.VMEM((ADAPTER_COUNT, ADAPTER_RANK, columns), bf16),
            pltpu.VMEM((2, 4, chunks, LEN, CHUNK), bf16),
            pltpu.VMEM((2, 4, chunks, LEN, CHUNK), bf16),
            pltpu.VMEM((PASSES, LEN, columns), f32),
            pltpu.VMEM((2 * PASSES, LEN, 128), f32),
            pltpu.VMEM((PASSES, LEN, columns), bf16),
            pltpu.VMEM((GROUP, rows, wide), f32),
            pltpu.VMEM((GROUP, rows, wide), f32),
            pltpu.VMEM((LEN, wide), bf16),
            pltpu.VMEM((PASSES, LEN, wide), bf16),
            pltpu.VMEM((PASSES, wide, columns), bf16),
            pltpu.VMEM((GROUP, 2 * PASSES, LEN), f32),
            pltpu.VMEM((GROUP, rows, wide), f32),
            pltpu.VMEM((GROUP, rows, wide), f32),
            pltpu.VMEM((LEN, wide), bf16),
            pltpu.VMEM((GROUP, wide // GROUP, columns), bf16),
            pltpu.VMEM((GROUP, wide // GROUP, columns), bf16),
            pltpu.VMEM((GROUP, wide // GROUP, features), bf16),
            pltpu.VMEM((GROUP, wide // GROUP, features), bf16),
            sem((5,)),
            sem((GROUP,)),
            sem((GROUP,)),
            sem((chunks,)),
            sem((chunks,)),
            sem((RING, 2)),
            sem((RING, 2)),
            sem((RING, 2)),
            sem((RING, 2)),
            sem((RING, 4)),
            sem((RING, 4)),
            sem((2, 4, chunks)),
            sem((2, 4, chunks)),
            sem((4, GROUP)),
            sem((4, GROUP)),
        ]
        + [sem((GROUP,))] * 6,
        compiler_params=pltpu.CompilerParams(
            collective_id=0, has_side_effects=True, vmem_limit_bytes=56 * 2**20
        ),
    )(
        objective,
        output_norm_scale[None],
        attention,
        output_weight_frozen,
        residual,
        cotangent,
        adapter_down_weights,
        adapter_up_weights,
    )


def solution(mesh):
    placed = (
        P("dp", "tensor"),
        P("dp", "tensor"),
        P("dp", "tensor"),
        P(None, "dp", "tensor"),
        P("tensor"),
        P(),
        P(None, None, "tensor"),
        P(),
    )
    return jax.shard_map(
        body,
        mesh=mesh,
        in_specs=placed,
        out_specs=(P(None, "dp", "tensor"), P(None, "dp", "tensor")),
        check_vma=False,
    )
```

```python
import jax
import jax.numpy as jnp
from jax import lax
from jax.experimental import pallas as pl
from jax.experimental.pallas import tpu as pltpu
from jax.sharding import PartitionSpec as P

MODEL_WIDTH = 16384
ADAPTER_RANK = 64
ADAPTER_COUNT = 4
PASSES = 4
LEN = 256
EXAMPLES = 16
GROUP = 16
MESH = pl.DeviceIdType.MESH

epsilon = 1e-05


def to_tensor(step):
    return (lax.axis_index("dp"), lax.rem(lax.axis_index("tensor") + step, GROUP))


def to_dp(step):
    return (lax.rem(lax.axis_index("dp") + step, GROUP), lax.axis_index("tensor"))


def each_other(action):
    def one(step, carry):
        action(step)
        return carry

    lax.fori_loop(1, GROUP, one, 0)


RING = 8
NEAR = (4, 3, -3, 2, -2, 1, -1, 0)
CHUNK = 256
PIECE = 32


def spread(picked, step):
    per = ADAPTER_RANK // GROUP
    size = (ADAPTER_COUNT * ADAPTER_RANK, PASSES * ADAPTER_RANK)
    row = lax.broadcasted_iota(jnp.int32, size, 0)
    col = lax.broadcasted_iota(jnp.int32, size, 1)
    goal = picked * ADAPTER_RANK + col // (PASSES * per) * per + col % per
    chosen = (row == goal) & (col // per % PASSES == step)
    return jnp.where(chosen, 1.0, 0.0).astype(jnp.bfloat16)


def remote(src, dst, send, recv, device):
    return pltpu.make_async_remote_copy(
        src_ref=src,
        dst_ref=dst,
        send_sem=send,
        recv_sem=recv,
        device_id=device,
        device_id_type=MESH,
    )


def whole_kernel(
    objective,
    scale,
    attention,
    weight_hbm,
    residual_hbm,
    cotangent_hbm,
    down_hbm,
    up_hbm,
    out_a,
    out_b,
    middle,
    tokens,
    weight,
    residual,
    cotangent,
    down,
    up,
    ring_out,
    ring_in,
    hidden,
    sums,
    grads,
    low_terms,
    low_slots,
    low_all,
    low_wide,
    up_wide,
    stat_slots,
    back_terms,
    back_slots,
    back_all,
    square_b,
    slots_b,
    square_a,
    slots_a,
    local,
    plane_send,
    plane_recv,
    z_send,
    z_recv,
    weight_send,
    weight_recv,
    y_send,
    y_recv,
    f_send,
    f_recv,
    core_send,
    core_recv,
    ring_send,
    ring_recv,
    low_sems,
    back_sems,
    stat_send,
    stat_recv,
    b_send,
    b_recv,
    a_send,
    a_recv,
):
    me_d = lax.axis_index("dp")
    me_t = lax.axis_index("tensor")
    half = me_d // RING
    me_z = lax.rem(me_d, RING)
    core = lax.rem(me_t, 2)
    rows = LEN // GROUP
    wide = PASSES * ADAPTER_RANK
    columns = weight.shape[2]
    chunks = columns // CHUNK
    features = attention.shape[1]

    barrier = pltpu.get_barrier_semaphore()

    def greet(step):
        pl.semaphore_signal(barrier, inc=1, device_id=to_tensor(step), device_id_type=MESH)
        pl.semaphore_signal(barrier, inc=1, device_id=to_dp(step), device_id_type=MESH)

    each_other(greet)

    def load(number):
        place = pl.ds(pl.multiple_of(me_t * features, features), features)
        pairs = (
            (down_hbm.at[:, :, place], down),
            (weight_hbm, weight.at[half]),
            (up_hbm, up),
            (residual_hbm, residual),
            (cotangent_hbm, cotangent),
        )
        return pltpu.make_async_copy(*pairs[number], local.at[number])

    for number in range(5):
        load(number).start()

    load(0).wait()
    low_terms[...] = lax.dot_general(
        attention[...],
        down[...].reshape(ADAPTER_COUNT * ADAPTER_RANK, features),
        (((1,), (1,)), ((), ())),
        preferred_element_type=jnp.float32,
    ).reshape(low_terms.shape)

    pl.semaphore_wait(barrier, 2 * (GROUP - 1))

    def piece(t):
        number = t // 4 * 2 + lax.rem(t, 2)
        return pl.ds(pl.multiple_of(number * PIECE, PIECE), PIECE)

    def plane_copy(step, source):
        t = lax.rem(me_t + step, GROUP)
        return remote(
            attention.at[piece(t), :],
            middle.at[lax.rem(source, RING), source // RING],
            plane_send.at[step],
            plane_recv.at[source],
            (me_d, t),
        )

    each_other(lambda step: plane_copy(step, me_t).start())
    middle[lax.rem(me_t, RING), me_t // RING] = attention[piece(me_t), :]

    def weight_copy(chunk, slot):
        place = pl.ds(chunk * CHUNK, CHUNK)
        return remote(
            weight_hbm.at[:, place],
            weight.at[slot, :, place],
            weight_send.at[chunk],
            weight_recv.at[chunk],
            (lax.rem(me_d + RING, GROUP), me_t),
        )

    for chunk in range(chunks):
        weight_copy(chunk, half).start()

    def add_rows(terms, slots, total, sems):
        def term_copy(step):
            return remote(
                terms.at[lax.rem(me_t + step, GROUP)],
                slots.at[step],
                sems.at[0, step],
                sems.at[1, step],
                to_tensor(step),
            )

        def full_copy(step, owner):
            place = pl.ds(pl.multiple_of(owner * rows, rows), rows)
            return remote(
                total.at[place, :],
                total.at[place, :],
                sems.at[2, step],
                sems.at[3, step],
                to_tensor(step),
            )

        def begin():
            each_other(lambda step: term_copy(step).start())

        def middle():
            each_other(lambda step: term_copy(step).wait())
            slots[0] = terms[me_t]
            mine = pl.ds(pl.multiple_of(me_t * rows, rows), rows)
            total[mine, :] = jnp.sum(slots[...], axis=0).astype(jnp.bfloat16)
            each_other(lambda step: full_copy(step, me_t).start())

        def end():
            each_other(lambda step: full_copy(step, me_t).wait_send())
            each_other(
                lambda step: full_copy(step, lax.rem(me_t + GROUP - step, GROUP)).wait_recv()
            )

        return begin, middle, end

    low_begin, low_middle, low_end = add_rows(low_terms, low_slots, low_all, low_sems)
    back_begin, back_middle, back_end = add_rows(back_terms, back_slots, back_all, back_sems)
    low_begin()

    def at_y(shift):
        return lax.rem(me_t + (shift % 4) * 4, GROUP)

    other = me_t + 1 - 2 * core

    def z_of(number):
        return lax.rem(me_z + NEAR[number] + RING, RING)

    def y_copy(number, way, owner):
        part = tokens.at[z_of(number), :, piece(owner), :]
        return remote(
            part, part, y_send.at[number, way], y_recv.at[number, way], (me_d, at_y((1, -1)[way]))
        )

    def f_copy(number, way, owner):
        part = tokens.at[z_of(number), way, piece(owner), :]
        return remote(
            part, part, f_send.at[number, way], f_recv.at[number, way], (me_d, at_y((1, -1)[way]))
        )

    def core_copy(number, shift, owner):
        part = tokens.at[z_of(number), :, piece(owner), :]
        return remote(
            part, part, core_send.at[number, shift], core_recv.at[number, shift], (me_d, other)
        )

    def z_copy(number, source):
        goal = z_of(number)
        return remote(
            middle.at[goal],
            tokens.at[source, :, piece(me_t), :],
            z_send.at[number],
            z_recv.at[source],
            (half * RING + goal, me_t),
        )

    def along_z(number):
        goal = z_of(number)
        for h in range(2):
            source = goal + h * RING
            pl.when(source != me_t)(plane_copy(1, source).wait_recv)
        if NEAR[number] == 0:
            tokens[me_z, :, piece(me_t), :] = middle[me_z]
        else:
            z_copy(number, me_z).start()

    def spread_own(number):
        if NEAR[number] != 0:
            z_copy(number, z_of(number)).wait_recv()
        y_copy(number, 0, me_t).start()
        y_copy(number, 1, me_t).start()
        core_copy(number, 0, me_t).start()

    def spread_next(number):
        y_copy(number, 0, at_y(-1)).wait_recv()
        f_copy(number, 0, at_y(-1)).start()
        core_copy(number, 3, at_y(-1)).start()
        y_copy(number, 1, at_y(1)).wait_recv()
        f_copy(number, 1, at_y(1)).start()
        core_copy(number, 1, at_y(1)).start()

    def spread_last(number):
        f_copy(number, 0, at_y(2)).wait_recv()
        f_copy(number, 1, at_y(2)).wait_recv()
        core_copy(number, 2, at_y(2)).start()

    def arrived(number):
        for shift in range(4):
            owner = lax.rem(other + shift * 4, GROUP)
            core_copy(number, shift, owner).wait_recv()

    def product(number, cols):
        z = z_of(number)
        total = jnp.dot(tokens[z, 0], weight[0, :, cols], preferred_element_type=jnp.float32)
        return total + jnp.dot(
            tokens[z, 1], weight[1, :, cols], preferred_element_type=jnp.float32
        )

    def ring_copy(way, far, chunk, slot):
        if far == 4:
            place = pl.ds(way * (LEN // 2), LEN // 2)
        else:
            place = pl.ds(0, LEN)
        z = lax.rem(me_z + (1, RING - 1)[way], RING)
        return remote(
            ring_out.at[way, far - 1, chunk, place, :],
            ring_in.at[way, far - 1, chunk, place, :],
            ring_send.at[way, far - 1, chunk],
            ring_recv.at[way, far - 1, chunk],
            (half * RING + z, me_t),
        )

    def cols_of(chunk):
        return pl.ds(pl.multiple_of(chunk * CHUNK, CHUNK), CHUNK)

    def send_products(far, begin):
        def one(chunk, carry):
            cols = cols_of(chunk)
            if far == 4:
                value = product(0, cols).astype(jnp.bfloat16)
                for way in range(2):
                    mine = slice(way * (LEN // 2), (way + 1) * (LEN // 2))
                    ring_out[way, 3, chunk, mine, :] = value[mine]
                    ring_copy(way, 4, chunk, 0).start()
                return carry
            for way in range(2):
                number = NEAR.index((far, -far)[way])
                value = product(number, cols)
                ring_copy(way, far + 1, chunk, 0).wait_recv()
                if far == 3:
                    mine = slice(way * (LEN // 2), (way + 1) * (LEN // 2))
                    rest = slice((1 - way) * (LEN // 2), (2 - way) * (LEN // 2))
                    ring_out[way, 2, chunk, mine, :] = (
                        value[mine] + ring_in[way, 3, chunk, mine, :].astype(jnp.float32)
                    ).astype(jnp.bfloat16)
                    ring_out[way, 2, chunk, rest, :] = value[rest].astype(jnp.bfloat16)
                else:
                    ring_out[way, far - 1, chunk] = (
                        value + ring_in[way, far, chunk].astype(jnp.float32)
                    ).astype(jnp.bfloat16)
                ring_copy(way, far, chunk, 0).start()
            return carry

        lax.fori_loop(begin, begin + chunks // 2, one, 0)

    def own_products(begin):
        def one(chunk, carry):
            cols = cols_of(chunk)
            value = product(NEAR.index(0), cols)
            for way in range(2):
                ring_copy(way, 1, chunk, 0).wait_recv()
                value = value + ring_in[way, 0, chunk].astype(jnp.float32)
            value = value + residual[:, cols].astype(jnp.float32)
            for step in range(PASSES):
                here = value + jnp.dot(
                    low_wide[step], up_wide[step, :, cols], preferred_element_type=jnp.float32
                )
                hidden[step, :, cols] = here
                weighted = cotangent[step, :, cols].astype(jnp.float32) * scale[:, cols]
                squares = here * here
                inner = weighted * here
                sums[2 * step] += squares[:, :128] + squares[:, 128:]
                sums[2 * step + 1] += inner[:, :128] + inner[:, 128:]
            return carry

        lax.fori_loop(begin, begin + chunks // 2, one, 0)

    for number in range(RING):
        along_z(number)
    spread_own(0)
    spread_own(1)
    spread_own(2)
    spread_next(0)
    spread_own(3)
    spread_next(1)
    spread_last(0)
    spread_own(4)
    spread_next(2)
    spread_last(1)
    load(1).wait()
    for chunk in range(chunks // 2):
        weight_copy(chunk, 1 - half).wait_recv()
    arrived(0)
    send_products(4, 0)
    spread_own(5)
    spread_next(3)
    spread_last(2)
    arrived(1)
    arrived(2)
    send_products(3, 0)
    spread_own(6)
    spread_next(4)
    spread_last(3)
    spread_own(7)
    spread_next(5)
    spread_last(4)
    arrived(3)
    arrived(4)
    send_products(2, 0)
    spread_next(6)
    spread_last(5)
    spread_next(7)
    spread_last(6)
    arrived(5)
    arrived(6)
    send_products(1, 0)
    spread_last(7)
    arrived(7)
    for chunk in range(chunks // 2, chunks):
        weight_copy(chunk, 1 - half).wait_recv()
    send_products(4, chunks // 2)
    low_middle()
    send_products(3, chunks // 2)
    low_end()
    for number in range(2, 5):
        load(number).wait()
    up_rows = up[...].reshape(ADAPTER_COUNT * ADAPTER_RANK, columns)
    for step in range(PASSES):
        choice = spread(objective[step], step)
        low_wide[step] = jnp.dot(
            low_all[...], choice, preferred_element_type=jnp.float32
        ).astype(jnp.bfloat16)
        up_wide[step] = lax.dot_general(
            choice, up_rows, (((0,), (0,)), ((), ())), preferred_element_type=jnp.float32
        ).astype(jnp.bfloat16)
    sums[...] = jnp.zeros(sums.shape, jnp.float32)
    send_products(2, chunks // 2)
    own_products(0)
    send_products(1, chunks // 2)
    own_products(chunks // 2)

    lane = lax.broadcasted_iota(jnp.int32, (LEN, 128), 1)
    stats = jnp.zeros((LEN, 128), jnp.float32)
    for kind in range(2 * PASSES):
        stats = jnp.where(lane == kind, jnp.sum(sums[kind], axis=1, keepdims=True), stats)
    stat_slots[0] = stats.T[: 2 * PASSES]

    def stat_copy(step):
        return remote(
            stat_slots.at[0],
            stat_slots.at[step],
            stat_send.at[step],
            stat_recv.at[step],
            to_tensor(step),
        )

    each_other(lambda step: stat_copy(step).start())
    each_other(lambda step: stat_copy(step).wait())
    totals = jnp.sum(stat_slots[...], axis=0)
    inner_first = jnp.concatenate([totals[1:], totals[:1]], axis=0)
    scale_inv = lax.rsqrt(totals / MODEL_WIDTH + epsilon)
    weight_hidden = inner_first * scale_inv**3 / MODEL_WIDTH
    keep = jnp.concatenate(
        [scale_inv, weight_hidden, jnp.zeros((128 - 4 * PASSES, LEN), jnp.float32)], axis=0
    )
    keep = jnp.where(lax.broadcasted_iota(jnp.int32, keep.shape, 0) % 2 == 0, keep, 0.0)
    by_token = keep.T

    terms = None
    for step in range(PASSES):
        weighted = cotangent[step].astype(jnp.float32) * scale[...]
        per_token = by_token[:, 2 * step : 2 * step + 1]
        back = by_token[:, 2 * PASSES + 2 * step : 2 * PASSES + 2 * step + 1]
        grads[step] = (per_token * weighted - hidden[step] * back).astype(jnp.bfloat16)
        term = lax.dot_general(
            grads[step], up_wide[step], (((1,), (1,)), ((), ())), preferred_element_type=jnp.float32
        )
        terms = term if terms is None else terms + term
    back_terms[...] = terms.reshape(back_terms.shape)
    back_begin()

    per_b = None
    for step in range(PASSES):
        term = lax.dot_general(
            low_wide[step], grads[step], (((0,), (0,)), ((), ())), preferred_element_type=jnp.float32
        )
        per_b = term if per_b is None else per_b + term
    square_b[...] = (per_b * per_b).astype(jnp.bfloat16).reshape(square_b.shape)

    def owner_copy(step, squares, slots, send, recv):
        return remote(
            squares.at[lax.rem(me_d + step, GROUP)],
            slots.at[step],
            send.at[step],
            recv.at[step],
            to_dp(step),
        )

    each_other(lambda step: owner_copy(step, square_b, slots_b, b_send, b_recv).start())

    back_middle()
    back_end()
    per_a = lax.dot_general(
        back_all[...], attention[...], (((0,), (0,)), ((), ())), preferred_element_type=jnp.float32
    )
    square_a[...] = (per_a * per_a).astype(jnp.bfloat16).reshape(square_a.shape)
    each_other(lambda step: owner_copy(step, square_a, slots_a, a_send, a_recv).start())

    per = ADAPTER_RANK // GROUP

    def finish(squares, slots, send, recv, out):
        each_other(lambda step: owner_copy(step, squares, slots, send, recv).wait())
        slots[0] = squares[me_d]
        total = jnp.sum(slots[...].astype(jnp.float32), axis=0)
        for adapter in range(ADAPTER_COUNT):
            chosen = None
            for step in range(PASSES):
                share = jnp.where(objective[step] == adapter, 1.0 / EXAMPLES, 0.0)
                part = share * total[step * per : (step + 1) * per]
                chosen = part if chosen is None else chosen + part
            out[adapter] = chosen

    finish(square_b, slots_b, b_send, b_recv, out_b)

    each_other(lambda step: plane_copy(step, me_t).wait_send())
    for number in range(RING - 1):
        z_copy(number, me_z).wait_send()
    for chunk in range(chunks):
        weight_copy(chunk, half).wait_send()
    for number in range(RING):
        for way in range(2):
            y_copy(number, way, me_t).wait_send()
            f_copy(number, way, me_t).wait_send()
        for shift in range(4):
            core_copy(number, shift, me_t).wait_send()

    def ring_done(chunk, carry):
        for way in range(2):
            for far in range(1, 5):
                ring_copy(way, far, chunk, 0).wait_send()
        return carry

    lax.fori_loop(0, chunks, ring_done, 0)
    finish(square_a, slots_a, a_send, a_recv, out_a)


def body(
    attention,
    output_weight_frozen,
    residual,
    cotangent,
    output_norm_scale,
    adapter_down_weights,
    adapter_up_weights,
    objective,
):
    features = attention.shape[1]
    depth, columns = output_weight_frozen.shape
    chunks = columns // CHUNK
    per = ADAPTER_RANK // GROUP
    wide = PASSES * ADAPTER_RANK
    rows = LEN // GROUP
    bf16, f32 = jnp.bfloat16, jnp.float32
    vmem = pl.BlockSpec(memory_space=pltpu.VMEM)
    hbm = pl.BlockSpec(memory_space=pl.ANY)
    sem = pltpu.SemaphoreType.DMA
    return pl.pallas_call(
        whole_kernel,
        name="fisher",
        out_shape=(
            jax.ShapeDtypeStruct((ADAPTER_COUNT, per, features), f32),
            jax.ShapeDtypeStruct((ADAPTER_COUNT, per, columns), f32),
        ),
        in_specs=[pl.BlockSpec(memory_space=pltpu.SMEM), vmem, vmem] + [hbm] * 5,
        out_specs=(vmem, vmem),
        scratch_shapes=[
            pltpu.VMEM((RING, 2, PIECE, features), bf16),
            pltpu.VMEM((RING, 2, LEN, features), bf16),
            pltpu.VMEM((2, depth, columns), bf16),
            pltpu.VMEM((LEN, columns), bf16),
            pltpu.VMEM((PASSES, LEN, columns), bf16),
            pltpu.VMEM((ADAPTER_COUNT, ADAPTER_RANK, features), bf16),
            pltpu.VMEM((ADAPTER_COUNT, ADAPTER_RANK, columns), bf16),
            pltpu.VMEM((2, 4, chunks, LEN, CHUNK), bf16),
            pltpu.VMEM((2, 4, chunks, LEN, CHUNK), bf16),
            pltpu.VMEM((PASSES, LEN, columns), f32),
            pltpu.VMEM((2 * PASSES, LEN, 128), f32),
            pltpu.VMEM((PASSES, LEN, columns), bf16),
            pltpu.VMEM((GROUP, rows, wide), f32),
            pltpu.VMEM((GROUP, rows, wide), f32),
            pltpu.VMEM((LEN, wide), bf16),
            pltpu.VMEM((PASSES, LEN, wide), bf16),
            pltpu.VMEM((PASSES, wide, columns), bf16),
            pltpu.VMEM((GROUP, 2 * PASSES, LEN), f32),
            pltpu.VMEM((GROUP, rows, wide), f32),
            pltpu.VMEM((GROUP, rows, wide), f32),
            pltpu.VMEM((LEN, wide), bf16),
            pltpu.VMEM((GROUP, wide // GROUP, columns), bf16),
            pltpu.VMEM((GROUP, wide // GROUP, columns), bf16),
            pltpu.VMEM((GROUP, wide // GROUP, features), bf16),
            pltpu.VMEM((GROUP, wide // GROUP, features), bf16),
            sem((5,)),
            sem((GROUP,)),
            sem((GROUP,)),
            sem((RING,)),
            sem((RING,)),
            sem((chunks,)),
            sem((chunks,)),
            sem((RING, 2)),
            sem((RING, 2)),
            sem((RING, 2)),
            sem((RING, 2)),
            sem((RING, 4)),
            sem((RING, 4)),
            sem((2, 4, chunks)),
            sem((2, 4, chunks)),
            sem((4, GROUP)),
            sem((4, GROUP)),
        ]
        + [sem((GROUP,))] * 6,
        compiler_params=pltpu.CompilerParams(
            collective_id=0, has_side_effects=True, vmem_limit_bytes=56 * 2**20
        ),
    )(
        objective,
        output_norm_scale[None],
        attention,
        output_weight_frozen,
        residual,
        cotangent,
        adapter_down_weights,
        adapter_up_weights,
    )


def solution(mesh):
    placed = (
        P("dp", "tensor"),
        P("dp", "tensor"),
        P("dp", "tensor"),
        P(None, "dp", "tensor"),
        P("tensor"),
        P(),
        P(None, None, "tensor"),
        P(),
    )
    return jax.shard_map(
        body,
        mesh=mesh,
        in_specs=placed,
        out_specs=(P(None, "dp", "tensor"), P(None, "dp", "tensor")),
        check_vma=False,
    )
```

```python
import jax
import jax.numpy as jnp
from jax import lax
from jax.experimental import pallas as pl
from jax.experimental.pallas import tpu as pltpu
from jax.sharding import PartitionSpec as P

MODEL_WIDTH = 16384
ADAPTER_RANK = 64
ADAPTER_COUNT = 4
PASSES = 4
LEN = 256
EXAMPLES = 16
GROUP = 16
MESH = pl.DeviceIdType.MESH

epsilon = 1e-05


def to_tensor(step):
    return (lax.axis_index("dp"), lax.rem(lax.axis_index("tensor") + step, GROUP))


def to_dp(step):
    return (lax.rem(lax.axis_index("dp") + step, GROUP), lax.axis_index("tensor"))


def each_other(action):
    def one(step, carry):
        action(step)
        return carry

    lax.fori_loop(1, GROUP, one, 0)


RING = 8
NEAR = (4, 3, -3, 2, -2, 1, -1, 0)
CHUNK = 256
PIECE = 32
DIRECT = 3


def spread(picked, step):
    per = ADAPTER_RANK // GROUP
    size = (ADAPTER_COUNT * ADAPTER_RANK, PASSES * ADAPTER_RANK)
    row = lax.broadcasted_iota(jnp.int32, size, 0)
    col = lax.broadcasted_iota(jnp.int32, size, 1)
    goal = picked * ADAPTER_RANK + col // (PASSES * per) * per + col % per
    chosen = (row == goal) & (col // per % PASSES == step)
    return jnp.where(chosen, 1.0, 0.0).astype(jnp.bfloat16)


def remote(src, dst, send, recv, device):
    return pltpu.make_async_remote_copy(
        src_ref=src,
        dst_ref=dst,
        send_sem=send,
        recv_sem=recv,
        device_id=device,
        device_id_type=MESH,
    )


def whole_kernel(
    objective,
    scale,
    attention,
    weight_hbm,
    residual_hbm,
    cotangent_hbm,
    down_hbm,
    up_hbm,
    out_a,
    out_b,
    middle,
    tokens,
    weight,
    residual,
    cotangent,
    down,
    up,
    ring_out,
    ring_in,
    hidden,
    sums,
    grads,
    low_terms,
    low_slots,
    low_all,
    low_wide,
    up_wide,
    stat_slots,
    back_terms,
    back_slots,
    back_all,
    square_b,
    slots_b,
    square_a,
    slots_a,
    local,
    plane_send,
    plane_recv,
    z_send,
    z_recv,
    x_send,
    x_recv,
    weight_send,
    weight_recv,
    y_send,
    y_recv,
    f_send,
    f_recv,
    core_send,
    core_recv,
    ring_send,
    ring_recv,
    low_sems,
    back_sems,
    stat_send,
    stat_recv,
    b_send,
    b_recv,
    a_send,
    a_recv,
):
    me_d = lax.axis_index("dp")
    me_t = lax.axis_index("tensor")
    half = me_d // RING
    me_z = lax.rem(me_d, RING)
    core = lax.rem(me_t, 2)
    rows = LEN // GROUP
    wide = PASSES * ADAPTER_RANK
    columns = weight.shape[2]
    chunks = columns // CHUNK
    features = attention.shape[1]

    barrier = pltpu.get_barrier_semaphore()

    def greet(step):
        pl.semaphore_signal(barrier, inc=1, device_id=to_tensor(step), device_id_type=MESH)
        pl.semaphore_signal(barrier, inc=1, device_id=to_dp(step), device_id_type=MESH)

    each_other(greet)

    def load(number):
        place = pl.ds(pl.multiple_of(me_t * features, features), features)
        pairs = (
            (down_hbm.at[:, :, place], down),
            (weight_hbm, weight.at[half]),
            (up_hbm, up),
            (residual_hbm, residual),
            (cotangent_hbm, cotangent),
        )
        return pltpu.make_async_copy(*pairs[number], local.at[number])

    for number in range(5):
        load(number).start()

    pl.semaphore_wait(barrier, 2 * (GROUP - 1))

    def piece(t):
        number = lax.rem(t // 4, 2) * 4 + lax.rem(t, 2) * 2 + lax.rem(t // 2, 2)
        return pl.ds(pl.multiple_of(number * PIECE, PIECE), PIECE)

    def both(t):
        number = lax.rem(t // 4, 2) * 2 + lax.rem(t, 2)
        return pl.ds(pl.multiple_of(number * 2 * PIECE, 2 * PIECE), 2 * PIECE)

    side = me_t // RING

    def plane_copy(step, source):
        t = side * RING + lax.rem(me_t + step, RING)
        return remote(
            attention.at[piece(t), :],
            middle.at[source],
            plane_send.at[step],
            plane_recv.at[source],
            (me_d, t),
        )

    own_place = lax.rem(me_t, RING)
    for step in range(1, RING):
        plane_copy(step, own_place).start()
    middle[own_place] = attention[piece(me_t), :]

    def weight_copy(chunk, slot):
        place = pl.ds(chunk * CHUNK, CHUNK)
        return remote(
            weight_hbm.at[:, place],
            weight.at[slot, :, place],
            weight_send.at[chunk],
            weight_recv.at[chunk],
            (lax.rem(me_d + RING, GROUP), me_t),
        )

    for chunk in range(chunks // 2):
        weight_copy(chunk, half).start()

    def add_rows(terms, slots, total, sems):
        def term_copy(step):
            return remote(
                terms.at[lax.rem(me_t + step, GROUP)],
                slots.at[step],
                sems.at[0, step],
                sems.at[1, step],
                to_tensor(step),
            )

        def full_copy(step, owner):
            place = pl.ds(pl.multiple_of(owner * rows, rows), rows)
            return remote(
                total.at[place, :],
                total.at[place, :],
                sems.at[2, step],
                sems.at[3, step],
                to_tensor(step),
            )

        def begin():
            each_other(lambda step: term_copy(step).start())

        def middle():
            each_other(lambda step: term_copy(step).wait())
            slots[0] = terms[me_t]
            mine = pl.ds(pl.multiple_of(me_t * rows, rows), rows)
            total[mine, :] = jnp.sum(slots[...], axis=0).astype(jnp.bfloat16)
            each_other(lambda step: full_copy(step, me_t).start())

        def end():
            each_other(lambda step: full_copy(step, me_t).wait_send())
            each_other(
                lambda step: full_copy(step, lax.rem(me_t + GROUP - step, GROUP)).wait_recv()
            )

        return begin, middle, end

    low_begin, low_middle, low_end = add_rows(low_terms, low_slots, low_all, low_sems)
    back_begin, back_middle, back_end = add_rows(back_terms, back_slots, back_all, back_sems)

    def at_y(shift):
        return lax.rem(me_t + (shift % 4) * 4, GROUP)

    other = me_t + 1 - 2 * core
    across = me_t + 2 - 4 * lax.rem(me_t // 2, 2)

    def z_of(number):
        return lax.rem(me_z + NEAR[number] + RING, RING)

    def z_copy(number, source):
        goal = z_of(number)
        return remote(
            middle.at[goal],
            tokens.at[source, side, piece(me_t), :],
            z_send.at[number],
            z_recv.at[source],
            (half * RING + goal, me_t),
        )

    def along_z(number):
        goal = z_of(number)
        pl.when(goal != own_place)(plane_copy(1, goal).wait_recv)
        if NEAR[number] == 0:
            tokens[me_z, side, piece(me_t), :] = middle[me_z]
        else:
            z_copy(number, me_z).start()

    def x_copy(number, owner):
        part = tokens.at[z_of(number), side, piece(owner), :]
        return remote(part, part, x_send.at[number], x_recv.at[number], (me_d, across))

    def y_copy(number, way, owner):
        part = tokens.at[z_of(number), owner // RING, both(owner), :]
        return remote(
            part,
            part,
            y_send.at[number, way],
            y_recv.at[number, way],
            (me_d, at_y((1, -1, 2)[way])),
        )

    def f_copy(number, way, owner):
        start = lax.rem(owner // 4, 2) * 4 + lax.rem(owner, 2) * 2 + way
        place = pl.ds(pl.multiple_of(start * PIECE, PIECE), PIECE)
        part = tokens.at[z_of(number), owner // RING, place, :]
        return remote(
            part, part, f_send.at[number, way], f_recv.at[number, way], (me_d, at_y((1, -1)[way]))
        )

    def core_copy(number, shift, owner):
        part = tokens.at[z_of(number), owner // RING, both(owner), :]
        return remote(
            part, part, core_send.at[number, shift], core_recv.at[number, shift], (me_d, other)
        )

    def over_x(number):
        if NEAR[number] != 0:
            z_copy(number, z_of(number)).wait_recv()
        x_copy(number, me_t).start()

    def spread_own(number):
        x_copy(number, across).wait_recv()
        y_copy(number, 0, me_t).start()
        y_copy(number, 1, me_t).start()
        if number < DIRECT:
            y_copy(number, 2, me_t).start()
        core_copy(number, 0, me_t).start()

    def spread_next(number):
        y_copy(number, 0, at_y(-1)).wait_recv()
        if number >= DIRECT:
            f_copy(number, 0, at_y(-1)).start()
        core_copy(number, 3, at_y(-1)).start()
        y_copy(number, 1, at_y(1)).wait_recv()
        if number >= DIRECT:
            f_copy(number, 1, at_y(1)).start()
        core_copy(number, 1, at_y(1)).start()

    def spread_last(number):
        if number < DIRECT:
            y_copy(number, 2, at_y(2)).wait_recv()
        else:
            f_copy(number, 0, at_y(2)).wait_recv()
            f_copy(number, 1, at_y(2)).wait_recv()
        core_copy(number, 2, at_y(2)).start()

    def arrived(number):
        for shift in range(4):
            owner = lax.rem(other + shift * 4, GROUP)
            core_copy(number, shift, owner).wait_recv()

    def product(number, cols):
        z = z_of(number)
        total = jnp.dot(tokens[z, 0], weight[0, :, cols], preferred_element_type=jnp.float32)
        return total + jnp.dot(
            tokens[z, 1], weight[1, :, cols], preferred_element_type=jnp.float32
        )

    def ring_copy(way, far, chunk, slot):
        if far == 4:
            place = pl.ds(way * (LEN // 2), LEN // 2)
        else:
            place = pl.ds(0, LEN)
        z = lax.rem(me_z + (1, RING - 1)[way], RING)
        return remote(
            ring_out.at[way, far - 1, chunk, place, :],
            ring_in.at[way, far - 1, chunk, place, :],
            ring_send.at[way, far - 1, chunk],
            ring_recv.at[way, far - 1, chunk],
            (half * RING + z, me_t),
        )

    def cols_of(chunk):
        return pl.ds(pl.multiple_of(chunk * CHUNK, CHUNK), CHUNK)

    def send_products(far, begin):
        def one(chunk, carry):
            cols = cols_of(chunk)
            if far == 4:
                value = product(0, cols).astype(jnp.bfloat16)
                for way in range(2):
                    mine = slice(way * (LEN // 2), (way + 1) * (LEN // 2))
                    ring_out[way, 3, chunk, mine, :] = value[mine]
                    ring_copy(way, 4, chunk, 0).start()
                return carry
            for way in range(2):
                number = NEAR.index((far, -far)[way])
                value = product(number, cols)
                ring_copy(way, far + 1, chunk, 0).wait_recv()
                if far == 3:
                    mine = slice(way * (LEN // 2), (way + 1) * (LEN // 2))
                    rest = slice((1 - way) * (LEN // 2), (2 - way) * (LEN // 2))
                    ring_out[way, 2, chunk, mine, :] = (
                        value[mine] + ring_in[way, 3, chunk, mine, :].astype(jnp.float32)
                    ).astype(jnp.bfloat16)
                    ring_out[way, 2, chunk, rest, :] = value[rest].astype(jnp.bfloat16)
                else:
                    ring_out[way, far - 1, chunk] = (
                        value + ring_in[way, far, chunk].astype(jnp.float32)
                    ).astype(jnp.bfloat16)
                ring_copy(way, far, chunk, 0).start()
            return carry

        lax.fori_loop(begin, begin + chunks // 2, one, 0)

    def own_products(begin):
        def one(chunk, carry):
            cols = cols_of(chunk)
            value = product(NEAR.index(0), cols)
            for way in range(2):
                ring_copy(way, 1, chunk, 0).wait_recv()
                value = value + ring_in[way, 0, chunk].astype(jnp.float32)
            value = value + residual[:, cols].astype(jnp.float32)
            for step in range(PASSES):
                here = value + jnp.dot(
                    low_wide[step], up_wide[step, :, cols], preferred_element_type=jnp.float32
                )
                hidden[step, :, cols] = here
                weighted = cotangent[step, :, cols].astype(jnp.float32) * scale[:, cols]
                squares = here * here
                inner = weighted * here
                sums[2 * step] += squares[:, :128] + squares[:, 128:]
                sums[2 * step + 1] += inner[:, :128] + inner[:, 128:]
            return carry

        lax.fori_loop(begin, begin + chunks // 2, one, 0)

    for number in range(RING):
        along_z(number)
    over_x(0)
    over_x(1)
    over_x(2)
    spread_own(0)
    over_x(3)
    over_x(4)
    spread_own(1)
    over_x(5)
    spread_next(0)
    spread_own(2)
    over_x(6)
    over_x(7)
    spread_next(1)
    spread_last(0)
    spread_own(3)
    load(1).wait()
    for chunk in range(chunks // 2):
        weight_copy(chunk, 1 - half).wait_recv()
    arrived(0)
    send_products(4, 0)
    for chunk in range(chunks // 2, chunks):
        weight_copy(chunk, half).start()
    spread_next(2)
    spread_last(1)
    spread_own(4)
    spread_next(3)
    spread_last(2)
    arrived(1)
    arrived(2)
    send_products(3, 0)
    load(0).wait()
    low_terms[...] = lax.dot_general(
        attention[...],
        down[...].reshape(ADAPTER_COUNT * ADAPTER_RANK, features),
        (((1,), (1,)), ((), ())),
        preferred_element_type=jnp.float32,
    ).reshape(low_terms.shape)
    low_begin()
    spread_own(5)
    spread_next(4)
    spread_last(3)
    spread_own(6)
    spread_next(5)
    spread_last(4)
    arrived(3)
    arrived(4)
    send_products(2, 0)
    spread_own(7)
    spread_next(6)
    spread_last(5)
    spread_next(7)
    spread_last(6)
    arrived(5)
    arrived(6)
    send_products(1, 0)
    spread_last(7)
    arrived(7)
    for chunk in range(chunks // 2, chunks):
        weight_copy(chunk, 1 - half).wait_recv()
    send_products(4, chunks // 2)
    low_middle()
    send_products(3, chunks // 2)
    low_end()
    for number in range(2, 5):
        load(number).wait()
    up_rows = up[...].reshape(ADAPTER_COUNT * ADAPTER_RANK, columns)
    for step in range(PASSES):
        choice = spread(objective[step], step)
        low_wide[step] = jnp.dot(
            low_all[...], choice, preferred_element_type=jnp.float32
        ).astype(jnp.bfloat16)
        up_wide[step] = lax.dot_general(
            choice, up_rows, (((0,), (0,)), ((), ())), preferred_element_type=jnp.float32
        ).astype(jnp.bfloat16)
    sums[...] = jnp.zeros(sums.shape, jnp.float32)
    send_products(2, chunks // 2)
    own_products(0)
    send_products(1, chunks // 2)
    own_products(chunks // 2)

    lane = lax.broadcasted_iota(jnp.int32, (LEN, 128), 1)
    stats = jnp.zeros((LEN, 128), jnp.float32)
    for kind in range(2 * PASSES):
        stats = jnp.where(lane == kind, jnp.sum(sums[kind], axis=1, keepdims=True), stats)
    stat_slots[0] = stats.T[: 2 * PASSES]

    def stat_copy(step):
        return remote(
            stat_slots.at[0],
            stat_slots.at[step],
            stat_send.at[step],
            stat_recv.at[step],
            to_tensor(step),
        )

    each_other(lambda step: stat_copy(step).start())
    each_other(lambda step: stat_copy(step).wait())
    totals = jnp.sum(stat_slots[...], axis=0)
    inner_first = jnp.concatenate([totals[1:], totals[:1]], axis=0)
    scale_inv = lax.rsqrt(totals / MODEL_WIDTH + epsilon)
    weight_hidden = inner_first * scale_inv**3 / MODEL_WIDTH
    keep = jnp.concatenate(
        [scale_inv, weight_hidden, jnp.zeros((128 - 4 * PASSES, LEN), jnp.float32)], axis=0
    )
    keep = jnp.where(lax.broadcasted_iota(jnp.int32, keep.shape, 0) % 2 == 0, keep, 0.0)
    by_token = keep.T

    terms = None
    for step in range(PASSES):
        weighted = cotangent[step].astype(jnp.float32) * scale[...]
        per_token = by_token[:, 2 * step : 2 * step + 1]
        back = by_token[:, 2 * PASSES + 2 * step : 2 * PASSES + 2 * step + 1]
        grads[step] = (per_token * weighted - hidden[step] * back).astype(jnp.bfloat16)
        term = lax.dot_general(
            grads[step], up_wide[step], (((1,), (1,)), ((), ())), preferred_element_type=jnp.float32
        )
        terms = term if terms is None else terms + term
    back_terms[...] = terms.reshape(back_terms.shape)
    back_begin()

    per_b = None
    for step in range(PASSES):
        term = lax.dot_general(
            low_wide[step], grads[step], (((0,), (0,)), ((), ())), preferred_element_type=jnp.float32
        )
        per_b = term if per_b is None else per_b + term
    square_b[...] = (per_b * per_b).astype(jnp.bfloat16).reshape(square_b.shape)

    def owner_copy(step, squares, slots, send, recv):
        return remote(
            squares.at[lax.rem(me_d + step, GROUP)],
            slots.at[step],
            send.at[step],
            recv.at[step],
            to_dp(step),
        )

    each_other(lambda step: owner_copy(step, square_b, slots_b, b_send, b_recv).start())

    back_middle()
    back_end()
    per_a = lax.dot_general(
        back_all[...], attention[...], (((0,), (0,)), ((), ())), preferred_element_type=jnp.float32
    )
    square_a[...] = (per_a * per_a).astype(jnp.bfloat16).reshape(square_a.shape)
    each_other(lambda step: owner_copy(step, square_a, slots_a, a_send, a_recv).start())

    per = ADAPTER_RANK // GROUP

    def finish(squares, slots, send, recv, out):
        each_other(lambda step: owner_copy(step, squares, slots, send, recv).wait())
        slots[0] = squares[me_d]
        total = jnp.sum(slots[...].astype(jnp.float32), axis=0)
        for adapter in range(ADAPTER_COUNT):
            chosen = None
            for step in range(PASSES):
                share = jnp.where(objective[step] == adapter, 1.0 / EXAMPLES, 0.0)
                part = share * total[step * per : (step + 1) * per]
                chosen = part if chosen is None else chosen + part
            out[adapter] = chosen

    finish(square_b, slots_b, b_send, b_recv, out_b)

    for step in range(1, RING):
        plane_copy(step, own_place).wait_send()
    for number in range(RING - 1):
        z_copy(number, me_z).wait_send()
    for chunk in range(chunks):
        weight_copy(chunk, half).wait_send()
    for number in range(RING):
        x_copy(number, me_t).wait_send()
        for way in range(2):
            y_copy(number, way, me_t).wait_send()
        if number < DIRECT:
            y_copy(number, 2, me_t).wait_send()
        else:
            for way in range(2):
                f_copy(number, way, me_t).wait_send()
        for shift in range(4):
            core_copy(number, shift, me_t).wait_send()

    def ring_done(chunk, carry):
        for way in range(2):
            for far in range(1, 5):
                ring_copy(way, far, chunk, 0).wait_send()
        return carry

    lax.fori_loop(0, chunks, ring_done, 0)
    finish(square_a, slots_a, a_send, a_recv, out_a)


def body(
    attention,
    output_weight_frozen,
    residual,
    cotangent,
    output_norm_scale,
    adapter_down_weights,
    adapter_up_weights,
    objective,
):
    features = attention.shape[1]
    depth, columns = output_weight_frozen.shape
    chunks = columns // CHUNK
    per = ADAPTER_RANK // GROUP
    wide = PASSES * ADAPTER_RANK
    rows = LEN // GROUP
    bf16, f32 = jnp.bfloat16, jnp.float32
    vmem = pl.BlockSpec(memory_space=pltpu.VMEM)
    hbm = pl.BlockSpec(memory_space=pl.ANY)
    sem = pltpu.SemaphoreType.DMA
    return pl.pallas_call(
        whole_kernel,
        name="fisher",
        out_shape=(
            jax.ShapeDtypeStruct((ADAPTER_COUNT, per, features), f32),
            jax.ShapeDtypeStruct((ADAPTER_COUNT, per, columns), f32),
        ),
        in_specs=[pl.BlockSpec(memory_space=pltpu.SMEM), vmem, vmem] + [hbm] * 5,
        out_specs=(vmem, vmem),
        scratch_shapes=[
            pltpu.VMEM((RING, PIECE, features), bf16),
            pltpu.VMEM((RING, 2, LEN, features), bf16),
            pltpu.VMEM((2, depth, columns), bf16),
            pltpu.VMEM((LEN, columns), bf16),
            pltpu.VMEM((PASSES, LEN, columns), bf16),
            pltpu.VMEM((ADAPTER_COUNT, ADAPTER_RANK, features), bf16),
            pltpu.VMEM((ADAPTER_COUNT, ADAPTER_RANK, columns), bf16),
            pltpu.VMEM((2, 4, chunks, LEN, CHUNK), bf16),
            pltpu.VMEM((2, 4, chunks, LEN, CHUNK), bf16),
            pltpu.VMEM((PASSES, LEN, columns), f32),
            pltpu.VMEM((2 * PASSES, LEN, 128), f32),
            pltpu.VMEM((PASSES, LEN, columns), bf16),
            pltpu.VMEM((GROUP, rows, wide), f32),
            pltpu.VMEM((GROUP, rows, wide), f32),
            pltpu.VMEM((LEN, wide), bf16),
            pltpu.VMEM((PASSES, LEN, wide), bf16),
            pltpu.VMEM((PASSES, wide, columns), bf16),
            pltpu.VMEM((GROUP, 2 * PASSES, LEN), f32),
            pltpu.VMEM((GROUP, rows, wide), f32),
            pltpu.VMEM((GROUP, rows, wide), f32),
            pltpu.VMEM((LEN, wide), bf16),
            pltpu.VMEM((GROUP, wide // GROUP, columns), bf16),
            pltpu.VMEM((GROUP, wide // GROUP, columns), bf16),
            pltpu.VMEM((GROUP, wide // GROUP, features), bf16),
            pltpu.VMEM((GROUP, wide // GROUP, features), bf16),
            sem((5,)),
            sem((RING,)),
            sem((RING,)),
            sem((RING,)),
            sem((RING,)),
            sem((RING,)),
            sem((RING,)),
            sem((chunks,)),
            sem((chunks,)),
            sem((RING, 3)),
            sem((RING, 3)),
            sem((RING, 2)),
            sem((RING, 2)),
            sem((RING, 4)),
            sem((RING, 4)),
            sem((2, 4, chunks)),
            sem((2, 4, chunks)),
            sem((4, GROUP)),
            sem((4, GROUP)),
        ]
        + [sem((GROUP,))] * 6,
        compiler_params=pltpu.CompilerParams(
            collective_id=0, has_side_effects=True, vmem_limit_bytes=56 * 2**20
        ),
    )(
        objective,
        output_norm_scale[None],
        attention,
        output_weight_frozen,
        residual,
        cotangent,
        adapter_down_weights,
        adapter_up_weights,
    )


def solution(mesh):
    placed = (
        P("dp", "tensor"),
        P("dp", "tensor"),
        P("dp", "tensor"),
        P(None, "dp", "tensor"),
        P("tensor"),
        P(),
        P(None, None, "tensor"),
        P(),
    )
    return jax.shard_map(
        body,
        mesh=mesh,
        in_specs=placed,
        out_specs=(P(None, "dp", "tensor"), P(None, "dp", "tensor")),
        check_vma=False,
    )
```

```python
import jax
import jax.numpy as jnp
from jax import lax
from jax.experimental import pallas as pl
from jax.experimental.pallas import tpu as pltpu
from jax.sharding import PartitionSpec as P

MODEL_WIDTH = 16384
ADAPTER_RANK = 64
ADAPTER_COUNT = 4
PASSES = 4
LEN = 256
EXAMPLES = 16
GROUP = 16
MESH = pl.DeviceIdType.MESH

epsilon = 1e-05


def to_tensor(step):
    return (lax.axis_index("dp"), lax.rem(lax.axis_index("tensor") + step, GROUP))


def to_dp(step):
    return (lax.rem(lax.axis_index("dp") + step, GROUP), lax.axis_index("tensor"))


def each_other(action):
    def one(step, carry):
        action(step)
        return carry

    lax.fori_loop(1, GROUP, one, 0)


RING = 8
NEAR = (4, 3, -3, 2, -2, 1, -1, 0)
CHUNK = 256
PIECE = 32


def spread(picked, step):
    per = ADAPTER_RANK // GROUP
    size = (ADAPTER_COUNT * ADAPTER_RANK, PASSES * ADAPTER_RANK)
    row = lax.broadcasted_iota(jnp.int32, size, 0)
    col = lax.broadcasted_iota(jnp.int32, size, 1)
    goal = picked * ADAPTER_RANK + col // (PASSES * per) * per + col % per
    chosen = (row == goal) & (col // per % PASSES == step)
    return jnp.where(chosen, 1.0, 0.0).astype(jnp.bfloat16)


def remote(src, dst, send, recv, device):
    return pltpu.make_async_remote_copy(
        src_ref=src,
        dst_ref=dst,
        send_sem=send,
        recv_sem=recv,
        device_id=device,
        device_id_type=MESH,
    )


def whole_kernel(
    objective,
    scale,
    attention,
    weight_hbm,
    residual_hbm,
    cotangent_hbm,
    down_hbm,
    up_hbm,
    out_a,
    out_b,
    middle,
    tokens,
    weight,
    residual,
    cotangent,
    down,
    up,
    ring_out,
    ring_in,
    hidden,
    sums,
    grads,
    low_terms,
    low_slots,
    low_all,
    low_wide,
    up_wide,
    stat_slots,
    back_terms,
    back_slots,
    back_all,
    square_b,
    slots_b,
    square_a,
    slots_a,
    local,
    plane_send,
    plane_recv,
    z_send,
    z_recv,
    x_send,
    x_recv,
    weight_send,
    weight_recv,
    y_send,
    y_recv,
    core_send,
    core_recv,
    ring_send,
    ring_recv,
    low_sems,
    back_sems,
    stat_send,
    stat_recv,
    b_send,
    b_recv,
    a_send,
    a_recv,
):
    me_d = lax.axis_index("dp")
    me_t = lax.axis_index("tensor")
    half = me_d // RING
    me_z = lax.rem(me_d, RING)
    core = lax.rem(me_t, 2)
    rows = LEN // GROUP
    wide = PASSES * ADAPTER_RANK
    columns = weight.shape[2]
    chunks = columns // CHUNK
    features = attention.shape[1]

    barrier = pltpu.get_barrier_semaphore()

    def greet(step):
        pl.semaphore_signal(barrier, inc=1, device_id=to_tensor(step), device_id_type=MESH)
        pl.semaphore_signal(barrier, inc=1, device_id=to_dp(step), device_id_type=MESH)

    each_other(greet)

    def load(number):
        place = pl.ds(pl.multiple_of(me_t * features, features), features)
        pairs = (
            (down_hbm.at[:, :, place], down),
            (weight_hbm, weight.at[half]),
            (up_hbm, up),
            (residual_hbm, residual),
            (cotangent_hbm, cotangent),
        )
        return pltpu.make_async_copy(*pairs[number], local.at[number])

    for number in range(5):
        load(number).start()

    pl.semaphore_wait(barrier, 2 * (GROUP - 1))

    def piece(t):
        number = lax.rem(t // 4, 2) * 4 + lax.rem(t, 2) * 2 + lax.rem(t // 2, 2)
        return pl.ds(pl.multiple_of(number * PIECE, PIECE), PIECE)

    def both(t):
        number = lax.rem(t // 4, 2) * 2 + lax.rem(t, 2)
        return pl.ds(pl.multiple_of(number * 2 * PIECE, 2 * PIECE), 2 * PIECE)

    side = me_t // RING

    def plane_copy(step, source):
        t = side * RING + lax.rem(me_t + step, RING)
        return remote(
            attention.at[piece(t), :],
            middle.at[source],
            plane_send.at[step],
            plane_recv.at[source],
            (me_d, t),
        )

    def weight_copy(chunk, slot):
        place = pl.ds(chunk * CHUNK, CHUNK)
        return remote(
            weight_hbm.at[:, place],
            weight.at[slot, :, place],
            weight_send.at[chunk],
            weight_recv.at[chunk],
            (lax.rem(me_d + RING, GROUP), me_t),
        )

    own_place = lax.rem(me_t, RING)
    for step in range(1, RING):
        plane_copy(step, own_place).start()
    middle[own_place] = attention[piece(me_t), :]

    weight_copy(0, half).start()

    def add_rows(terms, slots, total, sems):
        def term_copy(step):
            return remote(
                terms.at[lax.rem(me_t + step, GROUP)],
                slots.at[step],
                sems.at[0, step],
                sems.at[1, step],
                to_tensor(step),
            )

        def full_copy(step, owner):
            place = pl.ds(pl.multiple_of(owner * rows, rows), rows)
            return remote(
                total.at[place, :],
                total.at[place, :],
                sems.at[2, step],
                sems.at[3, step],
                to_tensor(step),
            )

        def begin():
            each_other(lambda step: term_copy(step).start())

        def middle():
            each_other(lambda step: term_copy(step).wait())
            slots[0] = terms[me_t]
            mine = pl.ds(pl.multiple_of(me_t * rows, rows), rows)
            total[mine, :] = jnp.sum(slots[...], axis=0).astype(jnp.bfloat16)
            each_other(lambda step: full_copy(step, me_t).start())

        def end():
            each_other(lambda step: full_copy(step, me_t).wait_send())
            each_other(
                lambda step: full_copy(step, lax.rem(me_t + GROUP - step, GROUP)).wait_recv()
            )

        return begin, middle, end

    low_begin, low_middle, low_end = add_rows(low_terms, low_slots, low_all, low_sems)
    back_begin, back_middle, back_end = add_rows(back_terms, back_slots, back_all, back_sems)

    def at_y(shift):
        return lax.rem(me_t + (shift % 4) * 4, GROUP)

    other = me_t + 1 - 2 * core
    across = me_t + 2 - 4 * lax.rem(me_t // 2, 2)

    def z_of(number):
        return lax.rem(me_z + NEAR[number] + RING, RING)

    def z_copy(number, source):
        goal = z_of(number)
        return remote(
            middle.at[goal],
            tokens.at[source, side, piece(me_t), :],
            z_send.at[number],
            z_recv.at[source],
            (half * RING + goal, me_t),
        )

    def along_z(number):
        goal = z_of(number)
        pl.when(goal != own_place)(plane_copy(1, goal).wait_recv)
        if NEAR[number] == 0:
            tokens[me_z, side, piece(me_t), :] = middle[me_z]
        else:
            z_copy(number, me_z).start()

    def x_copy(number, owner):
        part = tokens.at[z_of(number), side, piece(owner), :]
        return remote(part, part, x_send.at[number], x_recv.at[number], (me_d, across))

    def y_copy(number, way, owner):
        part = tokens.at[z_of(number), owner // RING, both(owner), :]
        return remote(
            part,
            part,
            y_send.at[number, way],
            y_recv.at[number, way],
            (me_d, at_y((1, -1, 2)[way])),
        )

    def core_copy(number, shift, owner):
        part = tokens.at[z_of(number), owner // RING, both(owner), :]
        return remote(
            part, part, core_send.at[number, shift], core_recv.at[number, shift], (me_d, other)
        )

    def over_x(number):
        if NEAR[number] != 0:
            z_copy(number, z_of(number)).wait_recv()
        x_copy(number, me_t).start()

    def spread_own(number):
        x_copy(number, across).wait_recv()
        y_copy(number, 2, me_t).start()
        y_copy(number, 0, me_t).start()
        y_copy(number, 1, me_t).start()
        core_copy(number, 0, me_t).start()

    def pass_on(number):
        for way, shift in ((0, -1), (1, 1), (2, 2)):
            y_copy(number, way, at_y(shift)).wait_recv()
            core_copy(number, shift % 4, at_y(shift)).start()

    def arrived(number):
        for shift in range(4):
            owner = lax.rem(other + shift * 4, GROUP)
            core_copy(number, shift, owner).wait_recv()

    def product(number, cols):
        z = z_of(number)
        total = jnp.dot(tokens[z, 0], weight[0, :, cols], preferred_element_type=jnp.float32)
        return total + jnp.dot(
            tokens[z, 1], weight[1, :, cols], preferred_element_type=jnp.float32
        )

    def ring_copy(way, far, chunk):
        if far == 4:
            place = pl.ds(way * (LEN // 2), LEN // 2)
        else:
            place = pl.ds(0, LEN)
        z = lax.rem(me_z + (1, RING - 1)[way], RING)
        return remote(
            ring_out.at[way, far - 1, chunk, place, :],
            ring_in.at[way, far - 1, chunk, place, :],
            ring_send.at[way, far - 1, chunk],
            ring_recv.at[way, far - 1, chunk],
            (half * RING + z, me_t),
        )

    def cols_of(chunk):
        return pl.ds(chunk * CHUNK, CHUNK)

    def send_products(far, chunk):
        cols = cols_of(chunk)
        if far == 4:
            value = product(0, cols).astype(jnp.bfloat16)
            for way in range(2):
                mine = slice(way * (LEN // 2), (way + 1) * (LEN // 2))
                ring_out[way, 3, chunk, mine, :] = value[mine]
                ring_copy(way, 4, chunk).start()
            return
        for way in range(2):
            value = product(NEAR.index((far, -far)[way]), cols)
            ring_copy(way, far + 1, chunk).wait_recv()
            if far == 3:
                mine = slice(way * (LEN // 2), (way + 1) * (LEN // 2))
                rest = slice((1 - way) * (LEN // 2), (2 - way) * (LEN // 2))
                ring_out[way, 2, chunk, mine, :] = (
                    value[mine] + ring_in[way, 3, chunk, mine, :].astype(jnp.float32)
                ).astype(jnp.bfloat16)
                ring_out[way, 2, chunk, rest, :] = value[rest].astype(jnp.bfloat16)
            else:
                ring_out[way, far - 1, chunk] = (
                    value + ring_in[way, far, chunk].astype(jnp.float32)
                ).astype(jnp.bfloat16)
            ring_copy(way, far, chunk).start()

    def own_products(chunk):
        cols = cols_of(chunk)
        value = product(NEAR.index(0), cols)
        for way in range(2):
            ring_copy(way, 1, chunk).wait_recv()
            value = value + ring_in[way, 0, chunk].astype(jnp.float32)
        value = value + residual[:, cols].astype(jnp.float32)
        for step in range(PASSES):
            here = value + jnp.dot(
                low_wide[step], up_wide[step, :, cols], preferred_element_type=jnp.float32
            )
            hidden[step, :, cols] = here
            weighted = cotangent[step, :, cols].astype(jnp.float32) * scale[:, cols]
            squares = here * here
            inner = weighted * here
            sums[2 * step] += squares[:, :128] + squares[:, 128:]
            sums[2 * step + 1] += inner[:, :128] + inner[:, 128:]

    along_z(0)
    along_z(1)
    along_z(2)
    along_z(3)
    along_z(4)
    along_z(5)
    along_z(6)
    along_z(7)
    over_x(0)
    over_x(1)
    over_x(2)
    over_x(3)
    over_x(4)
    over_x(5)
    over_x(6)
    over_x(7)
    weight_copy(1, half).start()
    spread_own(0)
    spread_own(1)
    spread_own(2)
    spread_own(3)
    spread_own(4)
    spread_own(5)
    spread_own(6)
    spread_own(7)
    weight_copy(2, half).start()
    weight_copy(3, half).start()
    pass_on(0)
    load(1).wait()
    weight_copy(0, 1 - half).wait_recv()
    arrived(0)
    send_products(4, 0)
    weight_copy(1, 1 - half).wait_recv()
    send_products(4, 1)
    pass_on(1)
    pass_on(2)
    arrived(1)
    arrived(2)
    send_products(3, 0)
    send_products(3, 1)
    load(0).wait()
    low_terms[...] = lax.dot_general(
        attention[...],
        down[...].reshape(ADAPTER_COUNT * ADAPTER_RANK, features),
        (((1,), (1,)), ((), ())),
        preferred_element_type=jnp.float32,
    ).reshape(low_terms.shape)
    low_begin()
    pass_on(3)
    pass_on(4)
    arrived(3)
    arrived(4)
    send_products(2, 0)
    send_products(2, 1)
    weight_copy(2, 1 - half).wait_recv()
    weight_copy(3, 1 - half).wait_recv()
    send_products(4, 2)
    send_products(4, 3)
    pass_on(5)
    pass_on(6)
    arrived(5)
    arrived(6)
    send_products(1, 0)
    send_products(1, 1)
    low_middle()
    pass_on(7)
    send_products(3, 2)
    send_products(3, 3)
    low_end()
    for number in range(2, 5):
        load(number).wait()
    up_rows = up[...].reshape(ADAPTER_COUNT * ADAPTER_RANK, columns)
    for step in range(PASSES):
        choice = spread(objective[step], step)
        low_wide[step] = jnp.dot(
            low_all[...], choice, preferred_element_type=jnp.float32
        ).astype(jnp.bfloat16)
        up_wide[step] = lax.dot_general(
            choice, up_rows, (((0,), (0,)), ((), ())), preferred_element_type=jnp.float32
        ).astype(jnp.bfloat16)
    sums[...] = jnp.zeros(sums.shape, jnp.float32)
    arrived(7)
    own_products(0)
    own_products(1)
    send_products(2, 2)
    send_products(2, 3)
    send_products(1, 2)
    send_products(1, 3)
    own_products(2)
    own_products(3)

    lane = lax.broadcasted_iota(jnp.int32, (LEN, 128), 1)
    stats = jnp.zeros((LEN, 128), jnp.float32)
    for kind in range(2 * PASSES):
        stats = jnp.where(lane == kind, jnp.sum(sums[kind], axis=1, keepdims=True), stats)
    stat_slots[0] = stats.T[: 2 * PASSES]

    def stat_copy(step):
        return remote(
            stat_slots.at[0],
            stat_slots.at[step],
            stat_send.at[step],
            stat_recv.at[step],
            to_tensor(step),
        )

    each_other(lambda step: stat_copy(step).start())
    each_other(lambda step: stat_copy(step).wait())
    totals = jnp.sum(stat_slots[...], axis=0)
    inner_first = jnp.concatenate([totals[1:], totals[:1]], axis=0)
    scale_inv = lax.rsqrt(totals / MODEL_WIDTH + epsilon)
    weight_hidden = inner_first * scale_inv**3 / MODEL_WIDTH
    keep = jnp.concatenate(
        [scale_inv, weight_hidden, jnp.zeros((128 - 4 * PASSES, LEN), jnp.float32)], axis=0
    )
    keep = jnp.where(lax.broadcasted_iota(jnp.int32, keep.shape, 0) % 2 == 0, keep, 0.0)
    by_token = keep.T

    terms = None
    for step in range(PASSES):
        weighted = cotangent[step].astype(jnp.float32) * scale[...]
        per_token = by_token[:, 2 * step : 2 * step + 1]
        back = by_token[:, 2 * PASSES + 2 * step : 2 * PASSES + 2 * step + 1]
        grads[step] = (per_token * weighted - hidden[step] * back).astype(jnp.bfloat16)
        term = lax.dot_general(
            grads[step], up_wide[step], (((1,), (1,)), ((), ())), preferred_element_type=jnp.float32
        )
        terms = term if terms is None else terms + term
    back_terms[...] = terms.reshape(back_terms.shape)
    back_begin()

    per_b = None
    for step in range(PASSES):
        term = lax.dot_general(
            low_wide[step], grads[step], (((0,), (0,)), ((), ())), preferred_element_type=jnp.float32
        )
        per_b = term if per_b is None else per_b + term
    square_b[...] = (per_b * per_b).astype(jnp.bfloat16).reshape(square_b.shape)

    def owner_copy(step, squares, slots, send, recv):
        return remote(
            squares.at[lax.rem(me_d + step, GROUP)],
            slots.at[step],
            send.at[step],
            recv.at[step],
            to_dp(step),
        )

    each_other(lambda step: owner_copy(step, square_b, slots_b, b_send, b_recv).start())

    back_middle()
    back_end()
    per_a = lax.dot_general(
        back_all[...], attention[...], (((0,), (0,)), ((), ())), preferred_element_type=jnp.float32
    )
    square_a[...] = (per_a * per_a).astype(jnp.bfloat16).reshape(square_a.shape)
    each_other(lambda step: owner_copy(step, square_a, slots_a, a_send, a_recv).start())

    per = ADAPTER_RANK // GROUP

    def finish(squares, slots, send, recv, out):
        each_other(lambda step: owner_copy(step, squares, slots, send, recv).wait())
        slots[0] = squares[me_d]
        total = jnp.sum(slots[...].astype(jnp.float32), axis=0)
        for adapter in range(ADAPTER_COUNT):
            chosen = None
            for step in range(PASSES):
                share = jnp.where(objective[step] == adapter, 1.0 / EXAMPLES, 0.0)
                part = share * total[step * per : (step + 1) * per]
                chosen = part if chosen is None else chosen + part
            out[adapter] = chosen

    finish(square_b, slots_b, b_send, b_recv, out_b)

    for step in range(1, RING):
        plane_copy(step, own_place).wait_send()
    for number in range(RING - 1):
        z_copy(number, me_z).wait_send()
    for chunk in range(chunks):
        weight_copy(chunk, half).wait_send()
    for number in range(RING):
        x_copy(number, me_t).wait_send()
        for way in range(3):
            y_copy(number, way, me_t).wait_send()
        for shift in range(4):
            core_copy(number, shift, me_t).wait_send()

    def ring_done(chunk, carry):
        for way in range(2):
            for far in range(1, 5):
                ring_copy(way, far, chunk).wait_send()
        return carry

    lax.fori_loop(0, chunks, ring_done, 0)
    finish(square_a, slots_a, a_send, a_recv, out_a)


def body(
    attention,
    output_weight_frozen,
    residual,
    cotangent,
    output_norm_scale,
    adapter_down_weights,
    adapter_up_weights,
    objective,
):
    features = attention.shape[1]
    depth, columns = output_weight_frozen.shape
    chunks = columns // CHUNK
    per = ADAPTER_RANK // GROUP
    wide = PASSES * ADAPTER_RANK
    rows = LEN // GROUP
    bf16, f32 = jnp.bfloat16, jnp.float32
    vmem = pl.BlockSpec(memory_space=pltpu.VMEM)
    hbm = pl.BlockSpec(memory_space=pl.ANY)
    sem = pltpu.SemaphoreType.DMA
    return pl.pallas_call(
        whole_kernel,
        name="fisher",
        out_shape=(
            jax.ShapeDtypeStruct((ADAPTER_COUNT, per, features), f32),
            jax.ShapeDtypeStruct((ADAPTER_COUNT, per, columns), f32),
        ),
        in_specs=[pl.BlockSpec(memory_space=pltpu.SMEM), vmem, vmem] + [hbm] * 5,
        out_specs=(vmem, vmem),
        scratch_shapes=[
            pltpu.VMEM((RING, PIECE, features), bf16),
            pltpu.VMEM((RING, 2, LEN, features), bf16),
            pltpu.VMEM((2, depth, columns), bf16),
            pltpu.VMEM((LEN, columns), bf16),
            pltpu.VMEM((PASSES, LEN, columns), bf16),
            pltpu.VMEM((ADAPTER_COUNT, ADAPTER_RANK, features), bf16),
            pltpu.VMEM((ADAPTER_COUNT, ADAPTER_RANK, columns), bf16),
            pltpu.VMEM((2, 4, chunks, LEN, CHUNK), bf16),
            pltpu.VMEM((2, 4, chunks, LEN, CHUNK), bf16),
            pltpu.VMEM((PASSES, LEN, columns), f32),
            pltpu.VMEM((2 * PASSES, LEN, 128), f32),
            pltpu.VMEM((PASSES, LEN, columns), bf16),
            pltpu.VMEM((GROUP, rows, wide), f32),
            pltpu.VMEM((GROUP, rows, wide), f32),
            pltpu.VMEM((LEN, wide), bf16),
            pltpu.VMEM((PASSES, LEN, wide), bf16),
            pltpu.VMEM((PASSES, wide, columns), bf16),
            pltpu.VMEM((GROUP, 2 * PASSES, LEN), f32),
            pltpu.VMEM((GROUP, rows, wide), f32),
            pltpu.VMEM((GROUP, rows, wide), f32),
            pltpu.VMEM((LEN, wide), bf16),
            pltpu.VMEM((GROUP, wide // GROUP, columns), bf16),
            pltpu.VMEM((GROUP, wide // GROUP, columns), bf16),
            pltpu.VMEM((GROUP, wide // GROUP, features), bf16),
            pltpu.VMEM((GROUP, wide // GROUP, features), bf16),
            sem((5,)),
            sem((RING,)),
            sem((RING,)),
            sem((RING,)),
            sem((RING,)),
            sem((RING,)),
            sem((RING,)),
            sem((chunks,)),
            sem((chunks,)),
            sem((RING, 3)),
            sem((RING, 3)),
            sem((RING, 4)),
            sem((RING, 4)),
            sem((2, 4, chunks)),
            sem((2, 4, chunks)),
            sem((4, GROUP)),
            sem((4, GROUP)),
        ]
        + [sem((GROUP,))] * 6,
        compiler_params=pltpu.CompilerParams(
            collective_id=0, has_side_effects=True, vmem_limit_bytes=56 * 2**20
        ),
    )(
        objective,
        output_norm_scale[None],
        attention,
        output_weight_frozen,
        residual,
        cotangent,
        adapter_down_weights,
        adapter_up_weights,
    )


def solution(mesh):
    placed = (
        P("dp", "tensor"),
        P("dp", "tensor"),
        P("dp", "tensor"),
        P(None, "dp", "tensor"),
        P("tensor"),
        P(),
        P(None, None, "tensor"),
        P(),
    )
    return jax.shard_map(
        body,
        mesh=mesh,
        in_specs=placed,
        out_specs=(P(None, "dp", "tensor"), P(None, "dp", "tensor")),
        check_vma=False,
    )
```

```python
import jax
import jax.numpy as jnp
from jax import lax
from jax.experimental import pallas as pl
from jax.experimental.pallas import tpu as pltpu
from jax.sharding import PartitionSpec as P

MODEL_WIDTH = 16384
ADAPTER_RANK = 64
ADAPTER_COUNT = 4
PASSES = 4
LEN = 256
EXAMPLES = 16
GROUP = 16
MESH = pl.DeviceIdType.MESH

epsilon = 1e-05


RING = 8
CHIPS = 8
NEAR = (4, 3, -3, 2, -2, 1, -1, 0)
CHUNK = 256
PIECE = 32


def spread(picked, step):
    per = ADAPTER_RANK // GROUP
    size = (ADAPTER_COUNT * ADAPTER_RANK, PASSES * ADAPTER_RANK)
    row = lax.broadcasted_iota(jnp.int32, size, 0)
    col = lax.broadcasted_iota(jnp.int32, size, 1)
    goal = picked * ADAPTER_RANK + col // (PASSES * per) * per + col % per
    chosen = (row == goal) & (col // per % PASSES == step)
    return jnp.where(chosen, 1.0, 0.0).astype(jnp.bfloat16)


def remote(src, dst, send, recv, device):
    return pltpu.make_async_remote_copy(
        src_ref=src,
        dst_ref=dst,
        send_sem=send,
        recv_sem=recv,
        device_id=device,
        device_id_type=MESH,
    )


def whole_kernel(
    objective,
    scale,
    attention,
    weight_hbm,
    residual_hbm,
    cotangent_hbm,
    down_hbm,
    up_hbm,
    out_a,
    out_b,
    middle,
    tokens,
    weight,
    residual,
    cotangent,
    down,
    up,
    ring_out,
    ring_in,
    hidden,
    sums,
    grads,
    low_terms,
    low_pair,
    low_slots,
    low_all,
    low_wide,
    up_wide,
    stat_own,
    stat_slots,
    back_terms,
    back_pair,
    back_slots,
    back_all,
    square_b,
    from_x_b,
    slots_b,
    square_a,
    from_x_a,
    slots_a,
    local,
    plane_send,
    plane_recv,
    z_send,
    z_recv,
    x_send,
    x_recv,
    weight_send,
    weight_recv,
    y_send,
    y_recv,
    core_send,
    core_recv,
    ring_send,
    ring_recv,
    low_sems,
    back_sems,
    stat_send,
    stat_recv,
    bx_sems,
    bz_sems,
    ax_sems,
    az_sems,
):
    me_d = lax.axis_index("dp")
    me_t = lax.axis_index("tensor")
    half = me_d // RING
    me_z = lax.rem(me_d, RING)
    core = lax.rem(me_t, 2)
    rows = LEN // GROUP
    wide = PASSES * ADAPTER_RANK
    columns = weight.shape[2]
    chunks = columns // CHUNK
    features = attention.shape[1]

    barrier = pltpu.get_barrier_semaphore()

    chip = me_t // 2
    other = me_t + 1 - 2 * core

    def same_core(step):
        return (me_d, lax.rem(chip + step, CHIPS) * 2 + core)

    def at_z(step):
        return (half * RING + lax.rem(me_z + step, RING), me_t)

    beside = (lax.rem(me_d + RING, GROUP), me_t)

    def greet(device):
        pl.semaphore_signal(barrier, inc=1, device_id=device, device_id_type=MESH)

    greet((me_d, other))
    greet(beside)
    for step in range(1, 4):
        greet((me_d, (chip // 4 * 4 + lax.rem(chip + step, 4)) * 2 + 1 - core))
    for step in range(1, CHIPS):
        greet(same_core(step))
    for step in range(1, RING):
        greet(at_z(step))

    def load(number):
        place = pl.ds(pl.multiple_of(me_t * features, features), features)
        pairs = (
            (down_hbm.at[:, :, place], down),
            (weight_hbm, weight.at[half]),
            (up_hbm, up),
            (residual_hbm, residual),
            (cotangent_hbm, cotangent),
        )
        return pltpu.make_async_copy(*pairs[number], local.at[number])

    for number in range(5):
        load(number).start()

    pl.semaphore_wait(barrier, 5 + CHIPS - 1 + RING - 1)

    def piece(t):
        number = lax.rem(t // 4, 2) * 4 + lax.rem(t, 2) * 2 + lax.rem(t // 2, 2)
        return pl.ds(pl.multiple_of(number * PIECE, PIECE), PIECE)

    def both(t):
        number = lax.rem(t // 4, 2) * 2 + lax.rem(t, 2)
        return pl.ds(pl.multiple_of(number * 2 * PIECE, 2 * PIECE), 2 * PIECE)

    side = me_t // RING

    def plane_copy(step, source):
        t = side * RING + lax.rem(me_t + step, RING)
        return remote(
            attention.at[piece(t), :],
            middle.at[source],
            plane_send.at[step],
            plane_recv.at[source],
            (me_d, t),
        )

    def weight_copy(chunk, slot):
        place = pl.ds(chunk * CHUNK, CHUNK)
        return remote(
            weight_hbm.at[:, place],
            weight.at[slot, :, place],
            weight_send.at[chunk],
            weight_recv.at[chunk],
            beside,
        )

    own_place = lax.rem(me_t, RING)
    for step in range(1, RING):
        plane_copy(step, own_place).start()
    middle[own_place] = attention[piece(me_t), :]

    weight_copy(0, half).start()

    def add_rows(terms, pair, slots, total, sems):
        def pair_copy(part):
            return remote(terms.at[part], pair, sems.at[0, 0], sems.at[1, 0], (me_d, other))

        def term_copy(step):
            return remote(
                terms.at[core, lax.rem(chip + step, CHIPS)],
                slots.at[step],
                sems.at[0, step],
                sems.at[1, step],
                same_core(step),
            )

        def full_copy(step, owner):
            part = total.at[core, owner]
            return remote(part, part, sems.at[2, step], sems.at[3, step], same_core(step))

        def last_copy(part):
            return remote(
                total.at[part], total.at[part], sems.at[2, 0], sems.at[3, 0], (me_d, other)
            )

        def begin():
            pair_copy(1 - core).start()

        def second():
            pair_copy(1 - core).wait()
            terms[core] = terms[core] + pair[...]
            for step in range(1, CHIPS):
                term_copy(step).start()

        def middle():
            for step in range(1, CHIPS):
                term_copy(step).wait()
            slots[0] = terms[core, chip]
            total[core, chip] = jnp.sum(slots[...], axis=0).astype(jnp.bfloat16)
            for step in range(1, CHIPS):
                full_copy(step, chip).start()

        def end():
            for step in range(1, CHIPS):
                full_copy(step, chip).wait_send()
            for step in range(1, CHIPS):
                full_copy(step, lax.rem(chip + CHIPS - step, CHIPS)).wait_recv()
            last_copy(core).start()
            last_copy(core).wait_send()
            last_copy(1 - core).wait_recv()

        return begin, second, middle, end

    low_begin, low_second, low_middle, low_end = add_rows(
        low_terms, low_pair, low_slots, low_all, low_sems
    )
    back_begin, back_second, back_middle, back_end = add_rows(
        back_terms, back_pair, back_slots, back_all, back_sems
    )

    def at_y(shift):
        return lax.rem(me_t + (shift % 4) * 4, GROUP)

    across = me_t + 2 - 4 * lax.rem(me_t // 2, 2)

    def z_of(number):
        return lax.rem(me_z + NEAR[number] + RING, RING)

    def z_copy(number, source):
        goal = z_of(number)
        return remote(
            middle.at[goal],
            tokens.at[source, side, piece(me_t), :],
            z_send.at[number],
            z_recv.at[source],
            (half * RING + goal, me_t),
        )

    def along_z(number):
        goal = z_of(number)
        pl.when(goal != own_place)(plane_copy(1, goal).wait_recv)
        if NEAR[number] == 0:
            tokens[me_z, side, piece(me_t), :] = middle[me_z]
        else:
            z_copy(number, me_z).start()

    def x_copy(number, owner):
        part = tokens.at[z_of(number), side, piece(owner), :]
        return remote(part, part, x_send.at[number], x_recv.at[number], (me_d, across))

    def y_copy(number, way, owner):
        part = tokens.at[z_of(number), owner // RING, both(owner), :]
        return remote(
            part,
            part,
            y_send.at[number, way],
            y_recv.at[number, way],
            (me_d, at_y((1, -1, 2)[way])),
        )

    def core_copy(number, shift, owner):
        part = tokens.at[z_of(number), owner // RING, both(owner), :]
        return remote(
            part, part, core_send.at[number, shift], core_recv.at[number, shift], (me_d, other)
        )

    def over_x(number):
        if NEAR[number] != 0:
            z_copy(number, z_of(number)).wait_recv()
        x_copy(number, me_t).start()

    def spread_own(number):
        x_copy(number, across).wait_recv()
        y_copy(number, 2, me_t).start()
        y_copy(number, 0, me_t).start()
        y_copy(number, 1, me_t).start()
        core_copy(number, 0, me_t).start()

    def pass_on(number):
        for way, shift in ((0, -1), (1, 1), (2, 2)):
            y_copy(number, way, at_y(shift)).wait_recv()
            core_copy(number, shift % 4, at_y(shift)).start()

    def arrived(number):
        for shift in range(4):
            owner = lax.rem(other + shift * 4, GROUP)
            core_copy(number, shift, owner).wait_recv()

    def product(number, cols):
        z = z_of(number)
        total = jnp.dot(tokens[z, 0], weight[0, :, cols], preferred_element_type=jnp.float32)
        return total + jnp.dot(
            tokens[z, 1], weight[1, :, cols], preferred_element_type=jnp.float32
        )

    def ring_copy(way, far, chunk):
        if far == 4:
            place = pl.ds(way * (LEN // 2), LEN // 2)
        else:
            place = pl.ds(0, LEN)
        z = lax.rem(me_z + (1, RING - 1)[way], RING)
        return remote(
            ring_out.at[way, far - 1, chunk, place, :],
            ring_in.at[way, far - 1, chunk, place, :],
            ring_send.at[way, far - 1, chunk],
            ring_recv.at[way, far - 1, chunk],
            (half * RING + z, me_t),
        )

    def cols_of(chunk):
        return pl.ds(chunk * CHUNK, CHUNK)

    def send_products(far, chunk):
        cols = cols_of(chunk)
        if far == 4:
            value = product(0, cols).astype(jnp.bfloat16)
            for way in range(2):
                mine = slice(way * (LEN // 2), (way + 1) * (LEN // 2))
                ring_out[way, 3, chunk, mine, :] = value[mine]
                ring_copy(way, 4, chunk).start()
            return
        for way in range(2):
            value = product(NEAR.index((far, -far)[way]), cols)
            ring_copy(way, far + 1, chunk).wait_recv()
            if far == 3:
                mine = slice(way * (LEN // 2), (way + 1) * (LEN // 2))
                rest = slice((1 - way) * (LEN // 2), (2 - way) * (LEN // 2))
                ring_out[way, 2, chunk, mine, :] = (
                    value[mine] + ring_in[way, 3, chunk, mine, :].astype(jnp.float32)
                ).astype(jnp.bfloat16)
                ring_out[way, 2, chunk, rest, :] = value[rest].astype(jnp.bfloat16)
            else:
                ring_out[way, far - 1, chunk] = (
                    value + ring_in[way, far, chunk].astype(jnp.float32)
                ).astype(jnp.bfloat16)
            ring_copy(way, far, chunk).start()

    def own_products(chunk):
        cols = cols_of(chunk)
        value = product(NEAR.index(0), cols)
        for way in range(2):
            ring_copy(way, 1, chunk).wait_recv()
            value = value + ring_in[way, 0, chunk].astype(jnp.float32)
        value = value + residual[:, cols].astype(jnp.float32)
        for step in range(PASSES):
            here = value + jnp.dot(
                low_wide[step], up_wide[step, :, cols], preferred_element_type=jnp.float32
            )
            hidden[step, :, cols] = here
            weighted = cotangent[step, :, cols].astype(jnp.float32) * scale[:, cols]
            squares = here * here
            inner = weighted * here
            sums[2 * step] += squares[:, :128] + squares[:, 128:]
            sums[2 * step + 1] += inner[:, :128] + inner[:, 128:]

    along_z(0)
    along_z(1)
    along_z(2)
    along_z(3)
    along_z(4)
    along_z(5)
    along_z(6)
    along_z(7)
    over_x(0)
    over_x(1)
    over_x(2)
    over_x(3)
    over_x(4)
    over_x(5)
    over_x(6)
    over_x(7)
    weight_copy(1, half).start()
    spread_own(0)
    spread_own(1)
    spread_own(2)
    spread_own(3)
    spread_own(4)
    spread_own(5)
    spread_own(6)
    spread_own(7)
    weight_copy(2, half).start()
    weight_copy(3, half).start()
    pass_on(0)
    load(1).wait()
    weight_copy(0, 1 - half).wait_recv()
    arrived(0)
    send_products(4, 0)
    weight_copy(1, 1 - half).wait_recv()
    send_products(4, 1)
    pass_on(1)
    pass_on(2)
    arrived(1)
    arrived(2)
    send_products(3, 0)
    send_products(3, 1)
    load(0).wait()
    low_terms[...] = lax.dot_general(
        attention[...],
        down[...].reshape(ADAPTER_COUNT * ADAPTER_RANK, features),
        (((1,), (1,)), ((), ())),
        preferred_element_type=jnp.float32,
    ).reshape(low_terms.shape)
    low_begin()
    pass_on(3)
    pass_on(4)
    low_second()
    arrived(3)
    arrived(4)
    send_products(2, 0)
    send_products(2, 1)
    weight_copy(2, 1 - half).wait_recv()
    weight_copy(3, 1 - half).wait_recv()
    send_products(4, 2)
    send_products(4, 3)
    pass_on(5)
    pass_on(6)
    arrived(5)
    arrived(6)
    send_products(1, 0)
    send_products(1, 1)
    low_middle()
    pass_on(7)
    send_products(3, 2)
    send_products(3, 3)
    low_end()
    for number in range(2, 5):
        load(number).wait()
    low_rows = low_all[...].reshape(LEN, wide)
    up_rows = up[...].reshape(ADAPTER_COUNT * ADAPTER_RANK, columns)
    for step in range(PASSES):
        choice = spread(objective[step], step)
        low_wide[step] = jnp.dot(
            low_rows, choice, preferred_element_type=jnp.float32
        ).astype(jnp.bfloat16)
        up_wide[step] = lax.dot_general(
            choice, up_rows, (((0,), (0,)), ((), ())), preferred_element_type=jnp.float32
        ).astype(jnp.bfloat16)
    sums[...] = jnp.zeros(sums.shape, jnp.float32)
    arrived(7)
    own_products(0)
    own_products(1)
    send_products(2, 2)
    send_products(2, 3)
    send_products(1, 2)
    send_products(1, 3)
    own_products(2)
    own_products(3)

    lane = lax.broadcasted_iota(jnp.int32, (LEN, 128), 1)
    stats = jnp.zeros((LEN, 128), jnp.float32)
    for kind in range(2 * PASSES):
        stats = jnp.where(lane == kind, jnp.sum(sums[kind], axis=1, keepdims=True), stats)
    stat_own[0] = stats.T[: 2 * PASSES]

    def stat_pair():
        return remote(
            stat_own.at[0], stat_own.at[1], stat_send.at[0], stat_recv.at[0], (me_d, other)
        )

    def stat_copy(step):
        return remote(
            stat_slots.at[0],
            stat_slots.at[step],
            stat_send.at[step],
            stat_recv.at[step],
            same_core(step),
        )

    stat_pair().start()
    stat_pair().wait()
    stat_slots[0] = stat_own[0] + stat_own[1]
    for step in range(1, CHIPS):
        stat_copy(step).start()
    for step in range(1, CHIPS):
        stat_copy(step).wait()
    totals = jnp.sum(stat_slots[...], axis=0)
    inner_first = jnp.concatenate([totals[1:], totals[:1]], axis=0)
    scale_inv = lax.rsqrt(totals / MODEL_WIDTH + epsilon)
    weight_hidden = inner_first * scale_inv**3 / MODEL_WIDTH
    keep = jnp.concatenate(
        [scale_inv, weight_hidden, jnp.zeros((128 - 4 * PASSES, LEN), jnp.float32)], axis=0
    )
    keep = jnp.where(lax.broadcasted_iota(jnp.int32, keep.shape, 0) % 2 == 0, keep, 0.0)
    by_token = keep.T

    terms = None
    for step in range(PASSES):
        weighted = cotangent[step].astype(jnp.float32) * scale[...]
        per_token = by_token[:, 2 * step : 2 * step + 1]
        back = by_token[:, 2 * PASSES + 2 * step : 2 * PASSES + 2 * step + 1]
        grads[step] = (per_token * weighted - hidden[step] * back).astype(jnp.bfloat16)
        term = lax.dot_general(
            grads[step], up_wide[step], (((1,), (1,)), ((), ())), preferred_element_type=jnp.float32
        )
        terms = term if terms is None else terms + term
    back_terms[...] = terms.reshape(back_terms.shape)
    back_begin()

    per_b = None
    for step in range(PASSES):
        term = lax.dot_general(
            low_wide[step], grads[step], (((0,), (0,)), ((), ())), preferred_element_type=jnp.float32
        )
        per_b = term if per_b is None else per_b + term
    square_b[...] = (per_b * per_b).astype(jnp.bfloat16).reshape(square_b.shape)

    def owners(squares, from_x, slots, x_sems, z_sems):
        def x_part(number):
            place = z_of(number)
            return remote(
                squares.at[1 - half, place],
                from_x.at[place],
                x_sems.at[0, number],
                x_sems.at[1, number],
                beside,
            )

        def z_part(number):
            return remote(
                squares.at[half, z_of(number)],
                slots.at[number],
                z_sems.at[0, number],
                z_sems.at[1, number],
                (half * RING + z_of(number), me_t),
            )

        def begin():
            for number in range(RING):
                x_part(number).start()

        def middle():
            for number in range(RING):
                x_part(number).wait_recv()
                place = z_of(number)
                total = squares[half, place].astype(jnp.float32) + from_x[place].astype(jnp.float32)
                if NEAR[number] == 0:
                    slots[number] = total.astype(jnp.bfloat16)
                else:
                    squares[half, place] = total.astype(jnp.bfloat16)
                    z_part(number).start()

        def end(out):
            for number in range(RING):
                if NEAR[number] != 0:
                    z_part(number).wait_recv()
            out[...] = jnp.sum(slots[...].astype(jnp.float32), axis=0)

        def drain():
            for number in range(RING):
                x_part(number).wait_send()
                if NEAR[number] != 0:
                    z_part(number).wait_send()

        return begin, middle, end, drain

    b_begin, b_middle, b_end, b_drain = owners(square_b, from_x_b, slots_b, bx_sems, bz_sems)
    a_begin, a_middle, a_end, a_drain = owners(square_a, from_x_a, slots_a, ax_sems, az_sems)
    b_begin()
    back_second()
    back_middle()
    b_middle()
    back_end()
    per_a = lax.dot_general(
        back_all[...].reshape(LEN, wide), attention[...], (((0,), (0,)), ((), ())), preferred_element_type=jnp.float32
    )
    square_a[...] = (per_a * per_a).astype(jnp.bfloat16).reshape(square_a.shape)
    a_begin()
    a_middle()
    b_end(out_b)

    for step in range(1, RING):
        plane_copy(step, own_place).wait_send()
    for number in range(RING - 1):
        z_copy(number, me_z).wait_send()
    for chunk in range(chunks):
        weight_copy(chunk, half).wait_send()
    for number in range(RING):
        x_copy(number, me_t).wait_send()
        for way in range(3):
            y_copy(number, way, me_t).wait_send()
        for shift in range(4):
            core_copy(number, shift, me_t).wait_send()

    def ring_done(chunk, carry):
        for way in range(2):
            for far in range(1, 5):
                ring_copy(way, far, chunk).wait_send()
        return carry

    lax.fori_loop(0, chunks, ring_done, 0)
    b_drain()
    a_end(out_a)
    a_drain()


def body(
    attention,
    output_weight_frozen,
    residual,
    cotangent,
    output_norm_scale,
    adapter_down_weights,
    adapter_up_weights,
    objective,
):
    features = attention.shape[1]
    depth, columns = output_weight_frozen.shape
    chunks = columns // CHUNK
    per = ADAPTER_RANK // GROUP
    wide = PASSES * ADAPTER_RANK
    rows = LEN // GROUP
    share = wide // GROUP
    bf16, f32 = jnp.bfloat16, jnp.float32
    vmem = pl.BlockSpec(memory_space=pltpu.VMEM)
    hbm = pl.BlockSpec(memory_space=pl.ANY)
    sem = pltpu.SemaphoreType.DMA
    squares = pl.pallas_call(
        whole_kernel,
        name="fisher",
        out_shape=(
            jax.ShapeDtypeStruct((share, features), f32),
            jax.ShapeDtypeStruct((share, columns), f32),
        ),
        in_specs=[pl.BlockSpec(memory_space=pltpu.SMEM), vmem, vmem] + [hbm] * 5,
        out_specs=(vmem, vmem),
        scratch_shapes=[
            pltpu.VMEM((RING, PIECE, features), bf16),
            pltpu.VMEM((RING, 2, LEN, features), bf16),
            pltpu.VMEM((2, depth, columns), bf16),
            pltpu.VMEM((LEN, columns), bf16),
            pltpu.VMEM((PASSES, LEN, columns), bf16),
            pltpu.VMEM((ADAPTER_COUNT, ADAPTER_RANK, features), bf16),
            pltpu.VMEM((ADAPTER_COUNT, ADAPTER_RANK, columns), bf16),
            pltpu.VMEM((2, 4, chunks, LEN, CHUNK), bf16),
            pltpu.VMEM((2, 4, chunks, LEN, CHUNK), bf16),
            pltpu.VMEM((PASSES, LEN, columns), f32),
            pltpu.VMEM((2 * PASSES, LEN, 128), f32),
            pltpu.VMEM((PASSES, LEN, columns), bf16),
            pltpu.VMEM((2, CHIPS, rows, wide), f32),
            pltpu.VMEM((CHIPS, rows, wide), f32),
            pltpu.VMEM((CHIPS, rows, wide), f32),
            pltpu.VMEM((2, CHIPS, rows, wide), bf16),
            pltpu.VMEM((PASSES, LEN, wide), bf16),
            pltpu.VMEM((PASSES, wide, columns), bf16),
            pltpu.VMEM((2, 2 * PASSES, LEN), f32),
            pltpu.VMEM((CHIPS, 2 * PASSES, LEN), f32),
            pltpu.VMEM((2, CHIPS, rows, wide), f32),
            pltpu.VMEM((CHIPS, rows, wide), f32),
            pltpu.VMEM((CHIPS, rows, wide), f32),
            pltpu.VMEM((2, CHIPS, rows, wide), bf16),
            pltpu.VMEM((2, RING, share, columns), bf16),
            pltpu.VMEM((RING, share, columns), bf16),
            pltpu.VMEM((RING, share, columns), bf16),
            pltpu.VMEM((2, RING, share, features), bf16),
            pltpu.VMEM((RING, share, features), bf16),
            pltpu.VMEM((RING, share, features), bf16),
            sem((5,)),
            sem((RING,)),
            sem((RING,)),
            sem((RING,)),
            sem((RING,)),
            sem((RING,)),
            sem((RING,)),
            sem((chunks,)),
            sem((chunks,)),
            sem((RING, 3)),
            sem((RING, 3)),
            sem((RING, 4)),
            sem((RING, 4)),
            sem((2, 4, chunks)),
            sem((2, 4, chunks)),
            sem((4, CHIPS)),
            sem((4, CHIPS)),
            sem((CHIPS,)),
            sem((CHIPS,)),
        ]
        + [sem((2, RING))] * 4,
        compiler_params=pltpu.CompilerParams(
            collective_id=0, has_side_effects=True, vmem_limit_bytes=56 * 2**20
        ),
    )(
        objective,
        output_norm_scale[None],
        attention,
        output_weight_frozen,
        residual,
        cotangent,
        adapter_down_weights,
        adapter_up_weights,
    )
    chosen = objective[:, None] == jnp.arange(ADAPTER_COUNT, dtype=jnp.int32)[None, :]
    weights = jnp.where(chosen, 1.0 / EXAMPLES, 0.0)[:, :, None, None]
    return tuple(
        jnp.sum(weights * total.reshape(PASSES, 1, per, total.shape[1]), axis=0)
        for total in squares
    )


def solution(mesh):
    placed = (
        P("dp", "tensor"),
        P("dp", "tensor"),
        P("dp", "tensor"),
        P(None, "dp", "tensor"),
        P("tensor"),
        P(),
        P(None, None, "tensor"),
        P(),
    )
    return jax.shard_map(
        body,
        mesh=mesh,
        in_specs=placed,
        out_specs=(P(None, "dp", "tensor"), P(None, "dp", "tensor")),
        check_vma=False,
    )
```

```python
import jax
import jax.numpy as jnp
from jax import lax
from jax.experimental import pallas as pl
from jax.experimental.pallas import tpu as pltpu
from jax.sharding import PartitionSpec as P

MODEL_WIDTH = 16384
ADAPTER_RANK = 64
ADAPTER_COUNT = 4
PASSES = 4
LEN = 256
EXAMPLES = 16
GROUP = 16
MESH = pl.DeviceIdType.MESH

epsilon = 1e-05


def each_other(action):
    def one(step, carry):
        action(step)
        return carry

    lax.fori_loop(1, GROUP, one, 0)


RING = 8
CHIPS = 8
NEAR = (4, 3, -3, 2, -2, 1, -1, 0)
CHUNK = 256
PIECE = 32


def spread(picked, step):
    per = ADAPTER_RANK // GROUP
    size = (ADAPTER_COUNT * ADAPTER_RANK, PASSES * ADAPTER_RANK)
    row = lax.broadcasted_iota(jnp.int32, size, 0)
    col = lax.broadcasted_iota(jnp.int32, size, 1)
    goal = picked * ADAPTER_RANK + col // (PASSES * per) * per + col % per
    chosen = (row == goal) & (col // per % PASSES == step)
    return jnp.where(chosen, 1.0, 0.0).astype(jnp.bfloat16)


def remote(src, dst, send, recv, device):
    return pltpu.make_async_remote_copy(
        src_ref=src,
        dst_ref=dst,
        send_sem=send,
        recv_sem=recv,
        device_id=device,
        device_id_type=MESH,
    )


def whole_kernel(
    objective,
    scale,
    attention,
    weight_hbm,
    residual_hbm,
    cotangent_hbm,
    down_hbm,
    up_hbm,
    out_a,
    out_b,
    middle,
    tokens,
    weight,
    residual,
    cotangent,
    down,
    up,
    ring_out,
    ring_in,
    hidden,
    sums,
    grads,
    low_terms,
    low_slots,
    low_all,
    low_wide,
    up_wide,
    stat_own,
    stat_slots,
    back_terms,
    back_slots,
    back_all,
    square_b,
    from_x_b,
    slots_b,
    square_a,
    from_x_a,
    slots_a,
    local,
    plane_send,
    plane_recv,
    z_send,
    z_recv,
    x_send,
    x_recv,
    weight_send,
    weight_recv,
    y_send,
    y_recv,
    core_send,
    core_recv,
    ring_send,
    ring_recv,
    low_sems,
    back_sems,
    stat_send,
    stat_recv,
    bx_sems,
    bz_sems,
    ax_sems,
    az_sems,
):
    me_d = lax.axis_index("dp")
    me_t = lax.axis_index("tensor")
    half = me_d // RING
    me_z = lax.rem(me_d, RING)
    core = lax.rem(me_t, 2)
    rows = LEN // GROUP
    wide = PASSES * ADAPTER_RANK
    columns = weight.shape[2]
    chunks = columns // CHUNK
    features = attention.shape[1]

    barrier = pltpu.get_barrier_semaphore()

    chip = me_t // 2
    other = me_t + 1 - 2 * core

    def same_core(step):
        return (me_d, lax.rem(chip + step, CHIPS) * 2 + core)

    def at_z(step):
        return (half * RING + lax.rem(me_z + step, RING), me_t)

    beside = (lax.rem(me_d + RING, GROUP), me_t)

    def greet(device):
        pl.semaphore_signal(barrier, inc=1, device_id=device, device_id_type=MESH)

    greet(beside)
    for step in range(1, GROUP):
        greet((me_d, lax.rem(me_t + step, GROUP)))
    for step in range(1, RING):
        greet(at_z(step))

    def load(number):
        place = pl.ds(pl.multiple_of(me_t * features, features), features)
        pairs = (
            (down_hbm.at[:, :, place], down),
            (weight_hbm, weight.at[half]),
            (up_hbm, up),
            (residual_hbm, residual),
            (cotangent_hbm, cotangent),
        )
        return pltpu.make_async_copy(*pairs[number], local.at[number])

    for number in range(5):
        load(number).start()

    pl.semaphore_wait(barrier, 1 + GROUP - 1 + RING - 1)

    def piece(t):
        number = lax.rem(t // 4, 2) * 4 + lax.rem(t, 2) * 2 + lax.rem(t // 2, 2)
        return pl.ds(pl.multiple_of(number * PIECE, PIECE), PIECE)

    def both(t):
        number = lax.rem(t // 4, 2) * 2 + lax.rem(t, 2)
        return pl.ds(pl.multiple_of(number * 2 * PIECE, 2 * PIECE), 2 * PIECE)

    side = me_t // RING

    def plane_copy(step, source):
        t = side * RING + lax.rem(me_t + step, RING)
        return remote(
            attention.at[piece(t), :],
            middle.at[source],
            plane_send.at[step],
            plane_recv.at[source],
            (me_d, t),
        )

    def weight_copy(chunk, slot):
        place = pl.ds(chunk * CHUNK, CHUNK)
        return remote(
            weight_hbm.at[:, place],
            weight.at[slot, :, place],
            weight_send.at[chunk],
            weight_recv.at[chunk],
            beside,
        )

    own_place = lax.rem(me_t, RING)
    for step in range(1, RING):
        plane_copy(step, own_place).start()
    middle[own_place] = attention[piece(me_t), :]

    weight_copy(0, half).start()

    def in_plane(step):
        return (me_d, lax.rem(me_t + step, GROUP))

    def add_rows(terms, slots, total, sems):
        def term_copy(step):
            return remote(
                terms.at[lax.rem(me_t + step, GROUP)],
                slots.at[step],
                sems.at[0, step],
                sems.at[1, step],
                in_plane(step),
            )

        def full_copy(step, owner):
            place = pl.ds(pl.multiple_of(owner * rows, rows), rows)
            return remote(
                total.at[place, :],
                total.at[place, :],
                sems.at[2, step],
                sems.at[3, step],
                in_plane(step),
            )

        def begin():
            each_other(lambda step: term_copy(step).start())

        def middle():
            each_other(lambda step: term_copy(step).wait())
            slots[0] = terms[me_t]
            mine = pl.ds(pl.multiple_of(me_t * rows, rows), rows)
            total[mine, :] = jnp.sum(slots[...], axis=0).astype(jnp.bfloat16)
            each_other(lambda step: full_copy(step, me_t).start())

        def end():
            each_other(lambda step: full_copy(step, me_t).wait_send())
            each_other(
                lambda step: full_copy(step, lax.rem(me_t + GROUP - step, GROUP)).wait_recv()
            )

        return begin, middle, end

    low_begin, low_middle, low_end = add_rows(low_terms, low_slots, low_all, low_sems)
    back_begin, back_middle, back_end = add_rows(back_terms, back_slots, back_all, back_sems)

    def at_y(shift):
        return lax.rem(me_t + (shift % 4) * 4, GROUP)

    across = me_t + 2 - 4 * lax.rem(me_t // 2, 2)

    def z_of(number):
        return lax.rem(me_z + NEAR[number] + RING, RING)

    def z_copy(number, source):
        goal = z_of(number)
        return remote(
            middle.at[goal],
            tokens.at[source, side, piece(me_t), :],
            z_send.at[number],
            z_recv.at[source],
            (half * RING + goal, me_t),
        )

    def along_z(number):
        goal = z_of(number)
        pl.when(goal != own_place)(plane_copy(1, goal).wait_recv)
        if NEAR[number] == 0:
            tokens[me_z, side, piece(me_t), :] = middle[me_z]
        else:
            z_copy(number, me_z).start()

    def x_copy(number, owner):
        part = tokens.at[z_of(number), side, piece(owner), :]
        return remote(part, part, x_send.at[number], x_recv.at[number], (me_d, across))

    def y_copy(number, way, owner):
        part = tokens.at[z_of(number), owner // RING, both(owner), :]
        return remote(
            part,
            part,
            y_send.at[number, way],
            y_recv.at[number, way],
            (me_d, at_y((1, -1, 2)[way])),
        )

    def core_copy(number, shift, owner):
        part = tokens.at[z_of(number), owner // RING, both(owner), :]
        return remote(
            part, part, core_send.at[number, shift], core_recv.at[number, shift], (me_d, other)
        )

    def over_x(number):
        if NEAR[number] != 0:
            z_copy(number, z_of(number)).wait_recv()
        x_copy(number, me_t).start()

    def spread_own(number):
        x_copy(number, across).wait_recv()
        y_copy(number, 2, me_t).start()
        y_copy(number, 0, me_t).start()
        y_copy(number, 1, me_t).start()
        core_copy(number, 0, me_t).start()

    def pass_on(number):
        for way, shift in ((0, -1), (1, 1), (2, 2)):
            y_copy(number, way, at_y(shift)).wait_recv()
            core_copy(number, shift % 4, at_y(shift)).start()

    def arrived(number):
        for shift in range(4):
            owner = lax.rem(other + shift * 4, GROUP)
            core_copy(number, shift, owner).wait_recv()

    def product(number, cols):
        z = z_of(number)
        total = jnp.dot(tokens[z, 0], weight[0, :, cols], preferred_element_type=jnp.float32)
        return total + jnp.dot(
            tokens[z, 1], weight[1, :, cols], preferred_element_type=jnp.float32
        )

    def ring_copy(way, far, chunk):
        if far == 4:
            place = pl.ds(way * (LEN // 2), LEN // 2)
        else:
            place = pl.ds(0, LEN)
        z = lax.rem(me_z + (1, RING - 1)[way], RING)
        return remote(
            ring_out.at[way, far - 1, chunk, place, :],
            ring_in.at[way, far - 1, chunk, place, :],
            ring_send.at[way, far - 1, chunk],
            ring_recv.at[way, far - 1, chunk],
            (half * RING + z, me_t),
        )

    def cols_of(chunk):
        return pl.ds(chunk * CHUNK, CHUNK)

    def send_products(far, chunk):
        cols = cols_of(chunk)
        if far == 4:
            value = product(0, cols).astype(jnp.bfloat16)
            for way in range(2):
                mine = slice(way * (LEN // 2), (way + 1) * (LEN // 2))
                ring_out[way, 3, chunk, mine, :] = value[mine]
                ring_copy(way, 4, chunk).start()
            return
        for way in range(2):
            value = product(NEAR.index((far, -far)[way]), cols)
            ring_copy(way, far + 1, chunk).wait_recv()
            if far == 3:
                mine = slice(way * (LEN // 2), (way + 1) * (LEN // 2))
                rest = slice((1 - way) * (LEN // 2), (2 - way) * (LEN // 2))
                ring_out[way, 2, chunk, mine, :] = (
                    value[mine] + ring_in[way, 3, chunk, mine, :].astype(jnp.float32)
                ).astype(jnp.bfloat16)
                ring_out[way, 2, chunk, rest, :] = value[rest].astype(jnp.bfloat16)
            else:
                ring_out[way, far - 1, chunk] = (
                    value + ring_in[way, far, chunk].astype(jnp.float32)
                ).astype(jnp.bfloat16)
            ring_copy(way, far, chunk).start()

    def own_products(chunk):
        cols = cols_of(chunk)
        value = product(NEAR.index(0), cols)
        for way in range(2):
            ring_copy(way, 1, chunk).wait_recv()
            value = value + ring_in[way, 0, chunk].astype(jnp.float32)
        value = value + residual[:, cols].astype(jnp.float32)
        for step in range(PASSES):
            here = value + jnp.dot(
                low_wide[step], up_wide[step, :, cols], preferred_element_type=jnp.float32
            )
            hidden[step, :, cols] = here
            weighted = cotangent[step, :, cols].astype(jnp.float32) * scale[:, cols]
            squares = here * here
            inner = weighted * here
            sums[2 * step] += squares[:, :128] + squares[:, 128:]
            sums[2 * step + 1] += inner[:, :128] + inner[:, 128:]

    along_z(0)
    along_z(1)
    along_z(2)
    along_z(3)
    along_z(4)
    along_z(5)
    along_z(6)
    along_z(7)
    over_x(0)
    over_x(1)
    over_x(2)
    over_x(3)
    over_x(4)
    over_x(5)
    over_x(6)
    over_x(7)
    weight_copy(1, half).start()
    spread_own(0)
    spread_own(1)
    spread_own(2)
    spread_own(3)
    spread_own(4)
    spread_own(5)
    spread_own(6)
    spread_own(7)
    weight_copy(2, half).start()
    weight_copy(3, half).start()
    pass_on(0)
    load(1).wait()
    weight_copy(0, 1 - half).wait_recv()
    arrived(0)
    send_products(4, 0)
    weight_copy(1, 1 - half).wait_recv()
    send_products(4, 1)
    pass_on(1)
    pass_on(2)
    arrived(1)
    arrived(2)
    send_products(3, 0)
    send_products(3, 1)
    load(0).wait()
    low_terms[...] = lax.dot_general(
        attention[...],
        down[...].reshape(ADAPTER_COUNT * ADAPTER_RANK, features),
        (((1,), (1,)), ((), ())),
        preferred_element_type=jnp.float32,
    ).reshape(low_terms.shape)
    low_begin()
    pass_on(3)
    pass_on(4)
    arrived(3)
    arrived(4)
    send_products(2, 0)
    send_products(2, 1)
    weight_copy(2, 1 - half).wait_recv()
    weight_copy(3, 1 - half).wait_recv()
    send_products(4, 2)
    send_products(4, 3)
    pass_on(5)
    pass_on(6)
    arrived(5)
    arrived(6)
    send_products(1, 0)
    send_products(1, 1)
    low_middle()
    pass_on(7)
    send_products(3, 2)
    send_products(3, 3)
    low_end()
    for number in range(2, 5):
        load(number).wait()
    up_rows = up[...].reshape(ADAPTER_COUNT * ADAPTER_RANK, columns)
    for step in range(PASSES):
        choice = spread(objective[step], step)
        low_wide[step] = jnp.dot(
            low_all[...], choice, preferred_element_type=jnp.float32
        ).astype(jnp.bfloat16)
        up_wide[step] = lax.dot_general(
            choice, up_rows, (((0,), (0,)), ((), ())), preferred_element_type=jnp.float32
        ).astype(jnp.bfloat16)
    sums[...] = jnp.zeros(sums.shape, jnp.float32)
    arrived(7)
    own_products(0)
    own_products(1)
    send_products(2, 2)
    send_products(2, 3)
    send_products(1, 2)
    send_products(1, 3)
    own_products(2)
    own_products(3)

    lane = lax.broadcasted_iota(jnp.int32, (LEN, 128), 1)
    stats = jnp.zeros((LEN, 128), jnp.float32)
    for kind in range(2 * PASSES):
        stats = jnp.where(lane == kind, jnp.sum(sums[kind], axis=1, keepdims=True), stats)
    stat_own[0] = stats.T[: 2 * PASSES]

    def stat_pair():
        return remote(
            stat_own.at[0], stat_own.at[1], stat_send.at[0], stat_recv.at[0], (me_d, other)
        )

    def stat_copy(step):
        return remote(
            stat_slots.at[0],
            stat_slots.at[step],
            stat_send.at[step],
            stat_recv.at[step],
            same_core(step),
        )

    stat_pair().start()
    stat_pair().wait()
    stat_slots[0] = stat_own[0] + stat_own[1]
    for step in range(1, CHIPS):
        stat_copy(step).start()
    for step in range(1, CHIPS):
        stat_copy(step).wait()
    totals = jnp.sum(stat_slots[...], axis=0)
    inner_first = jnp.concatenate([totals[1:], totals[:1]], axis=0)
    scale_inv = lax.rsqrt(totals / MODEL_WIDTH + epsilon)
    weight_hidden = inner_first * scale_inv**3 / MODEL_WIDTH
    keep = jnp.concatenate(
        [scale_inv, weight_hidden, jnp.zeros((128 - 4 * PASSES, LEN), jnp.float32)], axis=0
    )
    keep = jnp.where(lax.broadcasted_iota(jnp.int32, keep.shape, 0) % 2 == 0, keep, 0.0)
    by_token = keep.T

    terms = None
    for step in range(PASSES):
        weighted = cotangent[step].astype(jnp.float32) * scale[...]
        per_token = by_token[:, 2 * step : 2 * step + 1]
        back = by_token[:, 2 * PASSES + 2 * step : 2 * PASSES + 2 * step + 1]
        grads[step] = (per_token * weighted - hidden[step] * back).astype(jnp.bfloat16)
        term = lax.dot_general(
            grads[step], up_wide[step], (((1,), (1,)), ((), ())), preferred_element_type=jnp.float32
        )
        terms = term if terms is None else terms + term
    back_terms[...] = terms.reshape(back_terms.shape)
    back_begin()

    per_b = None
    for step in range(PASSES):
        term = lax.dot_general(
            low_wide[step], grads[step], (((0,), (0,)), ((), ())), preferred_element_type=jnp.float32
        )
        per_b = term if per_b is None else per_b + term
    square_b[...] = (per_b * per_b).astype(jnp.bfloat16).reshape(square_b.shape)

    def owners(squares, from_x, slots, x_sems, z_sems):
        def x_part(number):
            place = z_of(number)
            return remote(
                squares.at[1 - half, place],
                from_x.at[place],
                x_sems.at[0, number],
                x_sems.at[1, number],
                beside,
            )

        def z_part(number):
            return remote(
                squares.at[half, z_of(number)],
                slots.at[number],
                z_sems.at[0, number],
                z_sems.at[1, number],
                (half * RING + z_of(number), me_t),
            )

        def begin():
            for number in range(RING):
                x_part(number).start()

        def middle():
            for number in range(RING):
                x_part(number).wait_recv()
                place = z_of(number)
                total = squares[half, place].astype(jnp.float32) + from_x[place].astype(jnp.float32)
                if NEAR[number] == 0:
                    slots[number] = total.astype(jnp.bfloat16)
                else:
                    squares[half, place] = total.astype(jnp.bfloat16)
                    z_part(number).start()

        def end(out):
            for number in range(RING):
                if NEAR[number] != 0:
                    z_part(number).wait_recv()
            out[...] = jnp.sum(slots[...].astype(jnp.float32), axis=0)

        def drain():
            for number in range(RING):
                x_part(number).wait_send()
                if NEAR[number] != 0:
                    z_part(number).wait_send()

        return begin, middle, end, drain

    b_begin, b_middle, b_end, b_drain = owners(square_b, from_x_b, slots_b, bx_sems, bz_sems)
    a_begin, a_middle, a_end, a_drain = owners(square_a, from_x_a, slots_a, ax_sems, az_sems)
    b_begin()
    back_middle()
    b_middle()
    back_end()
    per_a = lax.dot_general(
        back_all[...], attention[...], (((0,), (0,)), ((), ())), preferred_element_type=jnp.float32
    )
    square_a[...] = (per_a * per_a).astype(jnp.bfloat16).reshape(square_a.shape)
    a_begin()
    a_middle()
    b_end(out_b)

    for step in range(1, RING):
        plane_copy(step, own_place).wait_send()
    for number in range(RING - 1):
        z_copy(number, me_z).wait_send()
    for chunk in range(chunks):
        weight_copy(chunk, half).wait_send()
    for number in range(RING):
        x_copy(number, me_t).wait_send()
        for way in range(3):
            y_copy(number, way, me_t).wait_send()
        for shift in range(4):
            core_copy(number, shift, me_t).wait_send()

    def ring_done(chunk, carry):
        for way in range(2):
            for far in range(1, 5):
                ring_copy(way, far, chunk).wait_send()
        return carry

    lax.fori_loop(0, chunks, ring_done, 0)
    b_drain()
    a_end(out_a)
    a_drain()


def choose(objective, total, out):
    per = ADAPTER_RANK // GROUP
    for adapter in range(ADAPTER_COUNT):
        chosen = None
        for step in range(PASSES):
            share = jnp.where(objective[step] == adapter, 1.0 / EXAMPLES, 0.0)
            part = share * total[step * per : (step + 1) * per]
            chosen = part if chosen is None else chosen + part
        out[adapter] = chosen


def choose_kernel(objective, total_a, total_b, out_a, out_b):
    choose(objective, total_a[...], out_a)
    choose(objective, total_b[...], out_b)


def body(
    attention,
    output_weight_frozen,
    residual,
    cotangent,
    output_norm_scale,
    adapter_down_weights,
    adapter_up_weights,
    objective,
):
    features = attention.shape[1]
    depth, columns = output_weight_frozen.shape
    chunks = columns // CHUNK
    per = ADAPTER_RANK // GROUP
    wide = PASSES * ADAPTER_RANK
    rows = LEN // GROUP
    share = wide // GROUP
    bf16, f32 = jnp.bfloat16, jnp.float32
    vmem = pl.BlockSpec(memory_space=pltpu.VMEM)
    hbm = pl.BlockSpec(memory_space=pl.ANY)
    sem = pltpu.SemaphoreType.DMA
    squares = pl.pallas_call(
        whole_kernel,
        name="fisher",
        out_shape=(
            jax.ShapeDtypeStruct((share, features), f32),
            jax.ShapeDtypeStruct((share, columns), f32),
        ),
        in_specs=[pl.BlockSpec(memory_space=pltpu.SMEM), vmem, vmem] + [hbm] * 5,
        out_specs=(vmem, vmem),
        scratch_shapes=[
            pltpu.VMEM((RING, PIECE, features), bf16),
            pltpu.VMEM((RING, 2, LEN, features), bf16),
            pltpu.VMEM((2, depth, columns), bf16),
            pltpu.VMEM((LEN, columns), bf16),
            pltpu.VMEM((PASSES, LEN, columns), bf16),
            pltpu.VMEM((ADAPTER_COUNT, ADAPTER_RANK, features), bf16),
            pltpu.VMEM((ADAPTER_COUNT, ADAPTER_RANK, columns), bf16),
            pltpu.VMEM((2, 4, chunks, LEN, CHUNK), bf16),
            pltpu.VMEM((2, 4, chunks, LEN, CHUNK), bf16),
            pltpu.VMEM((PASSES, LEN, columns), f32),
            pltpu.VMEM((2 * PASSES, LEN, 128), f32),
            pltpu.VMEM((PASSES, LEN, columns), bf16),
            pltpu.VMEM((GROUP, rows, wide), f32),
            pltpu.VMEM((GROUP, rows, wide), f32),
            pltpu.VMEM((LEN, wide), bf16),
            pltpu.VMEM((PASSES, LEN, wide), bf16),
            pltpu.VMEM((PASSES, wide, columns), bf16),
            pltpu.VMEM((2, 2 * PASSES, LEN), f32),
            pltpu.VMEM((CHIPS, 2 * PASSES, LEN), f32),
            pltpu.VMEM((GROUP, rows, wide), f32),
            pltpu.VMEM((GROUP, rows, wide), f32),
            pltpu.VMEM((LEN, wide), bf16),
            pltpu.VMEM((2, RING, share, columns), bf16),
            pltpu.VMEM((RING, share, columns), bf16),
            pltpu.VMEM((RING, share, columns), bf16),
            pltpu.VMEM((2, RING, share, features), bf16),
            pltpu.VMEM((RING, share, features), bf16),
            pltpu.VMEM((RING, share, features), bf16),
            sem((5,)),
            sem((RING,)),
            sem((RING,)),
            sem((RING,)),
            sem((RING,)),
            sem((RING,)),
            sem((RING,)),
            sem((chunks,)),
            sem((chunks,)),
            sem((RING, 3)),
            sem((RING, 3)),
            sem((RING, 4)),
            sem((RING, 4)),
            sem((2, 4, chunks)),
            sem((2, 4, chunks)),
            sem((4, GROUP)),
            sem((4, GROUP)),
            sem((CHIPS,)),
            sem((CHIPS,)),
        ]
        + [sem((2, RING))] * 4,
        compiler_params=pltpu.CompilerParams(
            collective_id=0, has_side_effects=True, vmem_limit_bytes=56 * 2**20
        ),
    )(
        objective,
        output_norm_scale[None],
        attention,
        output_weight_frozen,
        residual,
        cotangent,
        adapter_down_weights,
        adapter_up_weights,
    )
    return pl.pallas_call(
        choose_kernel,
        name="choose",
        out_shape=(
            jax.ShapeDtypeStruct((ADAPTER_COUNT, per, features), f32),
            jax.ShapeDtypeStruct((ADAPTER_COUNT, per, columns), f32),
        ),
        in_specs=[pl.BlockSpec(memory_space=pltpu.SMEM), vmem, vmem],
        out_specs=(vmem, vmem),
    )(objective, *squares)


def solution(mesh):
    placed = (
        P("dp", "tensor"),
        P("dp", "tensor"),
        P("dp", "tensor"),
        P(None, "dp", "tensor"),
        P("tensor"),
        P(),
        P(None, None, "tensor"),
        P(),
    )
    return jax.shard_map(
        body,
        mesh=mesh,
        in_specs=placed,
        out_specs=(P(None, "dp", "tensor"), P(None, "dp", "tensor")),
        check_vma=False,
    )
```

```python
import jax
import jax.numpy as jnp
from jax import lax
from jax.experimental import pallas as pl
from jax.experimental.pallas import tpu as pltpu
from jax.sharding import PartitionSpec as P

MODEL_WIDTH = 16384
ADAPTER_RANK = 64
ADAPTER_COUNT = 4
PASSES = 4
LEN = 256
EXAMPLES = 16
GROUP = 16
MESH = pl.DeviceIdType.MESH

epsilon = 1e-05


def each_other(action):
    def one(step, carry):
        action(step)
        return carry

    lax.fori_loop(1, GROUP, one, 0)


RING = 8
CHIPS = 8
NEAR = (4, 3, -3, 2, -2, 1, -1, 0)
CHUNK = 256
PIECE = 32


def spread(picked, step):
    per = ADAPTER_RANK // GROUP
    size = (ADAPTER_COUNT * ADAPTER_RANK, PASSES * ADAPTER_RANK)
    row = lax.broadcasted_iota(jnp.int32, size, 0)
    col = lax.broadcasted_iota(jnp.int32, size, 1)
    goal = picked * ADAPTER_RANK + col // (PASSES * per) * per + col % per
    chosen = (row == goal) & (col // per % PASSES == step)
    return jnp.where(chosen, 1.0, 0.0).astype(jnp.bfloat16)


def remote(src, dst, send, recv, device):
    return pltpu.make_async_remote_copy(
        src_ref=src,
        dst_ref=dst,
        send_sem=send,
        recv_sem=recv,
        device_id=device,
        device_id_type=MESH,
    )


def whole_kernel(
    objective,
    scale,
    attention_hbm,
    weight_hbm,
    residual_hbm,
    cotangent_hbm,
    down_hbm,
    up_hbm,
    out_a,
    out_b,
    attention,
    middle,
    tokens,
    weight,
    residual,
    cotangent,
    down,
    up,
    ring_out,
    ring_in,
    hidden,
    sums,
    grads,
    low_terms,
    low_slots,
    low_all,
    low_wide,
    up_wide,
    stat_own,
    stat_slots,
    back_terms,
    back_slots,
    back_all,
    square_b,
    from_x_b,
    slots_b,
    square_a,
    slots_a,
    local,
    plane_send,
    plane_recv,
    z_send,
    z_recv,
    x_send,
    x_recv,
    weight_send,
    weight_recv,
    y_send,
    y_recv,
    core_send,
    core_recv,
    ring_send,
    ring_recv,
    low_sems,
    back_sems,
    stat_send,
    stat_recv,
    bx_sems,
    bz_sems,
    a_sems,
):
    me_d = lax.axis_index("dp")
    me_t = lax.axis_index("tensor")
    half = me_d // RING
    me_z = lax.rem(me_d, RING)
    core = lax.rem(me_t, 2)
    rows = LEN // GROUP
    wide = PASSES * ADAPTER_RANK
    columns = weight.shape[2]
    chunks = columns // CHUNK
    features = attention.shape[1]

    barrier = pltpu.get_barrier_semaphore()

    chip = me_t // 2
    other = me_t + 1 - 2 * core

    def same_core(step):
        return (me_d, lax.rem(chip + step, CHIPS) * 2 + core)

    def at_z(step):
        return (half * RING + lax.rem(me_z + step, RING), me_t)

    beside = (lax.rem(me_d + RING, GROUP), me_t)

    def greet(device):
        pl.semaphore_signal(barrier, inc=1, device_id=device, device_id_type=MESH)

    block = me_t // RING
    own_place = lax.rem(me_t, RING)
    for step in NEAR[:-1]:
        greet(at_z(step + RING))
    for step in (0, 4):
        greet((me_d, (1 - block) * RING + lax.rem(own_place + step, RING)))
    for step in range(1, RING):
        greet((me_d, block * RING + lax.rem(own_place + step, RING)))
    greet(beside)

    def load(number):
        place = pl.ds(pl.multiple_of(me_t * features, features), features)
        pairs = (
            (down_hbm.at[:, :, place], down),
            (weight_hbm, weight.at[half]),
            (up_hbm, up),
            (residual_hbm, residual),
            (cotangent_hbm, cotangent),
            (attention_hbm, attention),
        )
        return pltpu.make_async_copy(*pairs[number], local.at[number])

    for number in (5, 0, 1, 2, 3, 4):
        load(number).start()

    pl.semaphore_wait(barrier, 2 * RING + 1)

    def piece(t):
        number = lax.rem(t // 4, 2) * 4 + lax.rem(t, 2) * 2 + lax.rem(t // 2, 2)
        return pl.ds(pl.multiple_of(number * PIECE, PIECE), PIECE)

    def both(t):
        number = lax.rem(t // 4, 2) * 2 + lax.rem(t, 2)
        return pl.ds(pl.multiple_of(number * 2 * PIECE, 2 * PIECE), 2 * PIECE)

    side = me_t // RING

    def plane_copy(step, source):
        t = side * RING + lax.rem(me_t + step, RING)
        return remote(
            attention_hbm.at[piece(t), :],
            middle.at[source],
            plane_send.at[step],
            plane_recv.at[source],
            (me_d, t),
        )

    def weight_copy(chunk, slot):
        place = pl.ds(chunk * CHUNK, CHUNK)
        return remote(
            weight_hbm.at[:, place],
            weight.at[slot, :, place],
            weight_send.at[chunk],
            weight_recv.at[chunk],
            beside,
        )

    for step in range(1, RING):
        plane_copy(step, own_place).start()
    load(5).wait()
    middle[own_place] = attention[piece(me_t), :]

    weight_copy(0, half).start()

    def in_plane(step):
        return (me_d, lax.rem(me_t + step, GROUP))

    def add_rows(terms, slots, total, sems):
        def term_copy(step):
            return remote(
                terms.at[lax.rem(me_t + step, GROUP)],
                slots.at[step],
                sems.at[0, step],
                sems.at[1, step],
                in_plane(step),
            )

        def full_copy(step, owner):
            place = pl.ds(pl.multiple_of(owner * rows, rows), rows)
            return remote(
                total.at[place, :],
                total.at[place, :],
                sems.at[2, step],
                sems.at[3, step],
                in_plane(step),
            )

        def begin():
            each_other(lambda step: term_copy(step).start())

        def middle():
            each_other(lambda step: term_copy(step).wait())
            slots[0] = terms[me_t]
            mine = pl.ds(pl.multiple_of(me_t * rows, rows), rows)
            total[mine, :] = jnp.sum(slots[...], axis=0).astype(jnp.bfloat16)
            each_other(lambda step: full_copy(step, me_t).start())

        def end():
            each_other(lambda step: full_copy(step, me_t).wait_send())
            each_other(
                lambda step: full_copy(step, lax.rem(me_t + GROUP - step, GROUP)).wait_recv()
            )

        return begin, middle, end

    low_begin, low_middle, low_end = add_rows(low_terms, low_slots, low_all, low_sems)
    back_begin, back_middle, back_end = add_rows(back_terms, back_slots, back_all, back_sems)

    def at_y(shift):
        return lax.rem(me_t + (shift % 4) * 4, GROUP)

    across = me_t + 2 - 4 * lax.rem(me_t // 2, 2)

    def z_of(number):
        return lax.rem(me_z + NEAR[number] + RING, RING)

    def z_copy(number, source):
        goal = z_of(number)
        return remote(
            middle.at[goal],
            tokens.at[source, side, piece(me_t), :],
            z_send.at[number],
            z_recv.at[source],
            (half * RING + goal, me_t),
        )

    def along_z(number):
        goal = z_of(number)
        pl.when(goal != own_place)(plane_copy(1, goal).wait_recv)
        if NEAR[number] == 0:
            tokens[me_z, side, piece(me_t), :] = middle[me_z]
        else:
            z_copy(number, me_z).start()

    def x_copy(number, owner):
        part = tokens.at[z_of(number), side, piece(owner), :]
        return remote(part, part, x_send.at[number], x_recv.at[number], (me_d, across))

    def y_copy(number, way, owner):
        part = tokens.at[z_of(number), owner // RING, both(owner), :]
        return remote(
            part,
            part,
            y_send.at[number, way],
            y_recv.at[number, way],
            (me_d, at_y((1, -1, 2)[way])),
        )

    def core_copy(number, shift, owner):
        part = tokens.at[z_of(number), owner // RING, both(owner), :]
        return remote(
            part, part, core_send.at[number, shift], core_recv.at[number, shift], (me_d, other)
        )

    def over_x(number):
        if NEAR[number] != 0:
            z_copy(number, z_of(number)).wait_recv()
        x_copy(number, me_t).start()

    def spread_own(number):
        x_copy(number, across).wait_recv()
        y_copy(number, 2, me_t).start()
        y_copy(number, 0, me_t).start()
        y_copy(number, 1, me_t).start()
        core_copy(number, 0, me_t).start()

    def pass_on(number):
        for way, shift in ((0, -1), (1, 1), (2, 2)):
            y_copy(number, way, at_y(shift)).wait_recv()
            core_copy(number, shift % 4, at_y(shift)).start()

    def arrived(number):
        for shift in range(4):
            owner = lax.rem(other + shift * 4, GROUP)
            core_copy(number, shift, owner).wait_recv()

    def product(number, cols):
        z = z_of(number)
        total = jnp.dot(tokens[z, 0], weight[0, :, cols], preferred_element_type=jnp.float32)
        return total + jnp.dot(
            tokens[z, 1], weight[1, :, cols], preferred_element_type=jnp.float32
        )

    def ring_copy(way, far, chunk):
        if far == 4:
            place = pl.ds(way * (LEN // 2), LEN // 2)
        else:
            place = pl.ds(0, LEN)
        z = lax.rem(me_z + (1, RING - 1)[way], RING)
        return remote(
            ring_out.at[way, far - 1, chunk, place, :],
            ring_in.at[way, far - 1, chunk, place, :],
            ring_send.at[way, far - 1, chunk],
            ring_recv.at[way, far - 1, chunk],
            (half * RING + z, me_t),
        )

    def cols_of(chunk):
        return pl.ds(chunk * CHUNK, CHUNK)

    def send_products(far, chunk):
        cols = cols_of(chunk)
        if far == 4:
            value = product(0, cols).astype(jnp.bfloat16)
            for way in range(2):
                mine = slice(way * (LEN // 2), (way + 1) * (LEN // 2))
                ring_out[way, 3, chunk, mine, :] = value[mine]
                ring_copy(way, 4, chunk).start()
            return
        for way in range(2):
            value = product(NEAR.index((far, -far)[way]), cols)
            ring_copy(way, far + 1, chunk).wait_recv()
            if far == 3:
                mine = slice(way * (LEN // 2), (way + 1) * (LEN // 2))
                rest = slice((1 - way) * (LEN // 2), (2 - way) * (LEN // 2))
                ring_out[way, 2, chunk, mine, :] = (
                    value[mine] + ring_in[way, 3, chunk, mine, :].astype(jnp.float32)
                ).astype(jnp.bfloat16)
                ring_out[way, 2, chunk, rest, :] = value[rest].astype(jnp.bfloat16)
            else:
                ring_out[way, far - 1, chunk] = (
                    value + ring_in[way, far, chunk].astype(jnp.float32)
                ).astype(jnp.bfloat16)
            ring_copy(way, far, chunk).start()

    def own_products(chunk):
        cols = cols_of(chunk)
        value = product(NEAR.index(0), cols)
        for way in range(2):
            ring_copy(way, 1, chunk).wait_recv()
            value = value + ring_in[way, 0, chunk].astype(jnp.float32)
        value = value + residual[:, cols].astype(jnp.float32)
        for step in range(PASSES):
            here = value + jnp.dot(
                low_wide[step], up_wide[step, :, cols], preferred_element_type=jnp.float32
            )
            hidden[step, :, cols] = here
            weighted = cotangent[step, :, cols].astype(jnp.float32) * scale[:, cols]
            squares = here * here
            inner = weighted * here
            sums[2 * step] += squares[:, :128] + squares[:, 128:]
            sums[2 * step + 1] += inner[:, :128] + inner[:, 128:]

    along_z(0)
    along_z(1)
    along_z(2)
    along_z(3)
    along_z(4)
    along_z(5)
    along_z(6)
    along_z(7)
    over_x(0)
    over_x(1)
    over_x(2)
    over_x(3)
    over_x(4)
    over_x(5)
    over_x(6)
    over_x(7)
    weight_copy(1, half).start()
    spread_own(0)
    spread_own(1)
    spread_own(2)
    spread_own(3)
    spread_own(4)
    spread_own(5)
    spread_own(6)
    spread_own(7)
    weight_copy(2, half).start()
    weight_copy(3, half).start()
    pass_on(0)
    load(1).wait()
    weight_copy(0, 1 - half).wait_recv()
    arrived(0)
    send_products(4, 0)
    weight_copy(1, 1 - half).wait_recv()
    send_products(4, 1)
    pass_on(1)
    pass_on(2)
    arrived(1)
    arrived(2)
    send_products(3, 0)
    send_products(3, 1)
    load(0).wait()
    low_terms[...] = lax.dot_general(
        attention[...],
        down[...].reshape(ADAPTER_COUNT * ADAPTER_RANK, features),
        (((1,), (1,)), ((), ())),
        preferred_element_type=jnp.float32,
    ).reshape(low_terms.shape)
    low_begin()
    pass_on(3)
    pass_on(4)
    arrived(3)
    arrived(4)
    send_products(2, 0)
    send_products(2, 1)
    for number in range(2, 5):
        load(number).wait()
    up_rows = up[...].reshape(ADAPTER_COUNT * ADAPTER_RANK, columns)
    for step in range(PASSES):
        up_wide[step] = lax.dot_general(
            spread(objective[step], step),
            up_rows,
            (((0,), (0,)), ((), ())),
            preferred_element_type=jnp.float32,
        ).astype(jnp.bfloat16)
    sums[...] = jnp.zeros(sums.shape, jnp.float32)
    weight_copy(2, 1 - half).wait_recv()
    weight_copy(3, 1 - half).wait_recv()
    send_products(4, 2)
    send_products(4, 3)
    pass_on(5)
    pass_on(6)
    arrived(5)
    arrived(6)
    send_products(1, 0)
    send_products(1, 1)
    low_middle()
    pass_on(7)
    send_products(3, 2)
    send_products(3, 3)
    send_products(2, 2)
    send_products(2, 3)
    low_end()
    for step in range(PASSES):
        low_wide[step] = jnp.dot(
            low_all[...], spread(objective[step], step), preferred_element_type=jnp.float32
        ).astype(jnp.bfloat16)
    arrived(7)
    own_products(0)
    own_products(1)
    send_products(1, 2)
    send_products(1, 3)
    own_products(2)
    own_products(3)

    lane = lax.broadcasted_iota(jnp.int32, (LEN, 128), 1)
    stats = jnp.zeros((LEN, 128), jnp.float32)
    for kind in range(2 * PASSES):
        stats = jnp.where(lane == kind, jnp.sum(sums[kind], axis=1, keepdims=True), stats)
    stat_own[0] = stats.T[: 2 * PASSES]

    def stat_pair():
        return remote(
            stat_own.at[0], stat_own.at[1], stat_send.at[0], stat_recv.at[0], (me_d, other)
        )

    def stat_copy(step):
        return remote(
            stat_slots.at[0],
            stat_slots.at[step],
            stat_send.at[step],
            stat_recv.at[step],
            same_core(step),
        )

    stat_pair().start()
    stat_pair().wait()
    stat_slots[0] = stat_own[0] + stat_own[1]
    for step in range(1, CHIPS):
        stat_copy(step).start()
    for step in range(1, CHIPS):
        stat_copy(step).wait()
    totals = jnp.sum(stat_slots[...], axis=0)
    inner_first = jnp.concatenate([totals[1:], totals[:1]], axis=0)
    scale_inv = lax.rsqrt(totals / MODEL_WIDTH + epsilon)
    weight_hidden = inner_first * scale_inv**3 / MODEL_WIDTH
    keep = jnp.concatenate(
        [scale_inv, weight_hidden, jnp.zeros((128 - 4 * PASSES, LEN), jnp.float32)], axis=0
    )
    keep = jnp.where(lax.broadcasted_iota(jnp.int32, keep.shape, 0) % 2 == 0, keep, 0.0)
    by_token = keep.T

    terms = None
    for step in range(PASSES):
        weighted = cotangent[step].astype(jnp.float32) * scale[...]
        per_token = by_token[:, 2 * step : 2 * step + 1]
        back = by_token[:, 2 * PASSES + 2 * step : 2 * PASSES + 2 * step + 1]
        grads[step] = (per_token * weighted - hidden[step] * back).astype(jnp.bfloat16)
        term = lax.dot_general(
            grads[step], up_wide[step], (((1,), (1,)), ((), ())), preferred_element_type=jnp.float32
        )
        terms = term if terms is None else terms + term
    back_terms[...] = terms.reshape(back_terms.shape)
    back_begin()

    per_b = None
    for step in range(PASSES):
        term = lax.dot_general(
            low_wide[step], grads[step], (((0,), (0,)), ((), ())), preferred_element_type=jnp.float32
        )
        per_b = term if per_b is None else per_b + term
    square_b[...] = (per_b * per_b).astype(jnp.bfloat16).reshape(square_b.shape)

    def owners(squares, from_x, slots, x_sems, z_sems):
        def x_part(number):
            place = z_of(number)
            return remote(
                squares.at[1 - half, place],
                from_x.at[place],
                x_sems.at[0, number],
                x_sems.at[1, number],
                beside,
            )

        def z_part(number):
            return remote(
                squares.at[half, z_of(number)],
                slots.at[number],
                z_sems.at[0, number],
                z_sems.at[1, number],
                (half * RING + z_of(number), me_t),
            )

        def begin():
            for number in range(RING):
                x_part(number).start()

        def middle():
            for number in range(RING):
                x_part(number).wait_recv()
                place = z_of(number)
                total = squares[half, place].astype(jnp.float32) + from_x[place].astype(jnp.float32)
                if NEAR[number] == 0:
                    slots[number] = total.astype(jnp.bfloat16)
                else:
                    squares[half, place] = total.astype(jnp.bfloat16)
                    z_part(number).start()

        def end(out):
            for number in range(RING):
                if NEAR[number] != 0:
                    z_part(number).wait_recv()
            out[...] = jnp.sum(slots[...].astype(jnp.float32), axis=0)

        def drain():
            for number in range(RING):
                x_part(number).wait_send()
                if NEAR[number] != 0:
                    z_part(number).wait_send()

        return begin, middle, end, drain

    b_begin, b_middle, b_end, b_drain = owners(square_b, from_x_b, slots_b, bx_sems, bz_sems)

    def a_copy(step):
        return remote(
            square_a.at[lax.rem(me_d + step, GROUP)],
            slots_a.at[step],
            a_sems.at[0, step],
            a_sems.at[1, step],
            (lax.rem(me_d + step, GROUP), me_t),
        )

    b_begin()
    back_middle()
    b_middle()
    back_end()
    per_a = lax.dot_general(
        back_all[...], attention[...], (((0,), (0,)), ((), ())), preferred_element_type=jnp.float32
    )
    square_a[...] = (per_a * per_a).astype(jnp.bfloat16).reshape(square_a.shape)
    each_other(lambda step: a_copy(step).start())
    b_end(out_b)

    for step in range(1, RING):
        plane_copy(step, own_place).wait_send()
    for number in range(RING - 1):
        z_copy(number, me_z).wait_send()
    for chunk in range(chunks):
        weight_copy(chunk, half).wait_send()
    for number in range(RING):
        x_copy(number, me_t).wait_send()
        for way in range(3):
            y_copy(number, way, me_t).wait_send()
        for shift in range(4):
            core_copy(number, shift, me_t).wait_send()

    def ring_done(chunk, carry):
        for way in range(2):
            for far in range(1, 5):
                ring_copy(way, far, chunk).wait_send()
        return carry

    lax.fori_loop(0, chunks, ring_done, 0)
    b_drain()
    each_other(lambda step: a_copy(step).wait())
    slots_a[0] = square_a[me_d]
    out_a[...] = jnp.sum(slots_a[...].astype(jnp.float32), axis=0)


def choose(objective, total, out):
    per = ADAPTER_RANK // GROUP
    for adapter in range(ADAPTER_COUNT):
        chosen = None
        for step in range(PASSES):
            share = jnp.where(objective[step] == adapter, 1.0 / EXAMPLES, 0.0)
            part = share * total[step * per : (step + 1) * per]
            chosen = part if chosen is None else chosen + part
        out[adapter] = chosen


def choose_kernel(objective, total_a, total_b, out_a, out_b):
    choose(objective, total_a[...], out_a)
    choose(objective, total_b[...], out_b)


def body(
    attention,
    output_weight_frozen,
    residual,
    cotangent,
    output_norm_scale,
    adapter_down_weights,
    adapter_up_weights,
    objective,
):
    features = attention.shape[1]
    depth, columns = output_weight_frozen.shape
    chunks = columns // CHUNK
    per = ADAPTER_RANK // GROUP
    wide = PASSES * ADAPTER_RANK
    rows = LEN // GROUP
    share = wide // GROUP
    bf16, f32 = jnp.bfloat16, jnp.float32
    vmem = pl.BlockSpec(memory_space=pltpu.VMEM)
    hbm = pl.BlockSpec(memory_space=pl.ANY)
    sem = pltpu.SemaphoreType.DMA
    squares = pl.pallas_call(
        whole_kernel,
        name="fisher",
        out_shape=(
            jax.ShapeDtypeStruct((share, features), f32),
            jax.ShapeDtypeStruct((share, columns), f32),
        ),
        in_specs=[pl.BlockSpec(memory_space=pltpu.SMEM), vmem] + [hbm] * 6,
        out_specs=(vmem, vmem),
        scratch_shapes=[
            pltpu.VMEM((LEN, features), bf16),
            pltpu.VMEM((RING, PIECE, features), bf16),
            pltpu.VMEM((RING, 2, LEN, features), bf16),
            pltpu.VMEM((2, depth, columns), bf16),
            pltpu.VMEM((LEN, columns), bf16),
            pltpu.VMEM((PASSES, LEN, columns), bf16),
            pltpu.VMEM((ADAPTER_COUNT, ADAPTER_RANK, features), bf16),
            pltpu.VMEM((ADAPTER_COUNT, ADAPTER_RANK, columns), bf16),
            pltpu.VMEM((2, 4, chunks, LEN, CHUNK), bf16),
            pltpu.VMEM((2, 4, chunks, LEN, CHUNK), bf16),
            pltpu.VMEM((PASSES, LEN, columns), f32),
            pltpu.VMEM((2 * PASSES, LEN, 128), f32),
            pltpu.VMEM((PASSES, LEN, columns), bf16),
            pltpu.VMEM((GROUP, rows, wide), f32),
            pltpu.VMEM((GROUP, rows, wide), f32),
            pltpu.VMEM((LEN, wide), bf16),
            pltpu.VMEM((PASSES, LEN, wide), bf16),
            pltpu.VMEM((PASSES, wide, columns), bf16),
            pltpu.VMEM((2, 2 * PASSES, LEN), f32),
            pltpu.VMEM((CHIPS, 2 * PASSES, LEN), f32),
            pltpu.VMEM((GROUP, rows, wide), f32),
            pltpu.VMEM((GROUP, rows, wide), f32),
            pltpu.VMEM((LEN, wide), bf16),
            pltpu.VMEM((2, RING, share, columns), bf16),
            pltpu.VMEM((RING, share, columns), bf16),
            pltpu.VMEM((RING, share, columns), bf16),
            pltpu.VMEM((GROUP, share, features), bf16),
            pltpu.VMEM((GROUP, share, features), bf16),
            sem((6,)),
            sem((RING,)),
            sem((RING,)),
            sem((RING,)),
            sem((RING,)),
            sem((RING,)),
            sem((RING,)),
            sem((chunks,)),
            sem((chunks,)),
            sem((RING, 3)),
            sem((RING, 3)),
            sem((RING, 4)),
            sem((RING, 4)),
            sem((2, 4, chunks)),
            sem((2, 4, chunks)),
            sem((4, GROUP)),
            sem((4, GROUP)),
            sem((CHIPS,)),
            sem((CHIPS,)),
        ]
        + [sem((2, RING))] * 2
        + [sem((2, GROUP))],
        compiler_params=pltpu.CompilerParams(
            collective_id=0, has_side_effects=True, vmem_limit_bytes=56 * 2**20
        ),
    )(
        objective,
        output_norm_scale[None],
        attention,
        output_weight_frozen,
        residual,
        cotangent,
        adapter_down_weights,
        adapter_up_weights,
    )
    return pl.pallas_call(
        choose_kernel,
        name="choose",
        out_shape=(
            jax.ShapeDtypeStruct((ADAPTER_COUNT, per, features), f32),
            jax.ShapeDtypeStruct((ADAPTER_COUNT, per, columns), f32),
        ),
        in_specs=[pl.BlockSpec(memory_space=pltpu.SMEM), vmem, vmem],
        out_specs=(vmem, vmem),
    )(objective, *squares)


def solution(mesh):
    placed = (
        P("dp", "tensor"),
        P("dp", "tensor"),
        P("dp", "tensor"),
        P(None, "dp", "tensor"),
        P("tensor"),
        P(),
        P(None, None, "tensor"),
        P(),
    )
    return jax.shard_map(
        body,
        mesh=mesh,
        in_specs=placed,
        out_specs=(P(None, "dp", "tensor"), P(None, "dp", "tensor")),
        check_vma=False,
    )
```

```python
import jax
import jax.numpy as jnp
from jax import lax
from jax.experimental import pallas as pl
from jax.experimental.pallas import tpu as pltpu
from jax.sharding import PartitionSpec as P

MODEL_WIDTH = 16384
ADAPTER_RANK = 64
ADAPTER_COUNT = 4
PASSES = 4
LEN = 256
EXAMPLES = 16
GROUP = 16
MESH = pl.DeviceIdType.MESH

epsilon = 1e-05


def each_other(action):
    def one(step, carry):
        action(step)
        return carry

    lax.fori_loop(1, GROUP, one, 0)


RING = 8
CHIPS = 8
NEAR = (4, 3, -3, 2, -2, 1, -1, 0)
CHUNK = 256
PIECE = 32


def spread(picked, step):
    per = ADAPTER_RANK // GROUP
    size = (ADAPTER_COUNT * ADAPTER_RANK, PASSES * ADAPTER_RANK)
    row = lax.broadcasted_iota(jnp.int32, size, 0)
    col = lax.broadcasted_iota(jnp.int32, size, 1)
    goal = picked * ADAPTER_RANK + col // (PASSES * per) * per + col % per
    chosen = (row == goal) & (col // per % PASSES == step)
    return jnp.where(chosen, 1.0, 0.0).astype(jnp.bfloat16)


def remote(src, dst, send, recv, device):
    return pltpu.make_async_remote_copy(
        src_ref=src,
        dst_ref=dst,
        send_sem=send,
        recv_sem=recv,
        device_id=device,
        device_id_type=MESH,
    )


def whole_kernel(
    objective,
    scale,
    attention_hbm,
    weight_hbm,
    residual_hbm,
    cotangent_hbm,
    down_hbm,
    up_hbm,
    out_a,
    out_b,
    attention,
    middle,
    tokens,
    weight,
    residual,
    cotangent,
    down,
    up,
    ring_out,
    ring_in,
    hidden,
    sums,
    grads,
    low_terms,
    low_slots,
    low_all,
    low_wide,
    up_wide,
    stat_own,
    stat_slots,
    back_terms,
    back_slots,
    back_all,
    square_b,
    from_x_b,
    slots_b,
    square_a,
    slots_a,
    local,
    plane_send,
    plane_recv,
    z_send,
    z_recv,
    x_send,
    x_recv,
    weight_send,
    weight_recv,
    y_send,
    y_recv,
    core_send,
    core_recv,
    ring_send,
    ring_recv,
    low_sems,
    back_sems,
    stat_send,
    stat_recv,
    bx_sems,
    bz_sems,
    a_sems,
):
    me_d = lax.axis_index("dp")
    me_t = lax.axis_index("tensor")
    half = me_d // RING
    me_z = lax.rem(me_d, RING)
    core = lax.rem(me_t, 2)
    rows = LEN // GROUP
    wide = PASSES * ADAPTER_RANK
    columns = weight.shape[2]
    chunks = columns // CHUNK
    features = attention.shape[1]

    barrier = pltpu.get_barrier_semaphore()

    chip = me_t // 2
    other = me_t + 1 - 2 * core

    def same_core(step):
        return (me_d, lax.rem(chip + step, CHIPS) * 2 + core)

    def at_z(step):
        return (half * RING + lax.rem(me_z + step, RING), me_t)

    beside = (lax.rem(me_d + RING, GROUP), me_t)

    def greet(device):
        pl.semaphore_signal(barrier, inc=1, device_id=device, device_id_type=MESH)

    block = me_t // RING
    own_place = lax.rem(me_t, RING)
    for step in NEAR[:-1]:
        greet(at_z(step + RING))
    for step in (0, 4):
        greet((me_d, (1 - block) * RING + lax.rem(own_place + step, RING)))
    for step in range(1, RING):
        greet((me_d, block * RING + lax.rem(own_place + step, RING)))
    greet(beside)

    def load(number):
        place = pl.ds(pl.multiple_of(me_t * features, features), features)
        pairs = (
            (down_hbm.at[:, :, place], down),
            (weight_hbm, weight.at[half]),
            (up_hbm, up),
            (residual_hbm, residual),
            (cotangent_hbm, cotangent),
            (attention_hbm, attention),
        )
        return pltpu.make_async_copy(*pairs[number], local.at[number])

    for number in (5, 0, 1, 2, 3, 4):
        load(number).start()

    pl.semaphore_wait(barrier, 2 * RING + 1)

    def piece(t):
        number = lax.rem(t // 4, 2) * 4 + lax.rem(t, 2) * 2 + lax.rem(t // 2, 2)
        return pl.ds(pl.multiple_of(number * PIECE, PIECE), PIECE)

    def both(t):
        number = lax.rem(t // 4, 2) * 2 + lax.rem(t, 2)
        return pl.ds(pl.multiple_of(number * 2 * PIECE, 2 * PIECE), 2 * PIECE)

    side = me_t // RING

    def plane_copy(step, source):
        t = side * RING + lax.rem(me_t + step, RING)
        return remote(
            attention_hbm.at[piece(t), :],
            middle.at[source],
            plane_send.at[step],
            plane_recv.at[source],
            (me_d, t),
        )

    def weight_copy(chunk, slot):
        place = pl.ds(chunk * CHUNK, CHUNK)
        return remote(
            weight_hbm.at[:, place],
            weight.at[slot, :, place],
            weight_send.at[chunk],
            weight_recv.at[chunk],
            beside,
        )

    for step in range(1, RING):
        plane_copy(step, own_place).start()
    load(5).wait()
    middle[own_place] = attention[piece(me_t), :]

    weight_copy(0, half).start()

    def in_plane(step):
        return (me_d, lax.rem(me_t + step, GROUP))

    def add_rows(terms, slots, total, sems):
        def term_copy(step):
            return remote(
                terms.at[lax.rem(me_t + step, GROUP)],
                slots.at[step],
                sems.at[0, step],
                sems.at[1, step],
                in_plane(step),
            )

        def full_copy(step, owner):
            place = pl.ds(pl.multiple_of(owner * rows, rows), rows)
            return remote(
                total.at[place, :],
                total.at[place, :],
                sems.at[2, step],
                sems.at[3, step],
                in_plane(step),
            )

        def begin():
            each_other(lambda step: term_copy(step).start())

        def middle():
            each_other(lambda step: term_copy(step).wait())
            slots[0] = terms[me_t]
            mine = pl.ds(pl.multiple_of(me_t * rows, rows), rows)
            total[mine, :] = jnp.sum(slots[...], axis=0).astype(jnp.bfloat16)
            each_other(lambda step: full_copy(step, me_t).start())

        def end():
            each_other(lambda step: full_copy(step, me_t).wait_send())
            each_other(
                lambda step: full_copy(step, lax.rem(me_t + GROUP - step, GROUP)).wait_recv()
            )

        return begin, middle, end

    low_begin, low_middle, low_end = add_rows(low_terms, low_slots, low_all, low_sems)
    back_begin, back_middle, back_end = add_rows(back_terms, back_slots, back_all, back_sems)

    def at_y(shift):
        return lax.rem(me_t + (shift % 4) * 4, GROUP)

    across = me_t + 2 - 4 * lax.rem(me_t // 2, 2)

    def z_of(number):
        return lax.rem(me_z + NEAR[number] + RING, RING)

    def z_copy(number, source):
        goal = z_of(number)
        return remote(
            middle.at[goal],
            tokens.at[source, side, piece(me_t), :],
            z_send.at[number],
            z_recv.at[source],
            (half * RING + goal, me_t),
        )

    def along_z(number):
        goal = z_of(number)
        pl.when(goal != own_place)(plane_copy(1, goal).wait_recv)
        if NEAR[number] == 0:
            tokens[me_z, side, piece(me_t), :] = middle[me_z]
        else:
            z_copy(number, me_z).start()

    def x_copy(number, owner):
        part = tokens.at[z_of(number), side, piece(owner), :]
        return remote(part, part, x_send.at[number], x_recv.at[number], (me_d, across))

    def y_copy(number, way, owner):
        part = tokens.at[z_of(number), owner // RING, both(owner), :]
        return remote(
            part,
            part,
            y_send.at[number, way],
            y_recv.at[number, way],
            (me_d, at_y((1, -1, 2)[way])),
        )

    def core_copy(number, shift, owner):
        part = tokens.at[z_of(number), owner // RING, both(owner), :]
        return remote(
            part, part, core_send.at[number, shift], core_recv.at[number, shift], (me_d, other)
        )

    def over_x(number):
        if NEAR[number] != 0:
            z_copy(number, z_of(number)).wait_recv()
        x_copy(number, me_t).start()

    def spread_own(number):
        x_copy(number, across).wait_recv()
        y_copy(number, 2, me_t).start()
        y_copy(number, 0, me_t).start()
        y_copy(number, 1, me_t).start()
        core_copy(number, 0, me_t).start()

    def pass_on(number):
        for way, shift in ((0, -1), (1, 1), (2, 2)):
            y_copy(number, way, at_y(shift)).wait_recv()
            core_copy(number, shift % 4, at_y(shift)).start()

    def arrived(number):
        for shift in range(4):
            owner = lax.rem(other + shift * 4, GROUP)
            core_copy(number, shift, owner).wait_recv()

    def product(number, cols):
        z = z_of(number)
        total = jnp.dot(tokens[z, 0], weight[0, :, cols], preferred_element_type=jnp.float32)
        return total + jnp.dot(
            tokens[z, 1], weight[1, :, cols], preferred_element_type=jnp.float32
        )

    def ring_copy(way, far, chunk):
        if far == 4:
            place = pl.ds(way * (LEN // 2), LEN // 2)
        else:
            place = pl.ds(0, LEN)
        z = lax.rem(me_z + (1, RING - 1)[way], RING)
        return remote(
            ring_out.at[way, far - 1, chunk, place, :],
            ring_in.at[way, far - 1, chunk, place, :],
            ring_send.at[way, far - 1, chunk],
            ring_recv.at[way, far - 1, chunk],
            (half * RING + z, me_t),
        )

    def cols_of(chunk):
        return pl.ds(chunk * CHUNK, CHUNK)

    def send_products(far, chunk):
        cols = cols_of(chunk)
        if far == 4:
            value = product(0, cols).astype(jnp.bfloat16)
            for way in range(2):
                mine = slice(way * (LEN // 2), (way + 1) * (LEN // 2))
                ring_out[way, 3, chunk, mine, :] = value[mine]
                ring_copy(way, 4, chunk).start()
            return
        for way in range(2):
            value = product(NEAR.index((far, -far)[way]), cols)
            ring_copy(way, far + 1, chunk).wait_recv()
            if far == 3:
                mine = slice(way * (LEN // 2), (way + 1) * (LEN // 2))
                rest = slice((1 - way) * (LEN // 2), (2 - way) * (LEN // 2))
                ring_out[way, 2, chunk, mine, :] = (
                    value[mine] + ring_in[way, 3, chunk, mine, :].astype(jnp.float32)
                ).astype(jnp.bfloat16)
                ring_out[way, 2, chunk, rest, :] = value[rest].astype(jnp.bfloat16)
            else:
                ring_out[way, far - 1, chunk] = (
                    value + ring_in[way, far, chunk].astype(jnp.float32)
                ).astype(jnp.bfloat16)
            ring_copy(way, far, chunk).start()

    def own_products(chunk):
        cols = cols_of(chunk)
        value = product(NEAR.index(0), cols) + residual[:, cols].astype(jnp.float32)
        for step in range(PASSES):
            hidden[step, :, cols] = value + jnp.dot(
                low_wide[step], up_wide[step, :, cols], preferred_element_type=jnp.float32
            )
        for way in range(2):
            ring_copy(way, 1, chunk).wait_recv()
        arrived_sum = ring_in[0, 0, chunk].astype(jnp.float32) + ring_in[1, 0, chunk].astype(
            jnp.float32
        )
        for step in range(PASSES):
            here = hidden[step, :, cols] + arrived_sum
            hidden[step, :, cols] = here
            weighted = cotangent[step, :, cols].astype(jnp.float32) * scale[:, cols]
            squares = here * here
            inner = weighted * here
            sums[2 * step] += squares[:, :128] + squares[:, 128:]
            sums[2 * step + 1] += inner[:, :128] + inner[:, 128:]

    along_z(0)
    along_z(1)
    along_z(2)
    along_z(3)
    along_z(4)
    along_z(5)
    along_z(6)
    along_z(7)
    over_x(0)
    over_x(1)
    over_x(2)
    over_x(3)
    over_x(4)
    over_x(5)
    over_x(6)
    over_x(7)
    weight_copy(1, half).start()
    spread_own(0)
    spread_own(1)
    spread_own(2)
    spread_own(3)
    spread_own(4)
    spread_own(5)
    spread_own(6)
    spread_own(7)
    weight_copy(2, half).start()
    weight_copy(3, half).start()
    pass_on(0)
    load(1).wait()
    weight_copy(0, 1 - half).wait_recv()
    arrived(0)
    send_products(4, 0)
    weight_copy(1, 1 - half).wait_recv()
    send_products(4, 1)
    pass_on(1)
    pass_on(2)
    arrived(1)
    arrived(2)
    send_products(3, 0)
    send_products(3, 1)
    load(0).wait()
    low_terms[...] = lax.dot_general(
        attention[...],
        down[...].reshape(ADAPTER_COUNT * ADAPTER_RANK, features),
        (((1,), (1,)), ((), ())),
        preferred_element_type=jnp.float32,
    ).reshape(low_terms.shape)
    low_begin()
    pass_on(3)
    pass_on(4)
    arrived(3)
    arrived(4)
    send_products(2, 0)
    send_products(2, 1)
    for number in range(2, 5):
        load(number).wait()
    up_rows = up[...].reshape(ADAPTER_COUNT * ADAPTER_RANK, columns)
    for step in range(PASSES):
        up_wide[step] = lax.dot_general(
            spread(objective[step], step),
            up_rows,
            (((0,), (0,)), ((), ())),
            preferred_element_type=jnp.float32,
        ).astype(jnp.bfloat16)
    sums[...] = jnp.zeros(sums.shape, jnp.float32)
    weight_copy(2, 1 - half).wait_recv()
    weight_copy(3, 1 - half).wait_recv()
    send_products(4, 2)
    send_products(4, 3)
    pass_on(5)
    pass_on(6)
    arrived(5)
    arrived(6)
    send_products(1, 0)
    send_products(1, 1)
    low_middle()
    pass_on(7)
    send_products(3, 2)
    send_products(3, 3)
    send_products(2, 2)
    send_products(2, 3)
    low_end()
    for step in range(PASSES):
        low_wide[step] = jnp.dot(
            low_all[...], spread(objective[step], step), preferred_element_type=jnp.float32
        ).astype(jnp.bfloat16)
    arrived(7)
    own_products(0)
    own_products(1)
    send_products(1, 2)
    send_products(1, 3)
    own_products(2)
    own_products(3)

    lane = lax.broadcasted_iota(jnp.int32, (LEN, 128), 1)
    stats = jnp.zeros((LEN, 128), jnp.float32)
    for kind in range(2 * PASSES):
        stats = jnp.where(lane == kind, jnp.sum(sums[kind], axis=1, keepdims=True), stats)
    stat_own[0] = stats.T[: 2 * PASSES]

    def stat_pair():
        return remote(
            stat_own.at[0], stat_own.at[1], stat_send.at[0], stat_recv.at[0], (me_d, other)
        )

    def stat_copy(step):
        return remote(
            stat_slots.at[0],
            stat_slots.at[step],
            stat_send.at[step],
            stat_recv.at[step],
            same_core(step),
        )

    stat_pair().start()
    stat_pair().wait()
    stat_slots[0] = stat_own[0] + stat_own[1]
    for step in range(1, CHIPS):
        stat_copy(step).start()
    for step in range(1, CHIPS):
        stat_copy(step).wait()
    totals = jnp.sum(stat_slots[...], axis=0)
    inner_first = jnp.concatenate([totals[1:], totals[:1]], axis=0)
    scale_inv = lax.rsqrt(totals / MODEL_WIDTH + epsilon)
    weight_hidden = inner_first * scale_inv**3 / MODEL_WIDTH
    keep = jnp.concatenate(
        [scale_inv, weight_hidden, jnp.zeros((128 - 4 * PASSES, LEN), jnp.float32)], axis=0
    )
    keep = jnp.where(lax.broadcasted_iota(jnp.int32, keep.shape, 0) % 2 == 0, keep, 0.0)
    by_token = keep.T

    terms = None
    for step in range(PASSES):
        weighted = cotangent[step].astype(jnp.float32) * scale[...]
        per_token = by_token[:, 2 * step : 2 * step + 1]
        back = by_token[:, 2 * PASSES + 2 * step : 2 * PASSES + 2 * step + 1]
        grads[step] = (per_token * weighted - hidden[step] * back).astype(jnp.bfloat16)
        term = lax.dot_general(
            grads[step], up_wide[step], (((1,), (1,)), ((), ())), preferred_element_type=jnp.float32
        )
        terms = term if terms is None else terms + term
    back_terms[...] = terms.reshape(back_terms.shape)
    back_begin()

    per_b = None
    for step in range(PASSES):
        term = lax.dot_general(
            low_wide[step], grads[step], (((0,), (0,)), ((), ())), preferred_element_type=jnp.float32
        )
        per_b = term if per_b is None else per_b + term
    square_b[...] = (per_b * per_b).astype(jnp.bfloat16).reshape(square_b.shape)

    def owners(squares, from_x, slots, x_sems, z_sems):
        def x_part(number):
            place = z_of(number)
            return remote(
                squares.at[1 - half, place],
                from_x.at[place],
                x_sems.at[0, number],
                x_sems.at[1, number],
                beside,
            )

        def z_part(number):
            return remote(
                squares.at[half, z_of(number)],
                slots.at[number],
                z_sems.at[0, number],
                z_sems.at[1, number],
                (half * RING + z_of(number), me_t),
            )

        def begin():
            for number in range(RING):
                x_part(number).start()

        def middle():
            for number in range(RING):
                x_part(number).wait_recv()
                place = z_of(number)
                total = squares[half, place].astype(jnp.float32) + from_x[place].astype(jnp.float32)
                if NEAR[number] == 0:
                    slots[number] = total.astype(jnp.bfloat16)
                else:
                    squares[half, place] = total.astype(jnp.bfloat16)
                    z_part(number).start()

        def end(out):
            for number in range(RING):
                if NEAR[number] != 0:
                    z_part(number).wait_recv()
            out[...] = jnp.sum(slots[...].astype(jnp.float32), axis=0)

        def drain():
            for number in range(RING):
                x_part(number).wait_send()
                if NEAR[number] != 0:
                    z_part(number).wait_send()

        return begin, middle, end, drain

    b_begin, b_middle, b_end, b_drain = owners(square_b, from_x_b, slots_b, bx_sems, bz_sems)

    def a_copy(step):
        return remote(
            square_a.at[lax.rem(me_d + step, GROUP)],
            slots_a.at[step],
            a_sems.at[0, step],
            a_sems.at[1, step],
            (lax.rem(me_d + step, GROUP), me_t),
        )

    b_begin()
    back_middle()
    b_middle()
    back_end()
    per_a = lax.dot_general(
        back_all[...], attention[...], (((0,), (0,)), ((), ())), preferred_element_type=jnp.float32
    )
    square_a[...] = (per_a * per_a).astype(jnp.bfloat16).reshape(square_a.shape)
    each_other(lambda step: a_copy(step).start())
    b_end(out_b)

    for step in range(1, RING):
        plane_copy(step, own_place).wait_send()
    for number in range(RING - 1):
        z_copy(number, me_z).wait_send()
    for chunk in range(chunks):
        weight_copy(chunk, half).wait_send()
    for number in range(RING):
        x_copy(number, me_t).wait_send()
        for way in range(3):
            y_copy(number, way, me_t).wait_send()
        for shift in range(4):
            core_copy(number, shift, me_t).wait_send()

    def ring_done(chunk, carry):
        for way in range(2):
            for far in range(1, 5):
                ring_copy(way, far, chunk).wait_send()
        return carry

    lax.fori_loop(0, chunks, ring_done, 0)
    b_drain()
    each_other(lambda step: a_copy(step).wait())
    slots_a[0] = square_a[me_d]
    out_a[...] = jnp.sum(slots_a[...].astype(jnp.float32), axis=0)


def choose(objective, total, out):
    per = ADAPTER_RANK // GROUP
    for adapter in range(ADAPTER_COUNT):
        chosen = None
        for step in range(PASSES):
            share = jnp.where(objective[step] == adapter, 1.0 / EXAMPLES, 0.0)
            part = share * total[step * per : (step + 1) * per]
            chosen = part if chosen is None else chosen + part
        out[adapter] = chosen


def choose_kernel(objective, total_a, total_b, out_a, out_b):
    choose(objective, total_a[...], out_a)
    choose(objective, total_b[...], out_b)


def body(
    attention,
    output_weight_frozen,
    residual,
    cotangent,
    output_norm_scale,
    adapter_down_weights,
    adapter_up_weights,
    objective,
):
    features = attention.shape[1]
    depth, columns = output_weight_frozen.shape
    chunks = columns // CHUNK
    per = ADAPTER_RANK // GROUP
    wide = PASSES * ADAPTER_RANK
    rows = LEN // GROUP
    share = wide // GROUP
    bf16, f32 = jnp.bfloat16, jnp.float32
    vmem = pl.BlockSpec(memory_space=pltpu.VMEM)
    hbm = pl.BlockSpec(memory_space=pl.ANY)
    sem = pltpu.SemaphoreType.DMA
    squares = pl.pallas_call(
        whole_kernel,
        name="fisher",
        out_shape=(
            jax.ShapeDtypeStruct((share, features), f32),
            jax.ShapeDtypeStruct((share, columns), f32),
        ),
        in_specs=[pl.BlockSpec(memory_space=pltpu.SMEM), vmem] + [hbm] * 6,
        out_specs=(vmem, vmem),
        scratch_shapes=[
            pltpu.VMEM((LEN, features), bf16),
            pltpu.VMEM((RING, PIECE, features), bf16),
            pltpu.VMEM((RING, 2, LEN, features), bf16),
            pltpu.VMEM((2, depth, columns), bf16),
            pltpu.VMEM((LEN, columns), bf16),
            pltpu.VMEM((PASSES, LEN, columns), bf16),
            pltpu.VMEM((ADAPTER_COUNT, ADAPTER_RANK, features), bf16),
            pltpu.VMEM((ADAPTER_COUNT, ADAPTER_RANK, columns), bf16),
            pltpu.VMEM((2, 4, chunks, LEN, CHUNK), bf16),
            pltpu.VMEM((2, 4, chunks, LEN, CHUNK), bf16),
            pltpu.VMEM((PASSES, LEN, columns), f32),
            pltpu.VMEM((2 * PASSES, LEN, 128), f32),
            pltpu.VMEM((PASSES, LEN, columns), bf16),
            pltpu.VMEM((GROUP, rows, wide), f32),
            pltpu.VMEM((GROUP, rows, wide), f32),
            pltpu.VMEM((LEN, wide), bf16),
            pltpu.VMEM((PASSES, LEN, wide), bf16),
            pltpu.VMEM((PASSES, wide, columns), bf16),
            pltpu.VMEM((2, 2 * PASSES, LEN), f32),
            pltpu.VMEM((CHIPS, 2 * PASSES, LEN), f32),
            pltpu.VMEM((GROUP, rows, wide), f32),
            pltpu.VMEM((GROUP, rows, wide), f32),
            pltpu.VMEM((LEN, wide), bf16),
            pltpu.VMEM((2, RING, share, columns), bf16),
            pltpu.VMEM((RING, share, columns), bf16),
            pltpu.VMEM((RING, share, columns), bf16),
            pltpu.VMEM((GROUP, share, features), bf16),
            pltpu.VMEM((GROUP, share, features), bf16),
            sem((6,)),
            sem((RING,)),
            sem((RING,)),
            sem((RING,)),
            sem((RING,)),
            sem((RING,)),
            sem((RING,)),
            sem((chunks,)),
            sem((chunks,)),
            sem((RING, 3)),
            sem((RING, 3)),
            sem((RING, 4)),
            sem((RING, 4)),
            sem((2, 4, chunks)),
            sem((2, 4, chunks)),
            sem((4, GROUP)),
            sem((4, GROUP)),
            sem((CHIPS,)),
            sem((CHIPS,)),
        ]
        + [sem((2, RING))] * 2
        + [sem((2, GROUP))],
        compiler_params=pltpu.CompilerParams(
            collective_id=0, has_side_effects=True, vmem_limit_bytes=56 * 2**20
        ),
    )(
        objective,
        output_norm_scale[None],
        attention,
        output_weight_frozen,
        residual,
        cotangent,
        adapter_down_weights,
        adapter_up_weights,
    )
    return pl.pallas_call(
        choose_kernel,
        name="choose",
        out_shape=(
            jax.ShapeDtypeStruct((ADAPTER_COUNT, per, features), f32),
            jax.ShapeDtypeStruct((ADAPTER_COUNT, per, columns), f32),
        ),
        in_specs=[pl.BlockSpec(memory_space=pltpu.SMEM), vmem, vmem],
        out_specs=(vmem, vmem),
    )(objective, *squares)


def solution(mesh):
    placed = (
        P("dp", "tensor"),
        P("dp", "tensor"),
        P("dp", "tensor"),
        P(None, "dp", "tensor"),
        P("tensor"),
        P(),
        P(None, None, "tensor"),
        P(),
    )
    return jax.shard_map(
        body,
        mesh=mesh,
        in_specs=placed,
        out_specs=(P(None, "dp", "tensor"), P(None, "dp", "tensor")),
        check_vma=False,
    )
```
